256 devices in a mesh: section: 4 (over z_lo), space: 64 (over y, x, z_hi, core).
Axes of the slice: x: 4, y: 4, z: 8 (z_hi: 2, z_lo: 4; z = z_hi * 4 + z_lo), core: 2. Of those that a mesh axis runs over, the one named last changes fastest.
Arguments:
- features: bfloat16 [1, 256, 128, 320], P(None, 'space'), may hold values from -30 to 30
- section_packs: bfloat16 [4, 11520, 640], P('section', None, 'space'), may hold values from -6 to 6
Outputs:
- output: bfloat16 [1, 256, 128, 320], P(None, 'space', 'section')
The draws below stay inside these ranges and needn't reach their ends.
All inputs are finite; a program needn't handle non-finite values.
Results may differ from the reference program's by a relative error of at most 0.009.
Values may be sent and summed in bfloat16 or wider, within the bound.
A program may use at most 128 MiB of HBM per device.

```python
import math
import jax
import jax.numpy as jnp
from jax import lax

NARROW = 320
BROAD = 640
GROUPS = 32
COLUMNS = 128
MICRO = 1
HEIGHT = 256
PACK_ROWS = 11520
N_SECTION = 4


def draw_features(key, part):
    base = jax.random.normal(key, (MICRO, HEIGHT, COLUMNS, NARROW), jnp.float32)
    ramp = lax.broadcasted_iota(jnp.float32, (1, HEIGHT, 1, 1), 1) / (HEIGHT - 1)
    offset = 1.5 + 0.5 * jax.random.normal(jax.random.fold_in(key, 7), (1, 1, 1, NARROW), jnp.float32)
    values = (base + offset) * (1.0 + 2.0 * ramp)
    return jnp.clip(values, -30.0, 30.0).astype(jnp.bfloat16)


def shard_levels(own_key, shape, pieces, least, top_value):
    level = 1.0
    for position, shards_of in pieces:
        heights = jax.random.uniform(jax.random.fold_in(jax.random.fold_in(own_key, 6), position), (shards_of,), jnp.float32, least / len(pieces), top_value / len(pieces))
        level = level * jnp.repeat(jnp.exp(heights), shape[position] // shards_of).reshape((-1,) + (1,) * (len(shape) - 1 - position))
    return level


def centred(rng, shape, scale, most, cuts=(), kind=jnp.bfloat16):
    entries = jax.random.normal(rng, shape, jnp.float32) * scale
    if len(cuts) > 0:
        entries = shard_levels(rng, shape, cuts, -0.22, 0.18) * entries
    return jnp.clip(entries, min=-most, max=most).astype(kind)


def setup_inputs(seed: int = 0) -> dict:
    key_list = jax.random.split(jax.random.key(seed), 3)
    return {
        "features": draw_features(jax.random.fold_in(key_list[2], 71), 0),
        "section_packs": centred(key_list[1], (N_SECTION, PACK_ROWS, BROAD), 1.0, 6.0, ((0, 4), (2, 64))),
    }


EPSILON = 1e-05

def convolve(field_in, kernel, fan_in, stride):
    result = lax.conv_general_dilated(field_in.astype(jnp.float32)[None], kernel.astype(jnp.float32), (stride, stride), ((1, 1), (1, 1)), dimension_numbers=('NHWC', 'HWIO', 'NHWC'), precision=lax.Precision.HIGHEST, preferred_element_type=jnp.float32)[0]
    return result * (1.0 / math.sqrt(fan_in))

def activate(field_in):
    values = field_in.astype(jnp.float32)
    n_rows, n_cols, n_chans = values.shape
    grouped = values.reshape(n_rows * n_cols, GROUPS, n_chans // GROUPS)
    group_mean = lax.optimization_barrier(jnp.mean(grouped, axis=(0, 2)))
    centered = grouped - group_mean[None, :, None]
    group_var = lax.optimization_barrier(jnp.mean(jnp.square(centered), axis=(0, 2)))
    normed = centered / jnp.sqrt(group_var + EPSILON)[None, :, None]
    return jax.nn.silu(normed.reshape(n_rows, n_cols, n_chans)).astype(jnp.bfloat16)

def kernel_at(flat_pack, offset, c_in, c_out):
    return flat_pack[offset:offset + 9 * c_in * c_out].reshape(3, 3, c_in, c_out)

def res_pair(field_in, kernel_one, kernel_two):
    c_in = field_in.shape[-1]
    c_out = kernel_two.shape[-1]
    hidden = convolve(activate(field_in), kernel_one, 9 * c_in, 1).astype(jnp.bfloat16)
    return (field_in.astype(jnp.float32) + convolve(activate(hidden), kernel_two, 9 * c_out, 1)).astype(jnp.bfloat16)

def reference(features, section_packs):
    narrow = NARROW
    wide_ch = BROAD
    square = narrow * narrow
    pack_zero = section_packs[0].reshape(-1)
    pack_one = section_packs[1].reshape(-1)
    pack_two = section_packs[2].reshape(-1)
    pack_three = section_packs[3].reshape(-1)

    def one_micro(field_in):
        skip = res_pair(field_in, kernel_at(pack_zero, 0, narrow, narrow), kernel_at(pack_zero, 9 * square, narrow, narrow))
        coarse = convolve(skip, kernel_at(pack_zero, 18 * square, narrow, wide_ch), 9 * narrow, 2).astype(jnp.bfloat16)
        coarse = res_pair(coarse, kernel_at(pack_one, 0, wide_ch, wide_ch), kernel_at(pack_one, 36 * square, wide_ch, wide_ch))
        coarse = res_pair(coarse, kernel_at(pack_two, 0, wide_ch, wide_ch), kernel_at(pack_two, 36 * square, wide_ch, wide_ch))
        upsampled = jnp.repeat(jnp.repeat(coarse, 2, 0), 2, 1)
        upper = convolve(upsampled, kernel_at(pack_three, 0, wide_ch, narrow), 9 * wide_ch, 1).astype(jnp.bfloat16)
        joined = jnp.concatenate([upper, skip], -1)
        hidden = convolve(activate(joined), kernel_at(pack_three, 18 * square, wide_ch, narrow), 9 * wide_ch, 1).astype(jnp.bfloat16)
        projection = jnp.dot(joined.reshape(-1, wide_ch), pack_three[45 * square:47 * square].reshape(wide_ch, narrow), preferred_element_type=jnp.float32)
        projection = projection.reshape(upper.shape) * (1.0 / math.sqrt(wide_ch))
        return (projection + convolve(activate(hidden), kernel_at(pack_three, 36 * square, narrow, narrow), 9 * narrow, 1)).astype(jnp.bfloat16)
    return lax.map(one_micro, features)
```

```python
import math

import jax
import jax.numpy as jnp
import numpy as np
from jax import lax
from jax.experimental import pallas as pl
from jax.experimental.pallas import tpu as pltpu
from jax.sharding import PartitionSpec as P

F32 = jnp.float32
BF16 = jnp.bfloat16
MESH = pl.DeviceIdType.MESH
EPSILON = 1e-05
CHUNK = 1920
HALF_A = 1024
HALF_B = CHUNK - HALF_A
ROW_N = 512 * 10


def selections():
    rows = np.arange(512)
    slot, lane = rows // 16, rows % 16
    chan_fine = np.where(lane < 10, 10 * ((slot % 16) * 2 + slot // 16) + lane, -1)
    rows = np.arange(1024)
    slot, lane = rows // 16, rows % 16
    chan_wide = np.where(lane < 10, 10 * ((slot % 32) * 2 + slot // 32) + lane, -1)
    split = lambda n: np.concatenate([np.arange(0, n, 2), np.arange(1, n, 2)])
    di, di_wide = split(320), split(640)
    nat, nat_wide = np.arange(320), np.arange(640)
    eq = lambda a, b: (a[:, None] == b[None, :])
    b = np.arange(128)
    shifts = np.stack([eq(b, b + dx) for dx in (-1, 1)])
    strided = np.stack(
        [
            np.stack([eq(b, 2 * (b % 64) + dx) & (b // 64 == i)[None, :] for dx in (-1, 0, 1)])
            for i in (0, 1)
        ]
    )
    doubled = np.stack(
        [
            np.stack(
                [
                    eq(b, 64 * half + (b + dx) // 2) & ((b + dx >= 0) & (b + dx < 128))[None, :]
                    for dx in (-1, 0, 1)
                ]
            )
            for half in (0, 1)
        ]
    )

    def taps(rows_in, rows_out):
        a, c = np.arange(rows_in * 64), np.arange(rows_out * 64)
        out = []
        for dy in (0, 1, 2):
            for dx in (-1, 0, 1):
                col = c % 64 + dx
                out.append(
                    eq(a, (c // 64 + dy) * 64 + col) & ((col >= 0) & (col < 64))[None, :]
                )
        return np.stack(out)

    group = np.arange(128)
    fine_groups = np.stack(
        [eq(di // 10, group), eq(di // 20, group), eq(16 + di // 20, group)]
    )
    wide_groups = eq(nat_wide // 20, group)
    bf = lambda m: np.asarray(m, np.float32).astype(jnp.bfloat16)
    return (
        bf(eq(di, chan_fine)),
        bf(eq(nat, chan_fine)),
        bf(eq(chan_fine, di)),
        bf(eq(chan_fine, nat)),
        bf(eq(nat_wide, chan_wide)),
        bf(eq(chan_wide, nat_wide)),
        bf(eq(di, nat)),
        bf(eq(di_wide, nat_wide)),
        bf(shifts),
        bf(strided),
        bf(doubled),
        bf(taps(6, 4)),
        bf(taps(4, 2)),
        np.asarray(fine_groups, np.float32),
        np.asarray(wide_groups, np.float32),
    )


def dot(a, b):
    return jnp.dot(a, b, preferred_element_type=F32)


def activate(values, mean, rstd):
    z = (values - mean) * rstd
    return z / (1.0 + jnp.exp(-z))


def kernel(
    x_ref, w_ref, sel_di, sel_nat, exp_di, exp_nat, sel_c, exp_c, perm_x, perm_c, shifts, strided,
    doubled, taps_one, taps_two, fine_groups, wide_groups, out_ref,
    W, col, colj, sh, xr, xd, hid, skd, skn, skb, cb, tile, a3, a2, hs, acc, ud, outs, landed,
    SA, SB, HS, gather_send, gather_recv, a_send, a_recv, b_send, b_recv,
    x_send, x_recv, c_send, c_recv, k_send, k_recv, o_send, o_recv,
):
    sec = lax.axis_index("section")
    d = lax.axis_index("space")
    c = lax.rem(d, 2)
    z = lax.rem(lax.div(d, 2), 2)
    x = lax.rem(lax.div(d, 4), 4)
    y = lax.div(d, 16)
    hi, lo = lax.div(d, 8), lax.rem(d, 8)
    space = lambda y, x, z, c: ((y * 4 + x) * 2 + z) * 2 + c
    xp, xm = lax.rem(x + 1, 4), lax.rem(x + 3, 4)
    yp, ym = lax.rem(y + 1, 4), lax.rem(y + 3, 4)
    below, above = lax.rem(d + 1, 64), lax.rem(d + 63, 64)
    lo_peer = lambda k: hi * 8 + lax.rem(lo + k, 8)
    hi_peer = lambda k: lax.rem(hi + k, 8) * 8 + lo
    after, before = lax.rem(sec + 1, 4), lax.rem(sec + 3, 4)
    is_top = d == 0
    is_bottom = d == 63
    keep_top = jnp.where(is_top, 0.0, 1.0)
    keep_bottom = jnp.where(is_bottom, 0.0, 1.0)

    barrier = pltpu.get_barrier_semaphore()
    peers = [(sec, lo_peer(k)) for k in range(1, 8)] + [(sec, hi_peer(k)) for k in range(1, 8)]
    peers += [(sec, space(y, xp, z, c)), (sec, space(y, xm, z, c)), (sec, below), (sec, above)]
    for other in (after, before):
        peers += [(other, hi_peer(k)) for k in range(8)] + [(other, below), (other, above)]
    peers += [(lax.rem(sec + 2, 4), d)]
    for peer in peers:
        pl.semaphore_signal(barrier, inc=1, device_id=peer, device_id_type=MESH)

    W[c, y, x, pl.ds(pl.multiple_of(16 * z, 16), 16), :] = w_ref[...]
    pl.semaphore_wait(barrier, len(peers))

    def remote(src, dst, send, recv, peer):
        return pltpu.make_async_remote_copy(
            src_ref=src, dst_ref=dst, send_sem=send, recv_sem=recv, device_id=peer,
            device_id_type=MESH,
        )

    def to_message(mean, deviation):
        return jnp.concatenate([mean, deviation, jnp.zeros((6, 128), F32)], axis=0)

    def combined(messages, count):
        means = messages[:, 0:1, :]
        mean = jnp.sum(means, axis=0) * 0.125
        spread = jnp.sum(jnp.square(means - mean[None]), axis=0) * count
        return mean, jnp.sum(messages[:, 1:2, :], axis=0) + spread

    def part_sums(blocks, groups, count, weight=None):
        total = blocks[0] if weight is None else blocks[0] * weight
        for block in blocks[1:]:
            total = total + block
        channel = jnp.sum(total, axis=1, keepdims=True)
        mean = jnp.sum(groups * channel, axis=0, keepdims=True) * (1.0 / count)
        own = jnp.sum(groups * mean, axis=1, keepdims=True)
        squares = None
        for block in blocks:
            off = jnp.square(block - own)
            off = off if weight is None else off * weight
            squares = off if squares is None else squares + off
        channel = jnp.sum(squares, axis=1, keepdims=True)
        return mean, jnp.sum(groups * channel, axis=0, keepdims=True)

    def first_copies(e):
        return [
            remote(SA.at[e, 0], SA.at[e, k], a_send.at[e, k], a_recv.at[e, k], (sec, lo_peer(k)))
            for k in range(1, 8)
        ]

    def start_first(e, mean, deviation):
        SA[e, 0] = to_message(mean, deviation)
        for copy in first_copies(e):
            copy.start()

    def finish_first(e, count):
        for copy in first_copies(e):
            copy.wait()
        return combined(SA[e], count)

    def second_copies(e):
        return [
            remote(SB.at[e, 0], SB.at[e, k], b_send.at[e, k], b_recv.at[e, k], (sec, hi_peer(k)))
            for k in range(1, 8)
        ]

    def scale_rows(e, count):
        mean, squares = combined(SB[e], 8 * count)
        return mean, lax.rsqrt(squares * (1.0 / (64 * count)) + EPSILON)

    def start_second(e, count):
        mean, deviation = finish_first(e, count)
        SB[e, 0] = to_message(mean, deviation)
        for copy in second_copies(e):
            copy.start()

    def finish_second(e, count):
        for copy in second_copies(e):
            copy.wait()
        return scale_rows(e, count)

    def exchanged(e, mean, deviation, count):
        start_first(e, mean, deviation)
        start_second(e, count)
        return finish_second(e, count)

    def columns(groups, rows):
        return [jnp.sum(groups * row, axis=1, keepdims=True) for row in rows]

    def across_copies():
        return [
            remote(HS, SB.at[2, k], b_send.at[2, k], b_recv.at[2, k], (after, hi_peer(k)))
            for k in range(8)
        ]

    def tile_copies():
        return [
            remote(tile, cb.at[slot], c_send.at[slot], c_recv.at[slot], (after, peer))
            for slot, peer in ((1, d), (0, below), (2, above))
        ]

    def skip_copies():
        return [
            remote(skd.at[lax_rows(1, 4)], skb.at[lax_rows(2, 4)], k_send.at[0], k_recv.at[0], (before, d)),
            remote(skd.at[lax_rows(3, 2)], skb.at[lax_rows(0, 2)], k_send.at[1], k_recv.at[1], (before, below)),
            remote(skd.at[lax_rows(1, 2)], skb.at[lax_rows(6, 2)], k_send.at[2], k_recv.at[2], (before, above)),
        ]

    def lax_rows(start, size):
        return pl.ds(start, size)

    def hand_over(count):
        for copy in tile_copies():
            copy.start()
        mean, deviation = part_sums([tile[...].astype(F32)], wide_groups[...], count)
        start_first(2, mean, deviation)
        HS[...] = to_message(*finish_first(2, count))
        for copy in across_copies():
            copy.start()
        for copy in tile_copies() + across_copies():
            copy.wait_send()

    def take_over():
        for copy in tile_copies() + across_copies():
            copy.wait_recv()

    chunks = jnp.where(sec == 0, 3, jnp.where(sec == 3, 4, 6))

    def gather_copies(stage, k):
        lane = lambda off, size: pl.ds(pl.multiple_of(k * CHUNK + off, 128), size)
        whole, part_a, part_b = lane(0, CHUNK), lane(0, HALF_A), lane(HALF_A, HALF_B)
        to_xp, to_xm = space(y, xp, z, c), space(y, xm, z, c)
        to_yp, to_ym = space(yp, x, z, c), space(ym, x, z, c)
        all32, first, second = pl.ds(0, 32), pl.ds(0, 16), pl.ds(16, 16)
        every, low, high = pl.ds(0, 4), pl.ds(0, 2), pl.ds(2, 2)
        if stage == 0:
            moves = [((c, y, x, pl.ds(pl.multiple_of(16 * z, 16), 16), whole), space(y, x, 1 - z, c))]
        elif stage == 1:
            a, b = (c, y, x, all32, part_a), (c, y, x, all32, part_b)
            moves = [(a, to_xp), (a, to_xm), (b, to_yp), (b, to_ym)]
        elif stage == 2:
            moves = [
                ((c, y, xm, first, part_a), to_xp),
                ((c, y, xp, second, part_a), to_xm),
                ((c, ym, x, first, part_b), to_yp),
                ((c, yp, x, second, part_b), to_ym),
            ]
        elif stage == 3:
            a, b = (c, y, every, all32, part_a), (c, every, x, all32, part_b)
            moves = [(a, to_yp), (a, to_ym), (b, to_xp), (b, to_xm)]
        elif stage == 4:
            moves = [
                ((c, ym, low, all32, part_a), to_yp),
                ((c, yp, high, all32, part_a), to_ym),
                ((c, low, xm, all32, part_b), to_xp),
                ((c, high, xp, all32, part_b), to_xm),
            ]
        else:
            moves = [((c, every, every, all32, whole), space(y, x, z, 1 - c))]
        first_id = (0, 1, 5, 9, 13, 17)[stage]
        return [
            remote(
                W.at[where], W.at[where], gather_send.at[first_id + i, k],
                gather_recv.at[first_id + i, k], (sec, peer),
            )
            for i, (where, peer) in enumerate(moves)
        ]

    def gather():
        def step(t, carry):
            for stage in range(7):
                k = t - stage

                @pl.when((k >= 0) & (k < chunks))
                def _():
                    if stage > 0:
                        for copy in gather_copies(stage - 1, k):
                            copy.wait_recv()
                    if stage < 6:
                        for copy in gather_copies(stage, k):
                            copy.start()

            return carry

        lax.fori_loop(0, chunks + 6, step, 0)

    def gather_end():
        def step(k, carry):
            for stage in range(6):
                for copy in gather_copies(stage, k):
                    copy.wait_send()
            return carry

        lax.fori_loop(0, chunks, step, 0)

    def put_shifted(index, base, values):
        size = values.shape[0]
        sh[1, index, base : base + size, :] = values
        sh[0, index, base : base + size, :] = dot(values, shifts[0]).astype(BF16)
        sh[2, index, base : base + size, :] = dot(values, shifts[1]).astype(BF16)

    def fine_conv(pairs, pieces, per_tap, lead, lane_start, depth, source_row, use):
        taps = 9 * per_tap
        for p in range(2):
            if lead:
                col[p, 0:lead, :] = jnp.zeros((lead, 256), BF16)
            if lead + taps < depth:
                col[p, lead + taps : depth, :] = jnp.zeros((depth - lead - taps, 256), BF16)

        def pair(q, carry):
            for p in range(2):
                for dy in range(3):
                    for j in range(2):
                        row = source_row(q, j + dy)
                        for dx in range(3):
                            at = lead + (dy * 3 + dx) * per_tap
                            for to, start, size in pieces(p):
                                col[p, at + to : at + to + size, 128 * j : 128 * j + 128] = sh[
                                    dx, row, start : start + size, :
                                ]
            use(q, weighted(lane_start, depth, col))
            return carry

        lax.fori_loop(0, pairs, pair, 0)

    def weighted(lane_start, depth, source):
        total = None
        for p in range(2):
            kernels = W[:, 2 * p : 2 * p + 2, :, :, lane_start : lane_start + depth]
            made = dot(kernels.reshape(512, depth), source[p, 0:depth, :])
            total = made if total is None else total + made
        return total

    narrow_pieces = lambda p: [(0, 160 * p, 160)]
    wide_pieces = lambda p: [(0, 320 * p, 320)]
    joined_pieces = lambda p: [(0, 160 * p, 160), (160, 320 + 160 * p, 160)]
    follow = lambda q, off: 2 * q + off
    narrow_scale = 1.0 / math.sqrt(9 * 320)
    wide_scale = 1.0 / math.sqrt(9 * 640)

    def row_kept(row):
        return jnp.where(row < 0, keep_top, jnp.where(row > 3, keep_bottom, 1.0))

    def activate_rows(source, count, first_row, mean, rstd):
        def one(r, carry):
            values = activate(source[r].astype(F32), mean, rstd) * row_kept(r + first_row)
            put_shifted(r, 0, values.astype(BF16))
            return carry

        lax.fori_loop(0, count, one, 0)

    @pl.when(sec == 0)
    def _():
        x_copies = [
            remote(x_ref.at[pl.ds(1, 3)], xr.at[pl.ds(0, 3)], x_send.at[0], x_recv.at[0], (0, below)),
            remote(x_ref.at[pl.ds(0, 2)], xr.at[pl.ds(7, 2)], x_send.at[1], x_recv.at[1], (0, above)),
        ]
        for copy in x_copies:
            copy.start()
        for r in range(4):
            xr[3 + r] = x_ref[r]
        xr[9] = jnp.zeros((320, 128), BF16)

        def permute(r, carry):
            xd[r] = dot(perm_x[...], xr[r]).astype(BF16)
            return carry

        lax.fori_loop(3, 7, permute, 0)
        groups = fine_groups[0]
        start_first(0, *part_sums([xd[r].astype(F32) for r in range(3, 7)], groups, ROW_N))
        gather()
        start_second(0, ROW_N)
        for copy in x_copies:
            copy.wait()
        lax.fori_loop(0, 3, permute, 0)
        lax.fori_loop(7, 10, permute, 0)
        mean, rstd = columns(groups, finish_second(0, ROW_N))
        activate_rows(xd, 10, -3, mean, rstd)

        def keep_hidden(q, made):
            rounded = (made * narrow_scale).astype(BF16)
            packed = dot(sel_di[...], rounded).astype(BF16)
            hid[2 * q] = packed[:, 0:128]
            hid[2 * q + 1] = packed[:, 128:256]

        fine_conv(4, narrow_pieces, 160, 0, 0, 1536, follow, keep_hidden)
        sums = part_sums([hid[r].astype(F32) for r in range(2, 6)], groups, ROW_N)
        mean, rstd = columns(groups, exchanged(1, *sums, ROW_N))
        activate_rows(hid, 8, -2, mean, rstd)

        def keep_skip(q, made):
            for j in range(2):
                own = dot(exp_di[...], xd[2 * q + j + 2])
                rounded = (own + made[:, 128 * j : 128 * j + 128] * narrow_scale).astype(BF16)
                skd[2 * q + j] = dot(sel_di[...], rounded).astype(BF16)
                skn[2 * q + j] = dot(sel_nat[...], rounded).astype(BF16)

        fine_conv(3, narrow_pieces, 160, 32, 1408, 1536, follow, keep_skip)
        for copy in skip_copies():
            copy.start()
        skn[0] = (skn[0].astype(F32) * keep_top).astype(BF16)
        col[0, 0:64, 0:128] = jnp.zeros((64, 128), BF16)
        for dy in range(3):
            for dx in range(3):
                at = 64 + (dy * 3 + dx) * 320
                made = dot(skn[dy], strided[0, dx]) + dot(skn[2 + dy], strided[1, dx])
                col[0, at : at + 320, 0:128] = made.astype(BF16)
        made = dot(W[:, :, :, :, 2816:5760].reshape(1024, 2944), col[0, :, 0:128])
        rounded = (made * narrow_scale).astype(BF16)
        tile[...] = dot(sel_c[...], rounded).astype(BF16)
        hand_over(128 * 20)
        for copy in skip_copies():
            copy.wait_send()

    @pl.when((sec == 1) | (sec == 2))
    def _():
        gather()
        take_over()
        count = 128 * 20
        groups = wide_groups[...]
        mean, rstd = columns(groups, scale_rows(2, count))
        for i in range(3):
            values = activate(cb[i].astype(F32), mean, rstd)
            values = values * (keep_top, 1.0, keep_bottom)[i]
            a3[:, 128 * i : 128 * i + 128] = values.astype(BF16)

        acc[...] = jnp.zeros((1024, 256), F32)

        def first_tap(t, carry):
            moved = dot(a3[...], taps_one[t]).astype(BF16)
            lanes = pl.ds(pl.multiple_of(t * 640, 128), 640)
            acc[...] += dot(W[:, :, :, :, lanes].reshape(1024, 640), moved)
            return carry

        lax.fori_loop(0, 9, first_tap, 0)
        rounded = (acc[...] * wide_scale).astype(BF16)
        hs[...] = dot(sel_c[...], rounded)
        column = lax.broadcasted_iota(jnp.int32, (1, 256), 1)
        inner = jnp.where((column >= 64) & (column < 192), 1.0, 0.0)
        kept = jnp.where(column < 64, keep_top, jnp.where(column >= 192, keep_bottom, 1.0))
        sums = part_sums([hs[...]], groups, count, inner)
        mean, rstd = columns(groups, exchanged(3, *sums, count))
        a2[...] = (activate(hs[...], mean, rstd) * kept).astype(BF16)
        acc[:, 0:128] = jnp.zeros((1024, 128), F32)

        def second_tap(t, carry):
            moved = dot(a2[...], taps_two[t]).astype(BF16)
            lanes = pl.ds(pl.multiple_of(5760 + t * 640, 128), 640)
            acc[:, 0:128] += dot(W[:, :, :, :, lanes].reshape(1024, 640), moved)
            return carry

        lax.fori_loop(0, 9, second_tap, 0)
        own = dot(exp_c[...], cb[1])
        rounded = (own + acc[:, 0:128] * wide_scale).astype(BF16)
        tile[...] = dot(sel_c[...], rounded).astype(BF16)
        hand_over(count)

    def out_copies(sections=range(3)):
        return [
            remote(
                outs.at[pl.ds(0, 4), pl.ds(32 * t, 32)], landed, o_send.at[t], o_recv.at[0], (t, d)
            )
            for t in sections
        ]

    @pl.when(sec == 3)
    def _():
        gather()
        for copy in skip_copies():
            copy.wait_recv()
        take_over()
        for i in range(3):
            moved = dot(perm_c[...], cb[i]) * (keep_top, 1.0, keep_bottom)[i]
            moved = moved.astype(BF16)
            for half in range(2):
                for dx in range(3):
                    sh[dx, 2 * i + half] = dot(moved, doubled[half, dx]).astype(BF16)

        def keep_upper(q, made):
            rounded = (made * wide_scale).astype(BF16)
            packed = dot(sel_di[...], rounded).astype(BF16)
            ud[2 * q] = packed[:, 0:128]
            ud[2 * q + 1] = packed[:, 128:256]

        half_row = lambda q, off: q + (off + 1) // 2
        fine_conv(4, wide_pieces, 320, 0, 0, 2944, half_row, keep_upper)
        groups_u, groups_s = fine_groups[1], fine_groups[2]
        mean_u, dev_u = part_sums([ud[r].astype(F32) for r in range(2, 6)], groups_u, 2 * ROW_N)
        mean_s, dev_s = part_sums([skb[r].astype(F32) for r in range(2, 6)], groups_s, 2 * ROW_N)
        rows = exchanged(4, mean_u + mean_s, dev_u + dev_s, 2 * ROW_N)
        mean_u, rstd_u = columns(groups_u, rows)
        mean_s, rstd_s = columns(groups_s, rows)

        def joined_row(r, carry):
            kept = row_kept(r - 2)
            upper = activate(ud[r].astype(F32), mean_u, rstd_u) * kept
            put_shifted(r, 0, upper.astype(BF16))
            lower = activate(skb[r].astype(F32), mean_s, rstd_s) * kept
            put_shifted(r, 320, lower.astype(BF16))
            return carry

        lax.fori_loop(0, 8, joined_row, 0)

        def keep_hidden(q, made):
            rounded = (made * wide_scale).astype(BF16)
            packed = dot(sel_di[...], rounded).astype(BF16)
            hid[2 * q] = packed[:, 0:128]
            hid[2 * q + 1] = packed[:, 128:256]

        fine_conv(3, joined_pieces, 320, 64, 2816, 2944, follow, keep_hidden)
        groups = fine_groups[0]
        sums = part_sums([hid[r].astype(F32) for r in range(1, 5)], groups, ROW_N)
        mean, rstd = columns(groups, exchanged(5, *sums, ROW_N))
        activate_rows(hid, 6, -1, mean, rstd)
        for p in range(2):
            colj[p, 0:32, :] = jnp.zeros((32, 256), BF16)
            colj[p, 352:384, :] = jnp.zeros((32, 256), BF16)

        def keep_output(q, made):
            for p in range(2):
                for j in range(2):
                    px = slice(128 * j, 128 * j + 128)
                    colj[p, 32:192, px] = ud[2 * q + j + 2, 160 * p : 160 * p + 160, :]
                    colj[p, 192:352, px] = skb[2 * q + j + 2, 160 * p : 160 * p + 160, :]
            straight = weighted(7168, 384, colj)
            total = made * narrow_scale + straight * (1.0 / math.sqrt(640))
            rounded = total.astype(BF16)
            for j in range(2):
                flipped = lax.dot_general(
                    rounded[:, 128 * j : 128 * j + 128], exp_nat[...], (((0,), (0,)), ((), ())),
                    preferred_element_type=F32,
                )
                outs[2 * q + j] = flipped.astype(BF16)

        fine_conv(2, narrow_pieces, 160, 0, 5760, 1536, follow, keep_output)
        for copy in out_copies():
            copy.start()
        out_ref[...] = outs[:, 96:128, :]
        for copy in out_copies():
            copy.wait_send()

    @pl.when(sec < 3)
    def _():
        for copy in out_copies((0,)):
            copy.wait_recv()
        out_ref[...] = landed[...]

    gather_end()


def shards(features, section_packs):
    fields = jnp.swapaxes(features[0], 1, 2)
    packs = jnp.pad(jnp.swapaxes(section_packs[0], 0, 1), ((0, 6), (0, 0)))
    tables = selections()
    dma = pltpu.SemaphoreType.DMA
    scratch = [
        pltpu.VMEM((2, 4, 4, 32, 11520), BF16),
        pltpu.VMEM((2, 2944, 256), BF16),
        pltpu.VMEM((2, 384, 256), BF16),
        pltpu.VMEM((3, 10, 640, 128), BF16),
        pltpu.VMEM((10, 320, 128), BF16),
        pltpu.VMEM((10, 320, 128), BF16),
        pltpu.VMEM((8, 320, 128), BF16),
        pltpu.VMEM((6, 320, 128), BF16),
        pltpu.VMEM((6, 320, 128), BF16),
        pltpu.VMEM((8, 320, 128), BF16),
        pltpu.VMEM((3, 640, 128), BF16),
        pltpu.VMEM((640, 128), BF16),
        pltpu.VMEM((640, 384), BF16),
        pltpu.VMEM((640, 256), BF16),
        pltpu.VMEM((640, 256), F32),
        pltpu.VMEM((1024, 256), F32),
        pltpu.VMEM((8, 320, 128), BF16),
        pltpu.VMEM((4, 128, 320), BF16),
        pltpu.VMEM((4, 32, 320), BF16),
        pltpu.VMEM((6, 8, 8, 128), F32),
        pltpu.VMEM((6, 8, 8, 128), F32),
        pltpu.VMEM((8, 128), F32),
        dma((18, 6)), dma((18, 6)),
        dma((6, 8)), dma((6, 8)), dma((6, 8)), dma((6, 8)),
        dma((2,)), dma((2,)), dma((3,)), dma((3,)), dma((3,)), dma((3,)), dma((3,)), dma((1,)),
    ]
    vmem = pl.BlockSpec(memory_space=pltpu.VMEM)
    out = pl.pallas_call(
        kernel,
        out_shape=jax.ShapeDtypeStruct((4, 32, 320), BF16),
        in_specs=[vmem] * (2 + len(tables)),
        out_specs=vmem,
        scratch_shapes=scratch,
        compiler_params=pltpu.CompilerParams(
            collective_id=0, has_side_effects=True, vmem_limit_bytes=62 * 1024 * 1024
        ),
        cost_estimate=pl.CostEstimate(
            flops=12_000_000_000, bytes_accessed=30_000_000, transcendentals=2_000_000
        ),
    )(fields, packs, *tables)
    return out[None]


def solution(mesh):
    return jax.shard_map(
        shards,
        mesh=mesh,
        in_specs=(P(None, "space", None, None), P("section", None, "space")),
        out_specs=P(None, "space", "section", None),
        check_vma=False,
    )
```

```python
import math

import jax
import jax.numpy as jnp
import numpy as np
from jax import lax
from jax.experimental import pallas as pl
from jax.experimental.pallas import tpu as pltpu
from jax.sharding import PartitionSpec as P

F32 = jnp.float32
BF16 = jnp.bfloat16
MESH = pl.DeviceIdType.MESH
EPSILON = 1e-05
CHUNK = 1536
HALF_A = 768
HALF_B = CHUNK - HALF_A
ROW_N = 512 * 10
LANES = 8 * CHUNK


def selections():
    rows = np.arange(512)
    slot, lane = rows // 16, rows % 16
    chan_fine = np.where(lane < 10, 10 * ((slot % 16) * 2 + slot // 16) + lane, -1)
    rows = np.arange(1024)
    slot, lane = rows // 16, rows % 16
    chan_wide = np.where(lane < 10, 10 * ((slot % 32) * 2 + slot // 32) + lane, -1)
    split = lambda n: np.concatenate([np.arange(0, n, 2), np.arange(1, n, 2)])
    di, di_wide = split(320), split(640)
    nat, nat_wide = np.arange(320), np.arange(640)
    eq = lambda a, b: (a[:, None] == b[None, :])
    b = np.arange(128)
    shifts = np.stack([eq(b, b + dx) for dx in (-1, 1)])
    strided = np.stack(
        [
            np.stack([eq(b, 2 * (b % 64) + dx) & (b // 64 == i)[None, :] for dx in (-1, 0, 1)])
            for i in (0, 1)
        ]
    )
    doubled = np.stack(
        [
            np.stack(
                [
                    eq(b, 64 * half + (b + dx) // 2) & ((b + dx >= 0) & (b + dx < 128))[None, :]
                    for dx in (-1, 0, 1)
                ]
            )
            for half in (0, 1)
        ]
    )

    def taps(rows_in, rows_out):
        a, c = np.arange(rows_in * 64), np.arange(rows_out * 64)
        out = []
        for dy in (0, 1, 2):
            for dx in (-1, 0, 1):
                col = c % 64 + dx
                out.append(
                    eq(a, (c // 64 + dy) * 64 + col) & ((col >= 0) & (col < 64))[None, :]
                )
        return np.stack(out)

    group = np.arange(128)
    fine_groups = np.stack(
        [eq(di // 10, group), eq(di // 20, group), eq(16 + di // 20, group)]
    )
    wide_groups = eq(nat_wide // 20, group)
    bf = lambda m: np.asarray(m, np.float32).astype(jnp.bfloat16)
    return (
        bf(eq(di, chan_fine)),
        bf(eq(nat, chan_fine)),
        bf(eq(chan_fine, di)),
        bf(eq(chan_fine, nat)),
        bf(eq(nat_wide, chan_wide)),
        bf(eq(chan_wide, nat_wide)),
        bf(eq(di, nat)),
        bf(eq(di_wide, nat_wide)),
        bf(shifts),
        bf(strided),
        bf(doubled),
        bf(taps(6, 4)),
        bf(taps(4, 2)),
        np.asarray(fine_groups, np.float32),
        np.asarray(wide_groups, np.float32),
    )


def dot(a, b):
    return jnp.dot(a, b, preferred_element_type=F32)


def activate(values, mean, rstd):
    z = (values - mean) * rstd
    return z / (1.0 + jnp.exp(-z))


def kernel(
    x_ref, w_ref, sel_di, sel_nat, exp_di, exp_nat, sel_c, exp_c, perm_x, perm_c, shifts, strided,
    doubled, taps_one, taps_two, fine_groups, wide_groups, out_ref,
    W, col, colw, colj, sh, xr, xd, hid, skd, skn, skb, cb, tile, a3, a2, hs, acc, ud, outs, landed,
    SA, HS, HR, gather_send, gather_recv, a_send, a_recv, b_send, b_recv,
    x_send, x_recv, c_send, c_recv, k_send, k_recv, o_send, o_recv,
):
    sec = lax.axis_index("section")
    d = lax.axis_index("space")
    c = lax.rem(d, 2)
    z = lax.rem(lax.div(d, 2), 2)
    x = lax.rem(lax.div(d, 4), 4)
    y = lax.div(d, 16)
    space = lambda y, x, z, c: ((y * 4 + x) * 2 + z) * 2 + c
    xp, xm = lax.rem(x + 1, 4), lax.rem(x + 3, 4)
    yp, ym = lax.rem(y + 1, 4), lax.rem(y + 3, 4)
    below, above = lax.rem(d + 1, 64), lax.rem(d + 63, 64)
    after, before = lax.rem(sec + 1, 4), lax.rem(sec + 3, 4)
    is_top = d == 0
    is_bottom = d == 63
    keep_top = jnp.where(is_top, 0.0, 1.0)
    keep_bottom = jnp.where(is_bottom, 0.0, 1.0)

    barrier = pltpu.get_barrier_semaphore()
    peers = [(lax.rem(sec + 2, 4), d)]
    for other in (after, before):
        peers += [(other, d), (other, below), (other, above)]
    for peer in peers:
        pl.semaphore_signal(barrier, inc=1, device_id=peer, device_id_type=MESH)

    def greet(k, carry):
        peer = (sec, lax.rem(d + k, 64))
        pl.semaphore_signal(barrier, inc=1, device_id=peer, device_id_type=MESH)
        return carry

    lax.fori_loop(1, 64, greet, 0)

    W[c, y, x, pl.ds(pl.multiple_of(16 * z, 16), 16), :] = w_ref[...]
    pl.semaphore_wait(barrier, len(peers) + 63)

    def remote(src, dst, send, recv, peer):
        return pltpu.make_async_remote_copy(
            src_ref=src, dst_ref=dst, send_sem=send, recv_sem=recv, device_id=peer,
            device_id_type=MESH,
        )

    def combined(messages, count):
        means = messages[:, 0:1, :]
        mean = jnp.sum(means, axis=0) * (1.0 / 64)
        spread = jnp.sum(jnp.square(means - mean[None]), axis=0) * count
        squares = jnp.sum(messages[:, 1:2, :], axis=0) + spread
        return mean, lax.rsqrt(squares * (1.0 / (64 * count)) + EPSILON)

    def part_sums(blocks, groups, count, weight=None):
        total = blocks[0] if weight is None else blocks[0] * weight
        for block in blocks[1:]:
            total = total + block
        channel = jnp.sum(total, axis=1, keepdims=True)
        mean = jnp.sum(groups * channel, axis=0, keepdims=True) * (1.0 / count)
        own = jnp.sum(groups * mean, axis=1, keepdims=True)
        squares = None
        for block in blocks:
            off = jnp.square(block - own)
            off = off if weight is None else off * weight
            squares = off if squares is None else squares + off
        channel = jnp.sum(squares, axis=1, keepdims=True)
        return mean, jnp.sum(groups * channel, axis=0, keepdims=True)

    def start_exchange(e, mean, deviation):
        SA[e, 0] = jnp.concatenate([mean, deviation], axis=0)

        def one(k, carry):
            peer = (sec, lax.rem(d + k, 64))
            remote(SA.at[e, 0], SA.at[e, k], a_send.at[e], a_recv.at[e], peer).start()
            return carry

        lax.fori_loop(1, 64, one, 0)

    def finish_exchange(e, count):
        others = SA.at[e, pl.ds(1, 63)]
        remote(others, others, a_send.at[e], a_recv.at[e], (sec, below)).wait()
        return combined(SA[e], count)

    def exchanged(e, mean, deviation, count):
        start_exchange(e, mean, deviation)
        return finish_exchange(e, count)

    def columns(groups, rows):
        return [jnp.sum(groups * row, axis=1, keepdims=True) for row in rows]

    def across_copy():
        return remote(HS, HR, b_send.at[0], b_recv.at[0], (after, d))

    def tile_copies():
        return [
            remote(tile, cb.at[slot], c_send.at[slot], c_recv.at[slot], (after, peer))
            for slot, peer in ((1, d), (0, below), (2, above))
        ]

    def skip_copies():
        return [
            remote(skd.at[lax_rows(1, 4)], skb.at[lax_rows(2, 4)], k_send.at[0], k_recv.at[0], (before, d)),
            remote(skd.at[lax_rows(3, 2)], skb.at[lax_rows(0, 2)], k_send.at[1], k_recv.at[1], (before, below)),
            remote(skd.at[lax_rows(1, 2)], skb.at[lax_rows(6, 2)], k_send.at[2], k_recv.at[2], (before, above)),
        ]

    def lax_rows(start, size):
        return pl.ds(start, size)

    def hand_over(count):
        for copy in tile_copies():
            copy.start()
        mean, deviation = part_sums([tile[...].astype(F32)], wide_groups[...], count)
        HS[...] = jnp.concatenate(exchanged(2, mean, deviation, count), axis=0)
        across_copy().start()
        for copy in tile_copies() + [across_copy()]:
            copy.wait_send()

    def take_over():
        for copy in tile_copies() + [across_copy()]:
            copy.wait_recv()

    chunks = jnp.where(sec == 0, 4, jnp.where(sec == 3, 5, 8))

    def gather_copies(stage, k):
        lane = lambda off, size: pl.ds(pl.multiple_of(k * CHUNK + off, 128), size)
        whole, part_a, part_b = lane(0, CHUNK), lane(0, HALF_A), lane(HALF_A, HALF_B)
        to_xp, to_xm = space(y, xp, z, c), space(y, xm, z, c)
        to_yp, to_ym = space(yp, x, z, c), space(ym, x, z, c)
        all32, first, second = pl.ds(0, 32), pl.ds(0, 16), pl.ds(16, 16)
        every, low, high = pl.ds(0, 4), pl.ds(0, 2), pl.ds(2, 2)
        if stage == 0:
            moves = [((c, y, x, pl.ds(pl.multiple_of(16 * z, 16), 16), whole), space(y, x, 1 - z, c))]
        elif stage == 1:
            a, b = (c, y, x, all32, part_a), (c, y, x, all32, part_b)
            moves = [(a, to_xp), (a, to_xm), (b, to_yp), (b, to_ym)]
        elif stage == 2:
            moves = [
                ((c, y, xm, first, part_a), to_xp),
                ((c, y, xp, second, part_a), to_xm),
                ((c, ym, x, first, part_b), to_yp),
                ((c, yp, x, second, part_b), to_ym),
            ]
        elif stage == 3:
            a, b = (c, y, every, all32, part_a), (c, every, x, all32, part_b)
            moves = [(a, to_yp), (a, to_ym), (b, to_xp), (b, to_xm)]
        elif stage == 4:
            moves = [
                ((c, ym, low, all32, part_a), to_yp),
                ((c, yp, high, all32, part_a), to_ym),
                ((c, low, xm, all32, part_b), to_xp),
                ((c, high, xp, all32, part_b), to_xm),
            ]
        else:
            moves = [((c, every, every, all32, whole), space(y, x, z, 1 - c))]
        first_id = (0, 1, 5, 9, 13, 17)[stage]
        return [
            remote(
                W.at[where], W.at[where], gather_send.at[first_id + i, k],
                gather_recv.at[first_id + i, k], (sec, peer),
            )
            for i, (where, peer) in enumerate(moves)
        ]

    def gather(first, last):
        def step(t, carry):
            for stage in range(7):
                k = t - stage

                @pl.when((k >= 0) & (k < chunks))
                def _():
                    if stage > 0:
                        for copy in gather_copies(stage - 1, k):
                            copy.wait_recv()
                    if stage < 6:
                        for copy in gather_copies(stage, k):
                            copy.start()

            return carry

        lax.fori_loop(first, last, step, 0)

    def gather_end():
        def step(k, carry):
            for stage in range(6):
                for copy in gather_copies(stage, k):
                    copy.wait_send()
            return carry

        lax.fori_loop(0, chunks, step, 0)

    def put_shifted(index, base, values):
        size = values.shape[0]
        sh[1, index, base : base + size, :] = values
        sh[0, index, base : base + size, :] = dot(values, shifts[0]).astype(BF16)
        sh[2, index, base : base + size, :] = dot(values, shifts[1]).astype(BF16)

    def fine_conv(pairs, pieces, per_tap, lead, lane_start, depth, source_row, use):
        taps = 9 * per_tap
        for p in range(2):
            if lead:
                col[p, 0:lead, :] = jnp.zeros((lead, 256), BF16)
            if lead + taps < depth:
                col[p, lead + taps : depth, :] = jnp.zeros((depth - lead - taps, 256), BF16)

        def pair(q, carry):
            for p in range(2):
                for dy in range(3):
                    for j in range(2):
                        row = source_row(q, j + dy)
                        for dx in range(3):
                            at = lead + (dy * 3 + dx) * per_tap
                            for to, start, size in pieces(p):
                                col[p, at + to : at + to + size, 128 * j : 128 * j + 128] = sh[
                                    dx, row, start : start + size, :
                                ]
            use(q, weighted(lane_start, depth, col))
            return carry

        lax.fori_loop(0, pairs, pair, 0)

    def weighted(lane_start, depth, source):
        total = None
        for p in range(2):
            kernels = W[:, 2 * p : 2 * p + 2, :, :, lane_start : lane_start + depth]
            made = dot(kernels.reshape(512, depth), source[p, 0:depth, :])
            total = made if total is None else total + made
        return total

    narrow_pieces = lambda p: [(0, 160 * p, 160)]
    wide_pieces = lambda p: [(0, 320 * p, 320)]
    joined_pieces = lambda p: [(0, 160 * p, 160), (160, 320 + 160 * p, 160)]
    follow = lambda q, off: 2 * q + off
    narrow_scale = 1.0 / math.sqrt(9 * 320)
    wide_scale = 1.0 / math.sqrt(9 * 640)

    def row_kept(row):
        return jnp.where(row < 0, keep_top, jnp.where(row > 3, keep_bottom, 1.0))

    def activate_rows(source, count, first_row, mean, rstd):
        def one(r, carry):
            values = activate(source[r].astype(F32), mean, rstd) * row_kept(r + first_row)
            put_shifted(r, 0, values.astype(BF16))
            return carry

        lax.fori_loop(0, count, one, 0)

    @pl.when(sec == 0)
    def _():
        x_copies = [
            remote(x_ref.at[pl.ds(1, 3)], xr.at[pl.ds(0, 3)], x_send.at[0], x_recv.at[0], (0, below)),
            remote(x_ref.at[pl.ds(0, 2)], xr.at[pl.ds(7, 2)], x_send.at[1], x_recv.at[1], (0, above)),
        ]
        for copy in x_copies:
            copy.start()
        for r in range(4):
            xr[3 + r] = x_ref[r]
        xr[9] = jnp.zeros((320, 128), BF16)

        def permute(r, carry):
            xd[r] = dot(perm_x[...], xr[r]).astype(BF16)
            return carry

        lax.fori_loop(3, 7, permute, 0)
        groups = fine_groups[0]
        start_exchange(0, *part_sums([xd[r].astype(F32) for r in range(3, 7)], groups, ROW_N))
        gather(0, 7)
        for copy in x_copies:
            copy.wait()
        lax.fori_loop(0, 3, permute, 0)
        lax.fori_loop(7, 10, permute, 0)
        mean, rstd = columns(groups, finish_exchange(0, ROW_N))
        activate_rows(xd, 10, -3, mean, rstd)

        def keep_hidden(q, made):
            rounded = (made * narrow_scale).astype(BF16)
            packed = dot(sel_di[...], rounded).astype(BF16)
            hid[2 * q] = packed[:, 0:128]
            hid[2 * q + 1] = packed[:, 128:256]

        fine_conv(4, narrow_pieces, 160, 0, 0, 1536, follow, keep_hidden)
        gather(7, 8)
        sums = part_sums([hid[r].astype(F32) for r in range(2, 6)], groups, ROW_N)
        mean, rstd = columns(groups, exchanged(1, *sums, ROW_N))
        activate_rows(hid, 8, -2, mean, rstd)

        def keep_skip(q, made):
            for j in range(2):
                own = dot(exp_di[...], xd[2 * q + j + 2])
                rounded = (own + made[:, 128 * j : 128 * j + 128] * narrow_scale).astype(BF16)
                skd[2 * q + j] = dot(sel_di[...], rounded).astype(BF16)
                skn[2 * q + j] = dot(sel_nat[...], rounded).astype(BF16)

        fine_conv(3, narrow_pieces, 160, 32, 1408, 1536, follow, keep_skip)
        for copy in skip_copies():
            copy.start()
        gather(8, 10)
        skn[0] = (skn[0].astype(F32) * keep_top).astype(BF16)
        col[0, 0:64, 0:128] = jnp.zeros((64, 128), BF16)
        for dy in range(3):
            for dx in range(3):
                at = 64 + (dy * 3 + dx) * 320
                made = dot(skn[dy], strided[0, dx]) + dot(skn[2 + dy], strided[1, dx])
                col[0, at : at + 320, 0:128] = made.astype(BF16)
        made = dot(W[:, :, :, :, 2816:5760].reshape(1024, 2944), col[0, :, 0:128])
        rounded = (made * narrow_scale).astype(BF16)
        tile[...] = dot(sel_c[...], rounded).astype(BF16)
        hand_over(128 * 20)
        for copy in skip_copies():
            copy.wait_send()

    @pl.when((sec == 1) | (sec == 2))
    def _():
        gather(0, chunks + 6)
        take_over()
        count = 128 * 20
        groups = wide_groups[...]
        mean, rstd = columns(groups, [HR[0:1, :], HR[1:2, :]])
        for i in range(3):
            values = activate(cb[i].astype(F32), mean, rstd)
            values = values * (keep_top, 1.0, keep_bottom)[i]
            a3[:, 128 * i : 128 * i + 128] = values.astype(BF16)

        for t in range(9):
            colw[640 * t : 640 * t + 640, :] = dot(a3[...], taps_one[t]).astype(BF16)
        for i in range(3):
            lanes = slice(1920 * i, 1920 * i + 1920)
            made = dot(W[:, :, :, :, lanes].reshape(1024, 1920), colw[lanes, :])
            acc[...] = made if i == 0 else acc[...] + made
        rounded = (acc[...] * wide_scale).astype(BF16)
        hs[...] = dot(sel_c[...], rounded)
        column = lax.broadcasted_iota(jnp.int32, (1, 256), 1)
        inner = jnp.where((column >= 64) & (column < 192), 1.0, 0.0)
        kept = jnp.where(column < 64, keep_top, jnp.where(column >= 192, keep_bottom, 1.0))
        sums = part_sums([hs[...]], groups, count, inner)
        mean, rstd = columns(groups, exchanged(3, *sums, count))
        a2[...] = (activate(hs[...], mean, rstd) * kept).astype(BF16)
        for t in range(9):
            colw[640 * t : 640 * t + 640, 0:128] = dot(a2[...], taps_two[t]).astype(BF16)
        for i in range(3):
            lanes = slice(5760 + 1920 * i, 5760 + 1920 * i + 1920)
            source = colw[1920 * i : 1920 * i + 1920, 0:128]
            made = dot(W[:, :, :, :, lanes].reshape(1024, 1920), source)
            acc[:, 0:128] = made if i == 0 else acc[:, 0:128] + made
        own = dot(exp_c[...], cb[1])
        rounded = (own + acc[:, 0:128] * wide_scale).astype(BF16)
        tile[...] = dot(sel_c[...], rounded).astype(BF16)
        hand_over(count)

    def out_copies(sections=range(3)):
        return [
            remote(
                outs.at[pl.ds(0, 4), pl.ds(32 * t, 32)], landed, o_send.at[t], o_recv.at[0], (t, d)
            )
            for t in sections
        ]

    @pl.when(sec == 3)
    def _():
        gather(0, chunks + 6)
        for copy in skip_copies():
            copy.wait_recv()
        take_over()
        for i in range(3):
            moved = dot(perm_c[...], cb[i]) * (keep_top, 1.0, keep_bottom)[i]
            moved = moved.astype(BF16)
            for half in range(2):
                for dx in range(3):
                    sh[dx, 2 * i + half] = dot(moved, doubled[half, dx]).astype(BF16)

        def keep_upper(q, made):
            rounded = (made * wide_scale).astype(BF16)
            packed = dot(sel_di[...], rounded).astype(BF16)
            ud[2 * q] = packed[:, 0:128]
            ud[2 * q + 1] = packed[:, 128:256]

        half_row = lambda q, off: q + (off + 1) // 2
        fine_conv(4, wide_pieces, 320, 0, 0, 2944, half_row, keep_upper)
        groups_u, groups_s = fine_groups[1], fine_groups[2]
        mean_u, dev_u = part_sums([ud[r].astype(F32) for r in range(2, 6)], groups_u, 2 * ROW_N)
        mean_s, dev_s = part_sums([skb[r].astype(F32) for r in range(2, 6)], groups_s, 2 * ROW_N)
        rows = exchanged(4, mean_u + mean_s, dev_u + dev_s, 2 * ROW_N)
        mean_u, rstd_u = columns(groups_u, rows)
        mean_s, rstd_s = columns(groups_s, rows)

        def joined_row(r, carry):
            kept = row_kept(r - 2)
            upper = activate(ud[r].astype(F32), mean_u, rstd_u) * kept
            put_shifted(r, 0, upper.astype(BF16))
            lower = activate(skb[r].astype(F32), mean_s, rstd_s) * kept
            put_shifted(r, 320, lower.astype(BF16))
            return carry

        lax.fori_loop(0, 8, joined_row, 0)

        def keep_hidden(q, made):
            rounded = (made * wide_scale).astype(BF16)
            packed = dot(sel_di[...], rounded).astype(BF16)
            hid[2 * q] = packed[:, 0:128]
            hid[2 * q + 1] = packed[:, 128:256]

        fine_conv(3, joined_pieces, 320, 64, 2816, 2944, follow, keep_hidden)
        groups = fine_groups[0]
        sums = part_sums([hid[r].astype(F32) for r in range(1, 5)], groups, ROW_N)
        mean, rstd = columns(groups, exchanged(5, *sums, ROW_N))
        activate_rows(hid, 6, -1, mean, rstd)
        for p in range(2):
            colj[p, 0:32, :] = jnp.zeros((32, 256), BF16)
            colj[p, 352:384, :] = jnp.zeros((32, 256), BF16)

        def keep_output(q, made):
            for p in range(2):
                for j in range(2):
                    px = slice(128 * j, 128 * j + 128)
                    colj[p, 32:192, px] = ud[2 * q + j + 2, 160 * p : 160 * p + 160, :]
                    colj[p, 192:352, px] = skb[2 * q + j + 2, 160 * p : 160 * p + 160, :]
            straight = weighted(7168, 384, colj)
            total = made * narrow_scale + straight * (1.0 / math.sqrt(640))
            rounded = total.astype(BF16)
            for j in range(2):
                flipped = lax.dot_general(
                    rounded[:, 128 * j : 128 * j + 128], exp_nat[...], (((0,), (0,)), ((), ())),
                    preferred_element_type=F32,
                )
                outs[2 * q + j] = flipped.astype(BF16)

        fine_conv(2, narrow_pieces, 160, 0, 5760, 1536, follow, keep_output)
        for copy in out_copies():
            copy.start()
        out_ref[...] = outs[:, 96:128, :]
        for copy in out_copies():
            copy.wait_send()

    @pl.when(sec < 3)
    def _():
        for copy in out_copies((0,)):
            copy.wait_recv()
        out_ref[...] = landed[...]

    gather_end()


def shards(features, section_packs):
    fields = jnp.swapaxes(features[0], 1, 2)
    packs = jnp.pad(jnp.swapaxes(section_packs[0], 0, 1), ((0, 6), (0, LANES - 11520)))
    tables = selections()
    dma = pltpu.SemaphoreType.DMA
    scratch = [
        pltpu.VMEM((2, 4, 4, 32, LANES), BF16),
        pltpu.VMEM((2, 2944, 256), BF16),
        pltpu.VMEM((5760, 256), BF16),
        pltpu.VMEM((2, 384, 256), BF16),
        pltpu.VMEM((3, 10, 640, 128), BF16),
        pltpu.VMEM((10, 320, 128), BF16),
        pltpu.VMEM((10, 320, 128), BF16),
        pltpu.VMEM((8, 320, 128), BF16),
        pltpu.VMEM((6, 320, 128), BF16),
        pltpu.VMEM((6, 320, 128), BF16),
        pltpu.VMEM((8, 320, 128), BF16),
        pltpu.VMEM((3, 640, 128), BF16),
        pltpu.VMEM((640, 128), BF16),
        pltpu.VMEM((640, 384), BF16),
        pltpu.VMEM((640, 256), BF16),
        pltpu.VMEM((640, 256), F32),
        pltpu.VMEM((1024, 256), F32),
        pltpu.VMEM((8, 320, 128), BF16),
        pltpu.VMEM((4, 128, 320), BF16),
        pltpu.VMEM((4, 32, 320), BF16),
        pltpu.VMEM((6, 64, 2, 128), F32),
        pltpu.VMEM((2, 128), F32),
        pltpu.VMEM((2, 128), F32),
        dma((18, 8)), dma((18, 8)),
        dma((6,)), dma((6,)), dma((1,)), dma((1,)),
        dma((2,)), dma((2,)), dma((3,)), dma((3,)), dma((3,)), dma((3,)), dma((3,)), dma((1,)),
    ]
    vmem = pl.BlockSpec(memory_space=pltpu.VMEM)
    out = pl.pallas_call(
        kernel,
        out_shape=jax.ShapeDtypeStruct((4, 32, 320), BF16),
        in_specs=[vmem] * (2 + len(tables)),
        out_specs=vmem,
        scratch_shapes=scratch,
        compiler_params=pltpu.CompilerParams(
            collective_id=0, has_side_effects=True, vmem_limit_bytes=62 * 1024 * 1024
        ),
        cost_estimate=pl.CostEstimate(
            flops=12_000_000_000, bytes_accessed=30_000_000, transcendentals=2_000_000
        ),
    )(fields, packs, *tables)
    return out[None]


def solution(mesh):
    return jax.shard_map(
        shards,
        mesh=mesh,
        in_specs=(P(None, "space", None, None), P("section", None, "space")),
        out_specs=P(None, "space", "section", None),
        check_vma=False,
    )
```

```python
import math

import jax
import jax.numpy as jnp
import numpy as np
from jax import lax
from jax.experimental import pallas as pl
from jax.experimental.pallas import tpu as pltpu
from jax.sharding import PartitionSpec as P

F32 = jnp.float32
BF16 = jnp.bfloat16
MESH = pl.DeviceIdType.MESH
EPSILON = 1e-05
CHUNK = 1536
HALF = CHUNK // 2
QUARTER = CHUNK // 4
ROW_N = 512 * 10
LANES = 8 * CHUNK


def selections():
    rows = np.arange(768)
    chan_wide = np.where(rows % 48 < 40, 40 * (rows // 48) + rows % 48, -1)
    chan_fine = chan_wide[:384]
    rows = np.arange(48)
    packed = np.where(rows < 40, 16 * (rows // 10) + rows % 10, -1)
    split = lambda n: np.concatenate([np.arange(0, n, 2), np.arange(1, n, 2)])
    di, di_wide = split(320), split(640)
    nat, nat_wide = np.arange(320), np.arange(640)
    eq = lambda a, b: (a[:, None] == b[None, :])
    b = np.arange(128)
    shifts = np.stack([eq(b, b + dx) for dx in (-1, 1)])
    strided = np.stack(
        [
            np.stack([eq(b, 2 * (b % 64) + dx) & (b // 64 == i)[None, :] for dx in (-1, 0, 1)])
            for i in (0, 1)
        ]
    )
    doubled = np.stack(
        [
            np.stack(
                [
                    eq(b, 64 * half + (b + dx) // 2) & ((b + dx >= 0) & (b + dx < 128))[None, :]
                    for dx in (-1, 0, 1)
                ]
            )
            for half in (0, 1)
        ]
    )

    def taps(rows_in, rows_out):
        a, c = np.arange(rows_in * 64), np.arange(rows_out * 64)
        out = []
        for dy in (0, 1, 2):
            for dx in (-1, 0, 1):
                col = c % 64 + dx
                out.append(
                    eq(a, (c // 64 + dy) * 64 + col) & ((col >= 0) & (col < 64))[None, :]
                )
        return np.stack(out)

    group = np.arange(128)
    fine_groups = np.stack(
        [eq(di // 10, group), eq(di // 20, group), eq(16 + di // 20, group)]
    )
    wide_groups = eq(nat_wide // 20, group)
    bf = lambda m: np.asarray(m, np.float32).astype(jnp.bfloat16)
    return (
        bf(eq(packed, np.arange(64))),
        bf(eq(di, chan_fine)),
        bf(eq(nat, chan_fine)),
        bf(eq(chan_fine, di)),
        bf(eq(chan_fine, nat)),
        bf(eq(nat_wide, chan_wide)),
        bf(eq(chan_wide, nat_wide)),
        bf(eq(di, nat)),
        bf(eq(di_wide, nat_wide)),
        bf(shifts),
        bf(strided),
        bf(doubled),
        bf(taps(6, 4)),
        bf(taps(4, 2)),
        np.asarray(fine_groups, np.float32),
        np.asarray(wide_groups, np.float32),
    )


def dot(a, b):
    return jnp.dot(a, b, preferred_element_type=F32)


def activate(values, mean, rstd):
    z = (values - mean) * rstd
    return z / (1.0 + jnp.exp(-z))


def kernel(
    x_ref, w_ref, pack, sel_di, sel_nat, exp_di, exp_nat, sel_c, exp_c, perm_x, perm_c, shifts, strided,
    doubled, taps_one, taps_two, fine_groups, wide_groups, out_ref,
    W, raw, col, colw, colj, sh, xr, xd, hid, skd, skn, skb, cb, tile, a3, a2, hs, acc, ud, outs, landed,
    SA, HS, HR, gather_send, gather_recv, a_send, a_recv, b_send, b_recv,
    x_send, x_recv, c_send, c_recv, k_send, k_recv, o_send, o_recv,
):
    sec = lax.axis_index("section")
    d = lax.axis_index("space")
    c = lax.rem(d, 2)
    z = lax.rem(lax.div(d, 2), 2)
    x = lax.rem(lax.div(d, 4), 4)
    y = lax.div(d, 16)
    space = lambda y, x, z, c: ((y * 4 + x) * 2 + z) * 2 + c
    xp, xm = lax.rem(x + 1, 4), lax.rem(x + 3, 4)
    yp, ym = lax.rem(y + 1, 4), lax.rem(y + 3, 4)
    below, above = lax.rem(d + 1, 64), lax.rem(d + 63, 64)
    after, before = lax.rem(sec + 1, 4), lax.rem(sec + 3, 4)
    is_top = d == 0
    is_bottom = d == 63
    keep_top = jnp.where(is_top, 0.0, 1.0)
    keep_bottom = jnp.where(is_bottom, 0.0, 1.0)

    barrier = pltpu.get_barrier_semaphore()
    peers = [(lax.rem(sec + 2, 4), d)]
    for other in (after, before):
        peers += [(other, d), (other, below), (other, above)]
    for peer in peers:
        pl.semaphore_signal(barrier, inc=1, device_id=peer, device_id_type=MESH)

    def greet(k, carry):
        peer = (sec, lax.rem(d + k, 64))
        pl.semaphore_signal(barrier, inc=1, device_id=peer, device_id_type=MESH)
        return carry

    lax.fori_loop(1, 64, greet, 0)

    raw[2 * z + c] = w_ref[...]
    pl.semaphore_wait(barrier, len(peers) + 63)

    def remote(src, dst, send, recv, peer):
        return pltpu.make_async_remote_copy(
            src_ref=src, dst_ref=dst, send_sem=send, recv_sem=recv, device_id=peer,
            device_id_type=MESH,
        )

    def combined(messages, count):
        means = messages[:, 0:1, :]
        mean = jnp.sum(means, axis=0) * (1.0 / 64)
        spread = jnp.sum(jnp.square(means - mean[None]), axis=0) * count
        squares = jnp.sum(messages[:, 1:2, :], axis=0) + spread
        return mean, lax.rsqrt(squares * (1.0 / (64 * count)) + EPSILON)

    def part_sums(blocks, groups, count, weight=None):
        total = blocks[0] if weight is None else blocks[0] * weight
        for block in blocks[1:]:
            total = total + block
        channel = jnp.sum(total, axis=1, keepdims=True)
        mean = jnp.sum(groups * channel, axis=0, keepdims=True) * (1.0 / count)
        own = jnp.sum(groups * mean, axis=1, keepdims=True)
        squares = None
        for block in blocks:
            off = jnp.square(block - own)
            off = off if weight is None else off * weight
            squares = off if squares is None else squares + off
        channel = jnp.sum(squares, axis=1, keepdims=True)
        return mean, jnp.sum(groups * channel, axis=0, keepdims=True)

    def start_exchange(e, mean, deviation):
        SA[e, 0] = jnp.concatenate([mean, deviation], axis=0)

        def one(k, carry):
            peer = (sec, lax.rem(d + k, 64))
            remote(SA.at[e, 0], SA.at[e, k], a_send.at[e], a_recv.at[e], peer).start()
            return carry

        lax.fori_loop(1, 64, one, 0)

    def finish_exchange(e, count):
        others = SA.at[e, pl.ds(1, 63)]
        remote(others, others, a_send.at[e], a_recv.at[e], (sec, below)).wait()
        return combined(SA[e], count)

    def exchanged(e, mean, deviation, count):
        start_exchange(e, mean, deviation)
        return finish_exchange(e, count)

    def columns(groups, rows):
        return [jnp.sum(groups * row, axis=1, keepdims=True) for row in rows]

    def across_copy():
        return remote(HS, HR, b_send.at[0], b_recv.at[0], (after, d))

    def tile_copies():
        return [
            remote(tile, cb.at[slot], c_send.at[slot], c_recv.at[slot], (after, peer))
            for slot, peer in ((1, d), (0, below), (2, above))
        ]

    def skip_copies():
        return [
            remote(skd.at[lax_rows(1, 4)], skb.at[lax_rows(2, 4)], k_send.at[0], k_recv.at[0], (before, d)),
            remote(skd.at[lax_rows(3, 2)], skb.at[lax_rows(0, 2)], k_send.at[1], k_recv.at[1], (before, below)),
            remote(skd.at[lax_rows(1, 2)], skb.at[lax_rows(6, 2)], k_send.at[2], k_recv.at[2], (before, above)),
        ]

    def lax_rows(start, size):
        return pl.ds(start, size)

    def hand_over(count):
        for copy in tile_copies():
            copy.start()
        mean, deviation = part_sums([tile[...].astype(F32)], wide_groups[...], count)
        HS[...] = jnp.concatenate(exchanged(2, mean, deviation, count), axis=0)
        across_copy().start()
        for copy in tile_copies() + [across_copy()]:
            copy.wait_send()

    def take_over():
        for copy in tile_copies() + [across_copy()]:
            copy.wait_recv()

    chunks = jnp.where(sec == 0, 4, jnp.where(sec == 3, 5, 8))

    def gather_copies(core, stage, k):
        lanes = lambda off, size: pl.ds(pl.multiple_of(k * CHUNK + off, 128), size)
        mine, other = lanes(HALF * core, HALF), lanes(HALF * (1 - core), HALF)
        left, right = lanes(HALF * core, QUARTER), lanes(HALF * core + QUARTER, QUARTER)
        along_x = (space(y, xp, z, c), space(y, xm, z, c))
        along_y = (space(yp, x, z, c), space(ym, x, z, c))
        rows, every = pl.ds(0, 48), pl.ds(0, 4)
        array = W
        if stage == 0:
            array, whole = raw, pl.ds(0, 16)
            moves = [
                ((2 * z + c, whole, mine), space(y, x, 1 - z, c)),
                ((2 * z + c, whole, other), space(y, x, 1 - z, 1 - c)),
                ((2 * z + c, whole, other), space(y, x, z, 1 - c)),
            ]
        elif stage == 1:
            moves = [((y, x, rows, mine), peer) for peer in (along_y if core else along_x)]
        elif stage == 2 and core == 0:
            moves = [((y, xm, rows, left), along_x[0]), ((y, xp, rows, right), along_x[1])]
        elif stage == 2:
            moves = [((ym, x, rows, left), along_y[0]), ((yp, x, rows, right), along_y[1])]
        elif stage == 3 and core == 0:
            moves = [((y, every, rows, mine), peer) for peer in along_y]
        elif stage == 3:
            moves = [((every, x, rows, mine), peer) for peer in along_x]
        elif stage == 4 and core == 0:
            moves = [((ym, every, rows, left), along_y[0]), ((yp, every, rows, right), along_y[1])]
        elif stage == 4:
            moves = [((every, xm, rows, left), along_x[0]), ((every, xp, rows, right), along_x[1])]
        else:
            moves = [((every, every, rows, mine), space(y, x, z, 1 - c))]
        first_id = (0, 3, 5, 7, 9, 11)[stage]
        return [
            remote(
                array.at[where], array.at[where], gather_send.at[first_id + i, k],
                gather_recv.at[first_id + i, k], (sec, peer),
            )
            for i, (where, peer) in enumerate(moves)
        ]

    def gather_step(core, t):
        for stage in range(7):
            k = t - stage

            @pl.when((k >= 0) & (k < chunks))
            def _():
                if stage > 0:
                    for copy in gather_copies(core, stage - 1, k):
                        copy.wait_recv()
                if stage == 1:
                    lanes = pl.ds(pl.multiple_of(k * CHUNK + HALF * core, 128), HALF)
                    blocks = raw[:, :, lanes].reshape(64, HALF)
                    W[y, x, :, lanes] = dot(pack[...], blocks).astype(BF16)
                if stage < 6:
                    for copy in gather_copies(core, stage, k):
                        copy.start()

    def gather(first, last):
        def step(t, carry):
            for core in range(2):
                pl.when(c == core)(lambda core=core: gather_step(core, t))
            return carry

        lax.fori_loop(first, last, step, 0)

    def gather_end():
        def waits(core, k):
            for stage in range(6):
                for copy in gather_copies(core, stage, k):
                    copy.wait_send()

        def step(k, carry):
            for core in range(2):
                pl.when(c == core)(lambda core=core: waits(core, k))
            return carry

        lax.fori_loop(0, chunks, step, 0)

    def put_shifted(index, base, values):
        size = values.shape[0]
        sh[1, index, base : base + size, :] = values
        sh[0, index, base : base + size, :] = dot(values, shifts[0]).astype(BF16)
        sh[2, index, base : base + size, :] = dot(values, shifts[1]).astype(BF16)

    def fine_conv(pairs, pieces, per_tap, lead, lane_start, depth, source_row, use):
        taps = 9 * per_tap
        for p in range(2):
            if lead:
                col[p, 0:lead, :] = jnp.zeros((lead, 256), BF16)
            if lead + taps < depth:
                col[p, lead + taps : depth, :] = jnp.zeros((depth - lead - taps, 256), BF16)

        def pair(q, carry):
            for p in range(2):
                for dy in range(3):
                    for j in range(2):
                        row = source_row(q, j + dy)
                        for dx in range(3):
                            at = lead + (dy * 3 + dx) * per_tap
                            for to, start, size in pieces(p):
                                col[p, at + to : at + to + size, 128 * j : 128 * j + 128] = sh[
                                    dx, row, start : start + size, :
                                ]
            use(q, weighted(lane_start, depth, col))
            return carry

        lax.fori_loop(0, pairs, pair, 0)

    def weighted(lane_start, depth, source):
        total = None
        for p in range(2):
            kernels = W[2 * p : 2 * p + 2, :, :, lane_start : lane_start + depth]
            made = dot(kernels.reshape(384, depth), source[p, 0:depth, :])
            total = made if total is None else total + made
        return total

    narrow_pieces = lambda p: [(0, 160 * p, 160)]
    wide_pieces = lambda p: [(0, 320 * p, 320)]
    joined_pieces = lambda p: [(0, 160 * p, 160), (160, 320 + 160 * p, 160)]
    follow = lambda q, off: 2 * q + off
    narrow_scale = 1.0 / math.sqrt(9 * 320)
    wide_scale = 1.0 / math.sqrt(9 * 640)

    def row_kept(row):
        return jnp.where(row < 0, keep_top, jnp.where(row > 3, keep_bottom, 1.0))

    def activate_rows(source, count, first_row, mean, rstd):
        def one(r, carry):
            values = activate(source[r].astype(F32), mean, rstd) * row_kept(r + first_row)
            put_shifted(r, 0, values.astype(BF16))
            return carry

        lax.fori_loop(0, count, one, 0)

    @pl.when(sec == 0)
    def _():
        x_copies = [
            remote(x_ref.at[pl.ds(1, 3)], xr.at[pl.ds(0, 3)], x_send.at[0], x_recv.at[0], (0, below)),
            remote(x_ref.at[pl.ds(0, 2)], xr.at[pl.ds(7, 2)], x_send.at[1], x_recv.at[1], (0, above)),
        ]
        for copy in x_copies:
            copy.start()
        for r in range(4):
            xr[3 + r] = x_ref[r]
        xr[9] = jnp.zeros((320, 128), BF16)

        def permute(r, carry):
            xd[r] = dot(perm_x[...], xr[r]).astype(BF16)
            return carry

        lax.fori_loop(3, 7, permute, 0)
        groups = fine_groups[0]
        start_exchange(0, *part_sums([xd[r].astype(F32) for r in range(3, 7)], groups, ROW_N))
        gather(0, 7)
        for copy in x_copies:
            copy.wait()
        lax.fori_loop(0, 3, permute, 0)
        lax.fori_loop(7, 10, permute, 0)
        mean, rstd = columns(groups, finish_exchange(0, ROW_N))
        activate_rows(xd, 10, -3, mean, rstd)

        def keep_hidden(q, made):
            rounded = (made * narrow_scale).astype(BF16)
            packed = dot(sel_di[...], rounded).astype(BF16)
            hid[2 * q] = packed[:, 0:128]
            hid[2 * q + 1] = packed[:, 128:256]

        fine_conv(4, narrow_pieces, 160, 0, 0, 1536, follow, keep_hidden)
        start_exchange(1, *part_sums([hid[r].astype(F32) for r in range(2, 6)], groups, ROW_N))
        gather(7, 8)
        mean, rstd = columns(groups, finish_exchange(1, ROW_N))
        activate_rows(hid, 8, -2, mean, rstd)

        def keep_skip(q, made):
            for j in range(2):
                own = dot(exp_di[...], xd[2 * q + j + 2])
                rounded = (own + made[:, 128 * j : 128 * j + 128] * narrow_scale).astype(BF16)
                skd[2 * q + j] = dot(sel_di[...], rounded).astype(BF16)
                skn[2 * q + j] = dot(sel_nat[...], rounded).astype(BF16)

        fine_conv(3, narrow_pieces, 160, 32, 1408, 1536, follow, keep_skip)
        for copy in skip_copies():
            copy.start()
        gather(8, 10)
        skn[0] = (skn[0].astype(F32) * keep_top).astype(BF16)
        col[0, 0:64, 0:128] = jnp.zeros((64, 128), BF16)
        for dy in range(3):
            for dx in range(3):
                at = 64 + (dy * 3 + dx) * 320
                made = dot(skn[dy], strided[0, dx]) + dot(skn[2 + dy], strided[1, dx])
                col[0, at : at + 320, 0:128] = made.astype(BF16)
        made = dot(W[:, :, :, 2816:5760].reshape(768, 2944), col[0, :, 0:128])
        rounded = (made * narrow_scale).astype(BF16)
        tile[...] = dot(sel_c[...], rounded).astype(BF16)
        hand_over(128 * 20)
        for copy in skip_copies():
            copy.wait_send()

    @pl.when((sec == 1) | (sec == 2))
    def _():
        gather(0, chunks + 6)
        take_over()
        count = 128 * 20
        groups = wide_groups[...]
        mean, rstd = columns(groups, [HR[0:1, :], HR[1:2, :]])
        for i in range(3):
            values = activate(cb[i].astype(F32), mean, rstd)
            values = values * (keep_top, 1.0, keep_bottom)[i]
            a3[:, 128 * i : 128 * i + 128] = values.astype(BF16)

        for t in range(9):
            colw[640 * t : 640 * t + 640, :] = dot(a3[...], taps_one[t]).astype(BF16)
        for i in range(3):
            lanes = slice(1920 * i, 1920 * i + 1920)
            made = dot(W[:, :, :, lanes].reshape(768, 1920), colw[lanes, :])
            acc[...] = made if i == 0 else acc[...] + made
        rounded = (acc[...] * wide_scale).astype(BF16)
        hs[...] = dot(sel_c[...], rounded)
        column = lax.broadcasted_iota(jnp.int32, (1, 256), 1)
        inner = jnp.where((column >= 64) & (column < 192), 1.0, 0.0)
        kept = jnp.where(column < 64, keep_top, jnp.where(column >= 192, keep_bottom, 1.0))
        sums = part_sums([hs[...]], groups, count, inner)
        mean, rstd = columns(groups, exchanged(3, *sums, count))
        a2[...] = (activate(hs[...], mean, rstd) * kept).astype(BF16)
        for t in range(9):
            colw[640 * t : 640 * t + 640, 0:128] = dot(a2[...], taps_two[t]).astype(BF16)
        for i in range(3):
            lanes = slice(5760 + 1920 * i, 5760 + 1920 * i + 1920)
            source = colw[1920 * i : 1920 * i + 1920, 0:128]
            made = dot(W[:, :, :, lanes].reshape(768, 1920), source)
            acc[:, 0:128] = made if i == 0 else acc[:, 0:128] + made
        own = dot(exp_c[...], cb[1])
        rounded = (own + acc[:, 0:128] * wide_scale).astype(BF16)
        tile[...] = dot(sel_c[...], rounded).astype(BF16)
        hand_over(count)

    def out_copies(sections=range(3)):
        return [
            remote(
                outs.at[pl.ds(0, 4), pl.ds(32 * t, 32)], landed, o_send.at[t], o_recv.at[0], (t, d)
            )
            for t in sections
        ]

    @pl.when(sec == 3)
    def _():
        gather(0, chunks + 6)
        for copy in skip_copies():
            copy.wait_recv()
        take_over()
        for i in range(3):
            moved = dot(perm_c[...], cb[i]) * (keep_top, 1.0, keep_bottom)[i]
            moved = moved.astype(BF16)
            for half in range(2):
                for dx in range(3):
                    sh[dx, 2 * i + half] = dot(moved, doubled[half, dx]).astype(BF16)

        def keep_upper(q, made):
            rounded = (made * wide_scale).astype(BF16)
            packed = dot(sel_di[...], rounded).astype(BF16)
            ud[2 * q] = packed[:, 0:128]
            ud[2 * q + 1] = packed[:, 128:256]

        half_row = lambda q, off: q + (off + 1) // 2
        fine_conv(4, wide_pieces, 320, 0, 0, 2944, half_row, keep_upper)
        groups_u, groups_s = fine_groups[1], fine_groups[2]
        mean_u, dev_u = part_sums([ud[r].astype(F32) for r in range(2, 6)], groups_u, 2 * ROW_N)
        mean_s, dev_s = part_sums([skb[r].astype(F32) for r in range(2, 6)], groups_s, 2 * ROW_N)
        rows = exchanged(4, mean_u + mean_s, dev_u + dev_s, 2 * ROW_N)
        mean_u, rstd_u = columns(groups_u, rows)
        mean_s, rstd_s = columns(groups_s, rows)

        def joined_row(r, carry):
            kept = row_kept(r - 2)
            upper = activate(ud[r].astype(F32), mean_u, rstd_u) * kept
            put_shifted(r, 0, upper.astype(BF16))
            lower = activate(skb[r].astype(F32), mean_s, rstd_s) * kept
            put_shifted(r, 320, lower.astype(BF16))
            return carry

        lax.fori_loop(0, 8, joined_row, 0)

        def keep_hidden(q, made):
            rounded = (made * wide_scale).astype(BF16)
            packed = dot(sel_di[...], rounded).astype(BF16)
            hid[2 * q] = packed[:, 0:128]
            hid[2 * q + 1] = packed[:, 128:256]

        fine_conv(3, joined_pieces, 320, 64, 2816, 2944, follow, keep_hidden)
        groups = fine_groups[0]
        sums = part_sums([hid[r].astype(F32) for r in range(1, 5)], groups, ROW_N)
        mean, rstd = columns(groups, exchanged(5, *sums, ROW_N))
        activate_rows(hid, 6, -1, mean, rstd)
        for p in range(2):
            colj[p, 0:32, :] = jnp.zeros((32, 256), BF16)
            colj[p, 352:384, :] = jnp.zeros((32, 256), BF16)

        def keep_output(q, made):
            for p in range(2):
                for j in range(2):
                    px = slice(128 * j, 128 * j + 128)
                    colj[p, 32:192, px] = ud[2 * q + j + 2, 160 * p : 160 * p + 160, :]
                    colj[p, 192:352, px] = skb[2 * q + j + 2, 160 * p : 160 * p + 160, :]
            straight = weighted(7168, 384, colj)
            total = made * narrow_scale + straight * (1.0 / math.sqrt(640))
            rounded = total.astype(BF16)
            for j in range(2):
                flipped = lax.dot_general(
                    rounded[:, 128 * j : 128 * j + 128], exp_nat[...], (((0,), (0,)), ((), ())),
                    preferred_element_type=F32,
                )
                outs[2 * q + j] = flipped.astype(BF16)

        fine_conv(2, narrow_pieces, 160, 0, 5760, 1536, follow, keep_output)
        for copy in out_copies():
            copy.start()
        out_ref[...] = outs[:, 96:128, :]
        for copy in out_copies():
            copy.wait_send()

    @pl.when(sec < 3)
    def _():
        for copy in out_copies((0,)):
            copy.wait_recv()
        out_ref[...] = landed[...]

    gather_end()


def shards(features, section_packs):
    fields = jnp.swapaxes(features[0], 1, 2)
    packs = jnp.pad(jnp.swapaxes(section_packs[0], 0, 1), ((0, 6), (0, LANES - 11520)))
    tables = selections()
    dma = pltpu.SemaphoreType.DMA
    scratch = [
        pltpu.VMEM((4, 4, 48, LANES), BF16),
        pltpu.VMEM((4, 16, LANES), BF16),
        pltpu.VMEM((2, 2944, 256), BF16),
        pltpu.VMEM((5760, 256), BF16),
        pltpu.VMEM((2, 384, 256), BF16),
        pltpu.VMEM((3, 10, 640, 128), BF16),
        pltpu.VMEM((10, 320, 128), BF16),
        pltpu.VMEM((10, 320, 128), BF16),
        pltpu.VMEM((8, 320, 128), BF16),
        pltpu.VMEM((6, 320, 128), BF16),
        pltpu.VMEM((6, 320, 128), BF16),
        pltpu.VMEM((8, 320, 128), BF16),
        pltpu.VMEM((3, 640, 128), BF16),
        pltpu.VMEM((640, 128), BF16),
        pltpu.VMEM((640, 384), BF16),
        pltpu.VMEM((640, 256), BF16),
        pltpu.VMEM((640, 256), F32),
        pltpu.VMEM((768, 256), F32),
        pltpu.VMEM((8, 320, 128), BF16),
        pltpu.VMEM((4, 128, 320), BF16),
        pltpu.VMEM((4, 32, 320), BF16),
        pltpu.VMEM((6, 64, 2, 128), F32),
        pltpu.VMEM((2, 128), F32),
        pltpu.VMEM((2, 128), F32),
        dma((12, 8)), dma((12, 8)),
        dma((6,)), dma((6,)), dma((1,)), dma((1,)),
        dma((2,)), dma((2,)), dma((3,)), dma((3,)), dma((3,)), dma((3,)), dma((3,)), dma((1,)),
    ]
    vmem = pl.BlockSpec(memory_space=pltpu.VMEM)
    out = pl.pallas_call(
        kernel,
        out_shape=jax.ShapeDtypeStruct((4, 32, 320), BF16),
        in_specs=[vmem] * (2 + len(tables)),
        out_specs=vmem,
        scratch_shapes=scratch,
        compiler_params=pltpu.CompilerParams(
            collective_id=0, has_side_effects=True, vmem_limit_bytes=62 * 1024 * 1024
        ),
        cost_estimate=pl.CostEstimate(
            flops=12_000_000_000, bytes_accessed=30_000_000, transcendentals=2_000_000
        ),
    )(fields, packs, *tables)
    return out[None]


def solution(mesh):
    return jax.shard_map(
        shards,
        mesh=mesh,
        in_specs=(P(None, "space", None, None), P("section", None, "space")),
        out_specs=P(None, "space", "section", None),
        check_vma=False,
    )
```

```python
import math

import jax
import jax.numpy as jnp
import numpy as np
from jax import lax
from jax.experimental import pallas as pl
from jax.experimental.pallas import tpu as pltpu
from jax.sharding import PartitionSpec as P

F32 = jnp.float32
BF16 = jnp.bfloat16
MESH = pl.DeviceIdType.MESH
EPSILON = 1e-05
CHUNK = 1536
HALF = CHUNK // 2
QUARTER = CHUNK // 4
ROW_N = 512 * 10
LANES = 8 * CHUNK


def selections():
    rows = np.arange(768)
    chan_wide = np.where(rows % 48 < 40, 40 * (rows // 48) + rows % 48, -1)
    chan_fine = chan_wide[:384]
    rows = np.arange(48)
    packed = np.where(rows < 40, 16 * (rows // 10) + rows % 10, -1)
    split = lambda n: np.concatenate([np.arange(0, n, 2), np.arange(1, n, 2)])
    di, di_wide = split(320), split(640)
    nat, nat_wide = np.arange(320), np.arange(640)
    eq = lambda a, b: (a[:, None] == b[None, :])
    b = np.arange(128)
    shifts = np.stack([eq(b, b + dx) for dx in (-1, 1)])
    strided = np.stack(
        [
            np.stack([eq(b, 2 * (b % 64) + dx) & (b // 64 == i)[None, :] for dx in (-1, 0, 1)])
            for i in (0, 1)
        ]
    )
    doubled = np.stack(
        [
            np.stack(
                [
                    eq(b, 64 * half + (b + dx) // 2) & ((b + dx >= 0) & (b + dx < 128))[None, :]
                    for dx in (-1, 0, 1)
                ]
            )
            for half in (0, 1)
        ]
    )

    def taps():
        a, c = np.arange(6 * 64), np.arange(2 * 64)
        out = []
        for dy in (0, 1, 2):
            for dx in (-1, 0, 1):
                col = c % 64 + dx
                out.append(
                    eq(a, (c // 64 + 1 + dy) * 64 + col) & ((col >= 0) & (col < 64))[None, :]
                )
        return np.stack(out)

    group = np.arange(128)
    fine_groups = np.stack(
        [eq(di // 10, group), eq(di // 20, group), eq(16 + di // 20, group)]
    )
    wide_groups = eq(nat_wide // 20, group)
    bf = lambda m: np.asarray(m, np.float32).astype(jnp.bfloat16)
    return (
        bf(eq(packed, np.arange(64))),
        bf(eq(di, chan_fine)),
        bf(eq(nat, chan_fine)),
        bf(eq(chan_fine, di)),
        bf(eq(chan_fine, nat)),
        bf(eq(nat_wide, chan_wide)),
        bf(eq(chan_wide, nat_wide)),
        bf(eq(di, nat)),
        bf(eq(di_wide, nat_wide)),
        bf(shifts),
        bf(strided),
        bf(doubled),
        bf(taps()),
        np.asarray(fine_groups, np.float32),
        np.asarray(wide_groups, np.float32),
    )


def dot(a, b):
    return jnp.dot(a, b, preferred_element_type=F32)


def activate(values, mean, rstd):
    z = (values - mean) * rstd
    return z / (1.0 + jnp.exp(-z))


def kernel(
    x_ref, w_ref, pack, sel_di, sel_nat, exp_di, exp_nat, sel_c, exp_c, perm_x, perm_c, shifts, strided,
    doubled, taps, fine_groups, wide_groups, out_ref,
    W, raw, col, colw, colj, sh, xr, xd, hid, skd, skn, skb, cb, ht, tile, a3, ud, outs, landed,
    SA, HS, HR, gather_send, gather_recv, a_send, a_recv, b_send, b_recv,
    x_send, x_recv, h_send, h_recv, c_send, c_recv, k_send, k_recv, o_send, o_recv,
):
    sec = lax.axis_index("section")
    d = lax.axis_index("space")
    c = lax.rem(d, 2)
    z = lax.rem(lax.div(d, 2), 2)
    x = lax.rem(lax.div(d, 4), 4)
    y = lax.div(d, 16)
    space = lambda y, x, z, c: ((y * 4 + x) * 2 + z) * 2 + c
    xp, xm = lax.rem(x + 1, 4), lax.rem(x + 3, 4)
    yp, ym = lax.rem(y + 1, 4), lax.rem(y + 3, 4)
    below, above = lax.rem(d + 1, 64), lax.rem(d + 63, 64)
    after, before = lax.rem(sec + 1, 4), lax.rem(sec + 3, 4)
    is_top = d == 0
    is_bottom = d == 63
    keep_top = jnp.where(is_top, 0.0, 1.0)
    keep_bottom = jnp.where(is_bottom, 0.0, 1.0)

    barrier = pltpu.get_barrier_semaphore()
    peers = [(lax.rem(sec + 2, 4), d)]
    for other in (after, before):
        peers += [(other, d), (other, below), (other, above)]
    for peer in peers:
        pl.semaphore_signal(barrier, inc=1, device_id=peer, device_id_type=MESH)

    def greet(k, carry):
        peer = (sec, lax.rem(d + k, 64))
        pl.semaphore_signal(barrier, inc=1, device_id=peer, device_id_type=MESH)
        return carry

    lax.fori_loop(1, 64, greet, 0)

    raw[2 * z + c] = w_ref[...]
    pl.semaphore_wait(barrier, len(peers) + 63)

    def remote(src, dst, send, recv, peer):
        return pltpu.make_async_remote_copy(
            src_ref=src, dst_ref=dst, send_sem=send, recv_sem=recv, device_id=peer,
            device_id_type=MESH,
        )

    def combined(messages, count):
        means = messages[:, 0:1, :]
        mean = jnp.sum(means, axis=0) * (1.0 / 64)
        spread = jnp.sum(jnp.square(means - mean[None]), axis=0) * count
        squares = jnp.sum(messages[:, 1:2, :], axis=0) + spread
        return mean, lax.rsqrt(squares * (1.0 / (64 * count)) + EPSILON)

    def part_sums(blocks, groups, count, weight=None):
        total = blocks[0] if weight is None else blocks[0] * weight
        for block in blocks[1:]:
            total = total + block
        channel = jnp.sum(total, axis=1, keepdims=True)
        mean = jnp.sum(groups * channel, axis=0, keepdims=True) * (1.0 / count)
        own = jnp.sum(groups * mean, axis=1, keepdims=True)
        squares = None
        for block in blocks:
            off = jnp.square(block - own)
            off = off if weight is None else off * weight
            squares = off if squares is None else squares + off
        channel = jnp.sum(squares, axis=1, keepdims=True)
        return mean, jnp.sum(groups * channel, axis=0, keepdims=True)

    def start_exchange(e, mean, deviation):
        SA[e, 0] = jnp.concatenate([mean, deviation], axis=0)

        def one(k, carry):
            peer = (sec, lax.rem(d + k, 64))
            remote(SA.at[e, 0], SA.at[e, k], a_send.at[e], a_recv.at[e], peer).start()
            return carry

        lax.fori_loop(1, 64, one, 0)

    def finish_exchange(e, count):
        others = SA.at[e, pl.ds(1, 63)]
        remote(others, others, a_send.at[e], a_recv.at[e], (sec, below)).wait()
        return combined(SA[e], count)

    def exchanged(e, mean, deviation, count):
        start_exchange(e, mean, deviation)
        return finish_exchange(e, count)

    def columns(groups, rows):
        return [jnp.sum(groups * row, axis=1, keepdims=True) for row in rows]

    def across_copy():
        return remote(HS, HR, b_send.at[0], b_recv.at[0], (after, d))

    def rim_copies(kind, array, down, up):
        (down_from, down_to), (up_from, up_to) = down, up
        return [
            remote(array.at[pl.ds(down_from, size)], array.at[pl.ds(down_to, size)],
                   h_send.at[kind, 0], h_recv.at[kind, 0], (sec, below))
            for size in (2 if kind == 0 else 1,)
        ] + [
            remote(array.at[pl.ds(up_from, 1)], array.at[pl.ds(up_to, 1)],
                   h_send.at[kind, 1], h_recv.at[kind, 1], (sec, above))
        ]

    def start_all(copies):
        for copy in copies:
            copy.start()

    def wait_all(copies):
        for copy in copies:
            copy.wait()

    def tile_copies():
        return [
            remote(tile, cb.at[slot], c_send.at[slot], c_recv.at[slot], (after, peer))
            for slot, peer in ((1, d), (0, below), (2, above))
        ]

    def skip_copies():
        return [
            remote(skd.at[lax_rows(1, 4)], skb.at[lax_rows(2, 4)], k_send.at[0], k_recv.at[0], (before, d)),
            remote(skd.at[lax_rows(4, 1)], skb.at[lax_rows(1, 1)], k_send.at[1], k_recv.at[1], (before, below)),
            remote(skd.at[lax_rows(1, 1)], skb.at[lax_rows(6, 1)], k_send.at[2], k_recv.at[2], (before, above)),
        ]

    def lax_rows(start, size):
        return pl.ds(start, size)

    def hand_over(count):
        for copy in tile_copies():
            copy.start()

        @pl.when(sec < 2)
        def _():
            mean, deviation = part_sums([tile[...].astype(F32)], wide_groups[...], count)
            HS[...] = jnp.concatenate(exchanged(2, mean, deviation, count), axis=0)
            across_copy().start()
            across_copy().wait_send()

        for copy in tile_copies():
            copy.wait_send()

    def take_over():
        for copy in tile_copies():
            copy.wait_recv()

    chunks = jnp.where(sec == 0, 4, jnp.where(sec == 3, 5, 8))

    def gather_copies(core, stage, k):
        lanes = lambda off, size: pl.ds(pl.multiple_of(k * CHUNK + off, 128), size)
        mine, other = lanes(HALF * core, HALF), lanes(HALF * (1 - core), HALF)
        left, right = lanes(HALF * core, QUARTER), lanes(HALF * core + QUARTER, QUARTER)
        along_x = (space(y, xp, z, c), space(y, xm, z, c))
        along_y = (space(yp, x, z, c), space(ym, x, z, c))
        rows, every = pl.ds(0, 48), pl.ds(0, 4)
        array = W
        if stage == 0:
            array, whole = raw, pl.ds(0, 16)
            moves = [
                ((2 * z + c, whole, mine), space(y, x, 1 - z, c)),
                ((2 * z + c, whole, other), space(y, x, 1 - z, 1 - c)),
                ((2 * z + c, whole, other), space(y, x, z, 1 - c)),
            ]
        elif stage == 1:
            moves = [((y, x, rows, mine), peer) for peer in (along_y if core else along_x)]
        elif stage == 2 and core == 0:
            moves = [((y, xm, rows, left), along_x[0]), ((y, xp, rows, right), along_x[1])]
        elif stage == 2:
            moves = [((ym, x, rows, left), along_y[0]), ((yp, x, rows, right), along_y[1])]
        elif stage == 3 and core == 0:
            moves = [((y, every, rows, mine), peer) for peer in along_y]
        elif stage == 3:
            moves = [((every, x, rows, mine), peer) for peer in along_x]
        elif stage == 4 and core == 0:
            moves = [((ym, every, rows, left), along_y[0]), ((yp, every, rows, right), along_y[1])]
        elif stage == 4:
            moves = [((every, xm, rows, left), along_x[0]), ((every, xp, rows, right), along_x[1])]
        else:
            moves = [((every, every, rows, mine), space(y, x, z, 1 - c))]
        first_id = (0, 3, 5, 7, 9, 11)[stage]
        return [
            remote(
                array.at[where], array.at[where], gather_send.at[first_id + i, k],
                gather_recv.at[first_id + i, k], (sec, peer),
            )
            for i, (where, peer) in enumerate(moves)
        ]

    def gather_step(core, t):
        for stage in range(7):
            k = t - stage

            @pl.when((k >= 0) & (k < chunks))
            def _():
                if stage > 0:
                    for copy in gather_copies(core, stage - 1, k):
                        copy.wait_recv()
                if stage == 1:
                    lanes = pl.ds(pl.multiple_of(k * CHUNK + HALF * core, 128), HALF)
                    blocks = raw[:, :, lanes].reshape(64, HALF)
                    W[y, x, :, lanes] = dot(pack[...], blocks).astype(BF16)
                if stage < 6:
                    for copy in gather_copies(core, stage, k):
                        copy.start()

    def gather(first, last):
        def step(t, carry):
            for core in range(2):
                pl.when(c == core)(lambda core=core: gather_step(core, t))
            return carry

        lax.fori_loop(first, last, step, 0)

    def gather_end():
        def waits(core, k):
            for stage in range(6):
                for copy in gather_copies(core, stage, k):
                    copy.wait_send()

        def step(k, carry):
            for core in range(2):
                pl.when(c == core)(lambda core=core: waits(core, k))
            return carry

        lax.fori_loop(0, chunks, step, 0)

    def put_shifted(index, base, values):
        size = values.shape[0]
        sh[1, index, base : base + size, :] = values
        sh[0, index, base : base + size, :] = dot(values, shifts[0]).astype(BF16)
        sh[2, index, base : base + size, :] = dot(values, shifts[1]).astype(BF16)

    def fine_conv(pairs, pieces, per_tap, lead, lane_start, depth, source_row, use):
        taps = 9 * per_tap
        for p in range(2):
            if lead:
                col[p, 0:lead, :] = jnp.zeros((lead, 256), BF16)
            if lead + taps < depth:
                col[p, lead + taps : depth, :] = jnp.zeros((depth - lead - taps, 256), BF16)

        def pair(q, carry):
            for p in range(2):
                for dy in range(3):
                    for j in range(2):
                        row = source_row(q, j + dy)
                        for dx in range(3):
                            at = lead + (dy * 3 + dx) * per_tap
                            for to, start, size in pieces(p):
                                col[p, at + to : at + to + size, 128 * j : 128 * j + 128] = sh[
                                    dx, row, start : start + size, :
                                ]
            use(q, weighted(lane_start, depth, col))
            return carry

        lax.fori_loop(0, pairs, pair, 0)

    def weighted(lane_start, depth, source):
        total = None
        for p in range(2):
            kernels = W[2 * p : 2 * p + 2, :, :, lane_start : lane_start + depth]
            made = dot(kernels.reshape(384, depth), source[p, 0:depth, :])
            total = made if total is None else total + made
        return total

    narrow_pieces = lambda p: [(0, 160 * p, 160)]
    wide_pieces = lambda p: [(0, 320 * p, 320)]
    joined_pieces = lambda p: [(0, 160 * p, 160), (160, 320 + 160 * p, 160)]
    follow = lambda q, off: 2 * q + off
    narrow_scale = 1.0 / math.sqrt(9 * 320)
    wide_scale = 1.0 / math.sqrt(9 * 640)

    def row_kept(row):
        return jnp.where(row < 0, keep_top, jnp.where(row > 3, keep_bottom, 1.0))

    def activate_rows(source, start, stop, own_row, mean, rstd):
        def one(r, carry):
            values = activate(source[r].astype(F32), mean, rstd) * row_kept(r - own_row)
            put_shifted(r, 0, values.astype(BF16))
            return carry

        lax.fori_loop(start, stop, one, 0)

    @pl.when(sec == 0)
    def _():
        x_copies = [
            remote(x_ref.at[pl.ds(3, 1)], xr.at[pl.ds(2, 1)], x_send.at[0], x_recv.at[0], (0, below)),
            remote(x_ref.at[pl.ds(0, 1)], xr.at[pl.ds(7, 1)], x_send.at[1], x_recv.at[1], (0, above)),
        ]
        for copy in x_copies:
            copy.start()
        for r in range(4):
            xr[3 + r] = x_ref[r]
        hid[7] = jnp.zeros((320, 128), BF16)

        def permute(r, carry):
            xd[r] = dot(perm_x[...], xr[r]).astype(BF16)
            return carry

        lax.fori_loop(3, 7, permute, 0)
        groups = fine_groups[0]
        start_exchange(0, *part_sums([xd[r].astype(F32) for r in range(3, 7)], groups, ROW_N))
        gather(0, 7)
        for copy in x_copies:
            copy.wait()
        lax.fori_loop(2, 3, permute, 0)
        lax.fori_loop(7, 8, permute, 0)
        mean, rstd = columns(groups, finish_exchange(0, ROW_N))
        activate_rows(xd, 2, 8, 3, mean, rstd)

        def keep_hidden(q, made):
            rounded = (made * narrow_scale).astype(BF16)
            packed = dot(sel_di[...], rounded).astype(BF16)
            hid[2 * q + 2] = packed[:, 0:128]
            hid[2 * q + 3] = packed[:, 128:256]

        from_two = lambda q, off: 2 * q + off + 2
        fine_conv(2, narrow_pieces, 160, 0, 0, 1536, from_two, keep_hidden)
        rims = rim_copies(0, hid, (4, 0), (2, 6))
        start_all(rims)
        start_exchange(1, *part_sums([hid[r].astype(F32) for r in range(2, 6)], groups, ROW_N))
        gather(7, 8)
        mean, rstd = columns(groups, finish_exchange(1, ROW_N))
        wait_all(rims)
        activate_rows(hid, 0, 8, 2, mean, rstd)

        def keep_skip(q, made):
            for j in range(2):
                own = dot(exp_di[...], xd[2 * q + j + 2])
                rounded = (own + made[:, 128 * j : 128 * j + 128] * narrow_scale).astype(BF16)
                skd[2 * q + j] = dot(sel_di[...], rounded).astype(BF16)
                skn[2 * q + j] = dot(sel_nat[...], rounded).astype(BF16)

        fine_conv(3, narrow_pieces, 160, 32, 1408, 1536, follow, keep_skip)
        gather(8, 10)
        skn[0] = (skn[0].astype(F32) * keep_top).astype(BF16)
        col[0, 0:64, 0:128] = jnp.zeros((64, 128), BF16)
        for dy in range(3):
            for dx in range(3):
                at = 64 + (dy * 3 + dx) * 320
                made = dot(skn[dy], strided[0, dx]) + dot(skn[2 + dy], strided[1, dx])
                col[0, at : at + 320, 0:128] = made.astype(BF16)
        made = dot(W[:, :, :, 2816:5760].reshape(768, 2944), col[0, :, 0:128])
        rounded = (made * narrow_scale).astype(BF16)
        tile[...] = dot(sel_c[...], rounded).astype(BF16)
        hand_over(128 * 20)
        start_all(skip_copies())
        for copy in skip_copies():
            copy.wait_send()

    @pl.when((sec == 1) | (sec == 2))
    def _():
        gather(0, chunks + 6)
        take_over()
        count = 128 * 20
        groups = wide_groups[...]
        across_copy().wait_recv()
        mean, rstd = columns(groups, [HR[0:1, :], HR[1:2, :]])

        def activate_tiles(source):
            for i in range(3):
                values = activate(source[i].astype(F32), mean, rstd)
                values = values * (keep_top, 1.0, keep_bottom)[i]
                a3[:, 128 * i : 128 * i + 128] = values.astype(BF16)

        def coarse_conv(lane_start):
            for t in range(9):
                px = ((0, 256), (128, 256), (128, 384))[t // 3]
                moved = dot(a3[:, px[0] : px[1]], taps[t, px[0] : px[1], :])
                colw[640 * t : 640 * t + 640, :] = moved.astype(BF16)
            total = None
            for i in range(3):
                lanes = slice(lane_start + 1920 * i, lane_start + 1920 * i + 1920)
                source = colw[1920 * i : 1920 * i + 1920, :]
                made = dot(W[:, :, :, lanes].reshape(768, 1920), source)
                total = made if total is None else total + made
            return total * wide_scale

        activate_tiles(cb)
        rounded = coarse_conv(0).astype(BF16)
        hidden = dot(sel_c[...], rounded)
        ht[1] = hidden.astype(BF16)
        rims = rim_copies(3, ht, (1, 0), (1, 2))
        start_all(rims)
        sums = part_sums([hidden], groups, count)
        mean, rstd = columns(groups, exchanged(3, *sums, count))
        wait_all(rims)
        activate_tiles(ht)
        made = coarse_conv(5760)
        own = dot(exp_c[...], cb[1])
        rounded = (own + made).astype(BF16)
        tile[...] = dot(sel_c[...], rounded).astype(BF16)
        hand_over(count)

    def out_copies(sections=range(3)):
        return [
            remote(
                outs.at[pl.ds(0, 4), pl.ds(32 * t, 32)], landed, o_send.at[t], o_recv.at[0], (t, d)
            )
            for t in sections
        ]

    @pl.when(sec == 3)
    def _():
        gather(0, chunks + 6)
        for copy in skip_copies():
            copy.wait_recv()
        take_over()
        for i in range(3):
            moved = dot(perm_c[...], cb[i]) * (keep_top, 1.0, keep_bottom)[i]
            moved = moved.astype(BF16)
            for half in ((1,), (0, 1), (0,))[i]:
                for dx in range(3):
                    sh[dx, 2 * i + half] = dot(moved, doubled[half, dx]).astype(BF16)

        def keep_upper(q, made):
            rounded = (made * wide_scale).astype(BF16)
            packed = dot(sel_di[...], rounded).astype(BF16)
            ud[2 * q + 2] = packed[:, 0:128]
            ud[2 * q + 3] = packed[:, 128:256]

        half_row = lambda q, off: q + 1 + (off + 1) // 2
        fine_conv(2, wide_pieces, 320, 0, 0, 2944, half_row, keep_upper)
        rims = rim_copies(1, ud, (5, 1), (2, 6))
        start_all(rims)
        groups_u, groups_s = fine_groups[1], fine_groups[2]
        mean_u, dev_u = part_sums([ud[r].astype(F32) for r in range(2, 6)], groups_u, 2 * ROW_N)
        mean_s, dev_s = part_sums([skb[r].astype(F32) for r in range(2, 6)], groups_s, 2 * ROW_N)
        rows = exchanged(4, mean_u + mean_s, dev_u + dev_s, 2 * ROW_N)
        wait_all(rims)
        mean_u, rstd_u = columns(groups_u, rows)
        mean_s, rstd_s = columns(groups_s, rows)

        def joined_row(r, carry):
            kept = row_kept(r - 2)
            upper = activate(ud[r].astype(F32), mean_u, rstd_u) * kept
            put_shifted(r, 0, upper.astype(BF16))
            lower = activate(skb[r].astype(F32), mean_s, rstd_s) * kept
            put_shifted(r, 320, lower.astype(BF16))
            return carry

        lax.fori_loop(1, 7, joined_row, 0)

        def keep_hidden(q, made):
            rounded = (made * wide_scale).astype(BF16)
            packed = dot(sel_di[...], rounded).astype(BF16)
            hid[2 * q + 1] = packed[:, 0:128]
            hid[2 * q + 2] = packed[:, 128:256]

        from_one = lambda q, off: 2 * q + off + 1
        fine_conv(2, joined_pieces, 320, 64, 2816, 2944, from_one, keep_hidden)
        rims = rim_copies(2, hid, (4, 0), (1, 5))
        start_all(rims)
        groups = fine_groups[0]
        sums = part_sums([hid[r].astype(F32) for r in range(1, 5)], groups, ROW_N)
        mean, rstd = columns(groups, exchanged(5, *sums, ROW_N))
        wait_all(rims)
        activate_rows(hid, 0, 6, 1, mean, rstd)
        for p in range(2):
            colj[p, 0:32, :] = jnp.zeros((32, 256), BF16)
            colj[p, 352:384, :] = jnp.zeros((32, 256), BF16)

        def keep_output(q, made):
            for p in range(2):
                for j in range(2):
                    px = slice(128 * j, 128 * j + 128)
                    colj[p, 32:192, px] = ud[2 * q + j + 2, 160 * p : 160 * p + 160, :]
                    colj[p, 192:352, px] = skb[2 * q + j + 2, 160 * p : 160 * p + 160, :]
            straight = weighted(7168, 384, colj)
            total = made * narrow_scale + straight * (1.0 / math.sqrt(640))
            rounded = total.astype(BF16)
            for j in range(2):
                flipped = lax.dot_general(
                    rounded[:, 128 * j : 128 * j + 128], exp_nat[...], (((0,), (0,)), ((), ())),
                    preferred_element_type=F32,
                )
                outs[2 * q + j] = flipped.astype(BF16)

        fine_conv(2, narrow_pieces, 160, 0, 5760, 1536, follow, keep_output)
        for copy in out_copies():
            copy.start()
        out_ref[...] = outs[:, 96:128, :]
        for copy in out_copies():
            copy.wait_send()

    @pl.when(sec < 3)
    def _():
        for copy in out_copies((0,)):
            copy.wait_recv()
        out_ref[...] = landed[...]

    gather_end()


def shards(features, section_packs):
    fields = jnp.swapaxes(features[0], 1, 2)
    packs = jnp.pad(jnp.swapaxes(section_packs[0], 0, 1), ((0, 6), (0, LANES - 11520)))
    tables = selections()
    dma = pltpu.SemaphoreType.DMA
    scratch = [
        pltpu.VMEM((4, 4, 48, LANES), BF16),
        pltpu.VMEM((4, 16, LANES), BF16),
        pltpu.VMEM((2, 2944, 256), BF16),
        pltpu.VMEM((5760, 128), BF16),
        pltpu.VMEM((2, 384, 256), BF16),
        pltpu.VMEM((3, 10, 640, 128), BF16),
        pltpu.VMEM((10, 320, 128), BF16),
        pltpu.VMEM((10, 320, 128), BF16),
        pltpu.VMEM((8, 320, 128), BF16),
        pltpu.VMEM((6, 320, 128), BF16),
        pltpu.VMEM((6, 320, 128), BF16),
        pltpu.VMEM((8, 320, 128), BF16),
        pltpu.VMEM((3, 640, 128), BF16),
        pltpu.VMEM((3, 640, 128), BF16),
        pltpu.VMEM((640, 128), BF16),
        pltpu.VMEM((640, 384), BF16),
        pltpu.VMEM((8, 320, 128), BF16),
        pltpu.VMEM((4, 128, 320), BF16),
        pltpu.VMEM((4, 32, 320), BF16),
        pltpu.VMEM((6, 64, 2, 128), F32),
        pltpu.VMEM((2, 128), F32),
        pltpu.VMEM((2, 128), F32),
        dma((12, 8)), dma((12, 8)),
        dma((6,)), dma((6,)), dma((1,)), dma((1,)),
        dma((2,)), dma((2,)), dma((4, 2)), dma((4, 2)), dma((3,)), dma((3,)), dma((3,)), dma((3,)), dma((3,)), dma((1,)),
    ]
    vmem = pl.BlockSpec(memory_space=pltpu.VMEM)
    out = pl.pallas_call(
        kernel,
        out_shape=jax.ShapeDtypeStruct((4, 32, 320), BF16),
        in_specs=[vmem] * (2 + len(tables)),
        out_specs=vmem,
        scratch_shapes=scratch,
        compiler_params=pltpu.CompilerParams(
            collective_id=0, has_side_effects=True, vmem_limit_bytes=62 * 1024 * 1024
        ),
        cost_estimate=pl.CostEstimate(
            flops=12_000_000_000, bytes_accessed=30_000_000, transcendentals=2_000_000
        ),
    )(fields, packs, *tables)
    return out[None]


def solution(mesh):
    return jax.shard_map(
        shards,
        mesh=mesh,
        in_specs=(P(None, "space", None, None), P("section", None, "space")),
        out_specs=P(None, "space", "section", None),
        check_vma=False,
    )
```

```python
import math

import jax
import jax.numpy as jnp
import numpy as np
from jax import lax
from jax.experimental import pallas as pl
from jax.experimental.pallas import tpu as pltpu
from jax.sharding import PartitionSpec as P

F32 = jnp.float32
BF16 = jnp.bfloat16
MESH = pl.DeviceIdType.MESH
EPSILON = 1e-05
CHUNK = 1536
HALF = CHUNK // 2
QUARTER = CHUNK // 4
ROW_N = 512 * 10
LANES = 8 * CHUNK


def selections():
    rows = np.arange(768)
    chan_wide = np.where(rows % 48 < 40, 40 * (rows // 48) + rows % 48, -1)
    chan_fine = chan_wide[:384]
    rows = np.arange(48)
    packed = np.where(rows < 40, 16 * (rows // 10) + rows % 10, -1)
    split = lambda n: np.concatenate([np.arange(0, n, 2), np.arange(1, n, 2)])
    di, di_wide = split(320), split(640)
    nat, nat_wide = np.arange(320), np.arange(640)
    eq = lambda a, b: (a[:, None] == b[None, :])
    b = np.arange(128)
    shifts = np.stack([eq(b, b + dx) for dx in (-1, 1)])
    strided = np.stack(
        [
            np.stack([eq(b, 2 * (b % 64) + dx) & (b // 64 == i)[None, :] for dx in (-1, 0, 1)])
            for i in (0, 1)
        ]
    )
    doubled = np.stack(
        [
            np.stack(
                [
                    eq(b, 64 * half + (b + dx) // 2) & ((b + dx >= 0) & (b + dx < 128))[None, :]
                    for dx in (-1, 0, 1)
                ]
            )
            for half in (0, 1)
        ]
    )

    def taps():
        a, c = np.arange(6 * 64), np.arange(2 * 64)
        out = []
        for dy in (0, 1, 2):
            for dx in (-1, 0, 1):
                col = c % 64 + dx
                out.append(
                    eq(a, (c // 64 + 1 + dy) * 64 + col) & ((col >= 0) & (col < 64))[None, :]
                )
        return np.stack(out)

    group = np.arange(128)
    fine_groups = np.stack(
        [eq(di // 10, group), eq(di // 20, group), eq(16 + di // 20, group)]
    )
    wide_groups = eq(nat_wide // 20, group)
    bf = lambda m: np.asarray(m, np.float32).astype(jnp.bfloat16)
    return (
        bf(eq(packed, np.arange(64))),
        bf(eq(di, chan_fine)),
        bf(eq(nat, chan_fine)),
        bf(eq(chan_fine, di)),
        bf(eq(chan_fine, nat)),
        bf(eq(nat_wide, chan_wide)),
        bf(eq(chan_wide, nat_wide)),
        bf(eq(di, nat)),
        bf(eq(di_wide, nat_wide)),
        bf(shifts),
        bf(strided),
        bf(doubled),
        bf(taps()),
        np.asarray(fine_groups, np.float32),
        np.asarray(wide_groups, np.float32),
    )


def dot(a, b):
    return jnp.dot(a, b, preferred_element_type=F32)


def activate(values, mean, rstd):
    z = (values - mean) * rstd
    return z / (1.0 + jnp.exp(-z))


def kernel(
    x_ref, w_ref, pack, sel_di, sel_nat, exp_di, exp_nat, sel_c, exp_c, perm_x, perm_c, shifts, strided,
    doubled, taps, fine_groups, wide_groups, out_ref,
    W, raw, col, colw, colj, sh, xr, xd, hid, skd, skn, skb, cb, ht, tile, a3, ud, outs, landed,
    SA, SB, HS, gather_send, gather_recv, a_send, a_recv, b_send, b_recv,
    x_send, x_recv, h_send, h_recv, c_send, c_recv, k_send, k_recv, o_send, o_recv,
):
    sec = lax.axis_index("section")
    d = lax.axis_index("space")
    c = lax.rem(d, 2)
    z = lax.rem(lax.div(d, 2), 2)
    x = lax.rem(lax.div(d, 4), 4)
    y = lax.div(d, 16)
    space = lambda y, x, z, c: ((y * 4 + x) * 2 + z) * 2 + c
    xp, xm = lax.rem(x + 1, 4), lax.rem(x + 3, 4)
    yp, ym = lax.rem(y + 1, 4), lax.rem(y + 3, 4)
    below, above = lax.rem(d + 1, 64), lax.rem(d + 63, 64)
    hi, lo = lax.div(d, 8), lax.rem(d, 8)
    lo_peer = lambda k: hi * 8 + lax.rem(lo + k, 8)
    hi_peer = lambda k: lax.rem(hi + k, 8) * 8 + lo
    after, before = lax.rem(sec + 1, 4), lax.rem(sec + 3, 4)
    is_top = d == 0
    is_bottom = d == 63
    keep_top = jnp.where(is_top, 0.0, 1.0)
    keep_bottom = jnp.where(is_bottom, 0.0, 1.0)

    barrier = pltpu.get_barrier_semaphore()
    peers = [(sec, lo_peer(k)) for k in range(1, 8)] + [(sec, hi_peer(k)) for k in range(1, 8)]
    peers += [(sec, space(y, xp, z, c)), (sec, space(y, xm, z, c)), (sec, below), (sec, above)]
    for other in (after, before):
        peers += [(other, hi_peer(k)) for k in range(8)] + [(other, below), (other, above)]
    peers += [(lax.rem(sec + 2, 4), d)]
    for peer in peers:
        pl.semaphore_signal(barrier, inc=1, device_id=peer, device_id_type=MESH)

    raw[2 * z + c] = jnp.zeros((16, LANES), BF16)
    raw[2 * z + c, 0:10, 0:11520] = w_ref[...]
    pl.semaphore_wait(barrier, len(peers))

    def remote(src, dst, send, recv, peer):
        return pltpu.make_async_remote_copy(
            src_ref=src, dst_ref=dst, send_sem=send, recv_sem=recv, device_id=peer,
            device_id_type=MESH,
        )

    def combined(messages, count):
        means = messages[:, 0:1, :]
        mean = jnp.sum(means, axis=0) * 0.125
        spread = jnp.sum(jnp.square(means - mean[None]), axis=0) * count
        return jnp.concatenate([mean, jnp.sum(messages[:, 1:2, :], axis=0) + spread], axis=0)

    def part_sums(blocks, groups, count, weight=None):
        total = blocks[0] if weight is None else blocks[0] * weight
        for block in blocks[1:]:
            total = total + block
        channel = jnp.sum(total, axis=1, keepdims=True)
        mean = jnp.sum(groups * channel, axis=0, keepdims=True) * (1.0 / count)
        own = jnp.sum(groups * mean, axis=1, keepdims=True)
        squares = None
        for block in blocks:
            off = jnp.square(block - own)
            off = off if weight is None else off * weight
            squares = off if squares is None else squares + off
        channel = jnp.sum(squares, axis=1, keepdims=True)
        return mean, jnp.sum(groups * channel, axis=0, keepdims=True)

    def first_copies(e):
        return [
            remote(SA.at[e, 0], SA.at[e, k], a_send.at[e, k], a_recv.at[e, k], (sec, lo_peer(k)))
            for k in range(1, 8)
        ]

    def second_copies(e):
        return [
            remote(SB.at[e, 0], SB.at[e, k], b_send.at[e, k], b_recv.at[e, k], (sec, hi_peer(k)))
            for k in range(1, 8)
        ]

    def start_first(e, mean, deviation):
        SA[e, 0] = jnp.concatenate([mean, deviation], axis=0)
        start_all(first_copies(e))

    def finish_first(e, count):
        wait_all(first_copies(e))
        return combined(SA[e], count)

    def start_second(e, count):
        SB[e, 0] = finish_first(e, count)
        start_all(second_copies(e))

    def scale_rows(e, count):
        total = combined(SB[e], 8 * count)
        return total[0:1, :], lax.rsqrt(total[1:2, :] * (1.0 / (64 * count)) + EPSILON)

    def finish_second(e, count):
        wait_all(second_copies(e))
        return scale_rows(e, count)

    def exchanged(e, mean, deviation, count):
        start_first(e, mean, deviation)
        start_second(e, count)
        return finish_second(e, count)

    def columns(groups, rows):
        return [jnp.sum(groups * row, axis=1, keepdims=True) for row in rows]

    def across_copies():
        return [
            remote(HS, SB.at[2, k], b_send.at[2, k], b_recv.at[2, k], (after, hi_peer(k)))
            for k in range(8)
        ]

    def rim_copies(kind, array, down, up):
        (down_from, down_to), (up_from, up_to) = down, up
        return [
            remote(array.at[pl.ds(down_from, size)], array.at[pl.ds(down_to, size)],
                   h_send.at[kind, 0], h_recv.at[kind, 0], (sec, below))
            for size in (2 if kind == 0 else 1,)
        ] + [
            remote(array.at[pl.ds(up_from, 1)], array.at[pl.ds(up_to, 1)],
                   h_send.at[kind, 1], h_recv.at[kind, 1], (sec, above))
        ]

    def start_all(copies):
        for copy in copies:
            copy.start()

    def wait_all(copies):
        for copy in copies:
            copy.wait()

    def tile_copies():
        return [
            remote(tile, cb.at[slot], c_send.at[slot], c_recv.at[slot], (after, peer))
            for slot, peer in ((1, d), (0, below), (2, above))
        ]

    def skip_copies():
        return [
            remote(skd.at[lax_rows(1, 4)], skb.at[lax_rows(2, 4)], k_send.at[0], k_recv.at[0], (before, d)),
            remote(skd.at[lax_rows(4, 1)], skb.at[lax_rows(1, 1)], k_send.at[1], k_recv.at[1], (before, below)),
            remote(skd.at[lax_rows(1, 1)], skb.at[lax_rows(6, 1)], k_send.at[2], k_recv.at[2], (before, above)),
        ]

    def lax_rows(start, size):
        return pl.ds(start, size)

    def hand_over(count):
        for copy in tile_copies():
            copy.start()

        @pl.when(sec < 2)
        def _():
            mean, deviation = part_sums([tile[...].astype(F32)], wide_groups[...], count)
            start_first(2, mean, deviation)
            HS[...] = finish_first(2, count)
            start_all(across_copies())
            for copy in across_copies():
                copy.wait_send()

        for copy in tile_copies():
            copy.wait_send()

    def take_over():
        for copy in tile_copies():
            copy.wait_recv()

    chunks = jnp.where(sec == 0, 4, jnp.where(sec == 3, 5, 8))

    def gather_copies(core, stage, k):
        lanes = lambda off, size: pl.ds(pl.multiple_of(k * CHUNK + off, 128), size)
        mine, other = lanes(HALF * core, HALF), lanes(HALF * (1 - core), HALF)
        left, right = lanes(HALF * core, QUARTER), lanes(HALF * core + QUARTER, QUARTER)
        along_x = (space(y, xp, z, c), space(y, xm, z, c))
        along_y = (space(yp, x, z, c), space(ym, x, z, c))
        rows, every = pl.ds(0, 48), pl.ds(0, 4)
        array, sibling = W, space(y, x, z, 1 - c)

        def line(core, at, lanes=mine):
            return (every, at, rows, lanes) if core else (at, every, rows, lanes)

        if stage == 0:
            array, whole = raw, pl.ds(0, 16)
            moves = [
                ((2 * z + c, whole, mine), space(y, x, 1 - z, c)),
                ((2 * z + c, whole, other), space(y, x, 1 - z, 1 - c)),
                ((2 * z + c, whole, other), space(y, x, z, 1 - c)),
            ]
        elif stage == 1:
            moves = [((y, x, rows, mine), peer) for peer in (along_y if core else along_x)]
        elif stage == 2 and core == 0:
            moves = [((y, xm, rows, left), along_x[0]), ((y, xp, rows, right), along_x[1])]
        elif stage == 2:
            moves = [((ym, x, rows, left), along_y[0]), ((yp, x, rows, right), along_y[1])]
        elif stage == 3:
            own = line(core, x if core else y)
            moves = [(own, peer) for peer in (along_x if core else along_y)] + [(own, sibling)]
        elif stage == 4:
            up, down = (xm, xp) if core else (ym, yp)
            to_next, to_last = along_x if core else along_y
            moves = [(line(core, up, left), to_next), (line(core, down, right), to_last)]
            moves += [(line(core, up), sibling), (line(core, down), sibling)]
        else:
            moves = [(line(core, lax.rem((x if core else y) + 2, 4)), sibling)]
        first_id = (0, 3, 5, 7, 10, 14)[stage]
        return [
            remote(
                array.at[where], array.at[where], gather_send.at[first_id + i, k],
                gather_recv.at[first_id + i, k], (sec, peer),
            )
            for i, (where, peer) in enumerate(moves)
        ]

    def gather_step(core, t):
        for stage in range(7):
            turn = t - stage
            k = jnp.maximum(turn - 2, 0)

            @pl.when((turn == 0) | ((turn > 2) & (k < chunks)))
            def _():
                if stage > 0:
                    for copy in gather_copies(core, stage - 1, k):
                        copy.wait_recv()
                if stage == 1:
                    lanes = pl.ds(pl.multiple_of(k * CHUNK + HALF * core, 128), HALF)
                    blocks = raw[:, :, lanes].reshape(64, HALF)
                    W[y, x, :, lanes] = dot(pack[...], blocks).astype(BF16)
                if stage < 6:
                    for copy in gather_copies(core, stage, k):
                        copy.start()

    def gather(first, last):
        def step(t, carry):
            for core in range(2):
                pl.when(c == core)(lambda core=core: gather_step(core, t))
            return carry

        lax.fori_loop(first, last, step, 0)

    def gather_end():
        def waits(core, k):
            for stage in range(6):
                for copy in gather_copies(core, stage, k):
                    copy.wait_send()

        def step(k, carry):
            for core in range(2):
                pl.when(c == core)(lambda core=core: waits(core, k))
            return carry

        lax.fori_loop(0, chunks, step, 0)

    def put_shifted(index, base, values):
        size = values.shape[0]
        sh[1, index, base : base + size, :] = values
        sh[0, index, base : base + size, :] = dot(values, shifts[0]).astype(BF16)
        sh[2, index, base : base + size, :] = dot(values, shifts[1]).astype(BF16)

    def fine_conv(pairs, pieces, per_tap, lead, lane_start, depth, source_row, use):
        taps = 9 * per_tap
        for p in range(2):
            if lead:
                col[p, 0:lead, :] = jnp.zeros((lead, 256), BF16)
            if lead + taps < depth:
                col[p, lead + taps : depth, :] = jnp.zeros((depth - lead - taps, 256), BF16)

        def pair(q, carry):
            for p in range(2):
                for dy in range(3):
                    for j in range(2):
                        row = source_row(q, j + dy)
                        for dx in range(3):
                            at = lead + (dy * 3 + dx) * per_tap
                            for to, start, size in pieces(p):
                                col[p, at + to : at + to + size, 128 * j : 128 * j + 128] = sh[
                                    dx, row, start : start + size, :
                                ]
            use(q, weighted(lane_start, depth, col))
            return carry

        lax.fori_loop(0, pairs, pair, 0)

    def weighted(lane_start, depth, source):
        total = None
        for p in range(2):
            kernels = W[2 * p : 2 * p + 2, :, :, lane_start : lane_start + depth]
            made = dot(kernels.reshape(384, depth), source[p, 0:depth, :])
            total = made if total is None else total + made
        return total

    narrow_pieces = lambda p: [(0, 160 * p, 160)]
    wide_pieces = lambda p: [(0, 320 * p, 320)]
    joined_pieces = lambda p: [(0, 160 * p, 160), (160, 320 + 160 * p, 160)]
    follow = lambda q, off: 2 * q + off
    narrow_scale = 1.0 / math.sqrt(9 * 320)
    wide_scale = 1.0 / math.sqrt(9 * 640)

    def row_kept(row):
        return jnp.where(row < 0, keep_top, jnp.where(row > 3, keep_bottom, 1.0))

    def activate_rows(source, start, stop, own_row, mean, rstd):
        def one(r, carry):
            values = activate(source[r].astype(F32), mean, rstd) * row_kept(r - own_row)
            put_shifted(r, 0, values.astype(BF16))
            return carry

        lax.fori_loop(start, stop, one, 0)

    @pl.when(sec == 0)
    def _():
        x_copies = [
            remote(x_ref.at[pl.ds(3, 1)], xr.at[pl.ds(2, 1)], x_send.at[0], x_recv.at[0], (0, below)),
            remote(x_ref.at[pl.ds(0, 1)], xr.at[pl.ds(7, 1)], x_send.at[1], x_recv.at[1], (0, above)),
        ]
        gather(0, 1)
        for copy in x_copies:
            copy.start()
        for r in range(4):
            xr[3 + r] = x_ref[r]
        hid[7] = jnp.zeros((320, 128), BF16)

        def permute(r, carry):
            xd[r] = dot(perm_x[...], xr[r]).astype(BF16)
            return carry

        lax.fori_loop(3, 7, permute, 0)
        groups = fine_groups[0]
        start_first(0, *part_sums([xd[r].astype(F32) for r in range(3, 7)], groups, ROW_N))
        gather(1, 4)
        start_second(0, ROW_N)
        gather(4, 7)
        for copy in x_copies:
            copy.wait()
        lax.fori_loop(2, 3, permute, 0)
        lax.fori_loop(7, 8, permute, 0)
        mean, rstd = columns(groups, finish_second(0, ROW_N))
        activate_rows(xd, 2, 8, 3, mean, rstd)

        def keep_hidden(q, made):
            rounded = (made * narrow_scale).astype(BF16)
            packed = dot(sel_di[...], rounded).astype(BF16)
            hid[2 * q + 2] = packed[:, 0:128]
            hid[2 * q + 3] = packed[:, 128:256]

        from_two = lambda q, off: 2 * q + off + 2
        fine_conv(2, narrow_pieces, 160, 0, 0, 1536, from_two, keep_hidden)
        rims = rim_copies(0, hid, (4, 0), (2, 6))
        start_all(rims)
        start_first(1, *part_sums([hid[r].astype(F32) for r in range(2, 6)], groups, ROW_N))
        gather(7, 8)
        start_second(1, ROW_N)
        gather(8, 10)
        mean, rstd = columns(groups, finish_second(1, ROW_N))
        wait_all(rims)
        activate_rows(hid, 0, 8, 2, mean, rstd)

        def keep_skip(q, made):
            for j in range(2):
                own = dot(exp_di[...], xd[2 * q + j + 2])
                rounded = (own + made[:, 128 * j : 128 * j + 128] * narrow_scale).astype(BF16)
                skd[2 * q + j] = dot(sel_di[...], rounded).astype(BF16)
                skn[2 * q + j] = dot(sel_nat[...], rounded).astype(BF16)

        fine_conv(3, narrow_pieces, 160, 32, 1408, 1536, follow, keep_skip)
        gather(10, 12)
        skn[0] = (skn[0].astype(F32) * keep_top).astype(BF16)
        col[0, 0:64, 0:128] = jnp.zeros((64, 128), BF16)
        for dy in range(3):
            for dx in range(3):
                at = 64 + (dy * 3 + dx) * 320
                made = dot(skn[dy], strided[0, dx]) + dot(skn[2 + dy], strided[1, dx])
                col[0, at : at + 320, 0:128] = made.astype(BF16)
        made = dot(W[:, :, :, 2816:5760].reshape(768, 2944), col[0, :, 0:128])
        rounded = (made * narrow_scale).astype(BF16)
        tile[...] = dot(sel_c[...], rounded).astype(BF16)
        hand_over(128 * 20)
        start_all(skip_copies())
        for copy in skip_copies():
            copy.wait_send()

    @pl.when((sec == 1) | (sec == 2))
    def _():
        gather(0, jnp.where(sec == 1, 14, chunks + 8))
        take_over()
        count = 128 * 20
        groups = wide_groups[...]
        for copy in across_copies():
            copy.wait_recv()
        mean, rstd = columns(groups, scale_rows(2, count))

        def activate_tiles(source):
            for i in range(3):
                values = activate(source[i].astype(F32), mean, rstd)
                values = values * (keep_top, 1.0, keep_bottom)[i]
                a3[:, 128 * i : 128 * i + 128] = values.astype(BF16)

        def coarse_conv(lane_start):
            for t in range(9):
                px = ((0, 256), (128, 256), (128, 384))[t // 3]
                moved = dot(a3[:, px[0] : px[1]], taps[t, px[0] : px[1], :])
                colw[640 * t : 640 * t + 640, :] = moved.astype(BF16)
            total = None
            for i in range(3):
                lanes = slice(lane_start + 1920 * i, lane_start + 1920 * i + 1920)
                source = colw[1920 * i : 1920 * i + 1920, :]
                made = dot(W[:, :, :, lanes].reshape(768, 1920), source)
                total = made if total is None else total + made
            return total * wide_scale

        activate_tiles(cb)
        rounded = coarse_conv(0).astype(BF16)
        hidden = dot(sel_c[...], rounded)
        ht[1] = hidden.astype(BF16)
        rims = rim_copies(3, ht, (1, 0), (1, 2))
        start_all(rims)
        sums = part_sums([hidden], groups, count)
        start_first(3, *sums)
        start_second(3, count)

        @pl.when(sec == 1)
        def _():
            gather(14, 16)

        mean, rstd = columns(groups, finish_second(3, count))
        wait_all(rims)
        activate_tiles(ht)
        made = coarse_conv(5760)
        own = dot(exp_c[...], cb[1])
        rounded = (own + made).astype(BF16)
        tile[...] = dot(sel_c[...], rounded).astype(BF16)
        hand_over(count)

    def out_copies(sections=range(3)):
        return [
            remote(
                outs.at[pl.ds(0, 4), pl.ds(32 * t, 32)], landed, o_send.at[t], o_recv.at[0], (t, d)
            )
            for t in sections
        ]

    @pl.when(sec == 3)
    def _():
        gather(0, chunks + 8)
        for copy in skip_copies():
            copy.wait_recv()
        take_over()
        for i in range(3):
            moved = dot(perm_c[...], cb[i]) * (keep_top, 1.0, keep_bottom)[i]
            moved = moved.astype(BF16)
            for half in ((1,), (0, 1), (0,))[i]:
                for dx in range(3):
                    sh[dx, 2 * i + half] = dot(moved, doubled[half, dx]).astype(BF16)

        def keep_upper(q, made):
            rounded = (made * wide_scale).astype(BF16)
            packed = dot(sel_di[...], rounded).astype(BF16)
            ud[2 * q + 2] = packed[:, 0:128]
            ud[2 * q + 3] = packed[:, 128:256]

        half_row = lambda q, off: q + 1 + (off + 1) // 2
        fine_conv(2, wide_pieces, 320, 0, 0, 2944, half_row, keep_upper)
        rims = rim_copies(1, ud, (5, 1), (2, 6))
        start_all(rims)
        groups_u, groups_s = fine_groups[1], fine_groups[2]
        mean_u, dev_u = part_sums([ud[r].astype(F32) for r in range(2, 6)], groups_u, 2 * ROW_N)
        mean_s, dev_s = part_sums([skb[r].astype(F32) for r in range(2, 6)], groups_s, 2 * ROW_N)
        rows = exchanged(4, mean_u + mean_s, dev_u + dev_s, 2 * ROW_N)
        wait_all(rims)
        mean_u, rstd_u = columns(groups_u, rows)
        mean_s, rstd_s = columns(groups_s, rows)

        def joined_row(r, carry):
            kept = row_kept(r - 2)
            upper = activate(ud[r].astype(F32), mean_u, rstd_u) * kept
            put_shifted(r, 0, upper.astype(BF16))
            lower = activate(skb[r].astype(F32), mean_s, rstd_s) * kept
            put_shifted(r, 320, lower.astype(BF16))
            return carry

        lax.fori_loop(1, 7, joined_row, 0)

        def keep_hidden(q, made):
            rounded = (made * wide_scale).astype(BF16)
            packed = dot(sel_di[...], rounded).astype(BF16)
            hid[2 * q + 1] = packed[:, 0:128]
            hid[2 * q + 2] = packed[:, 128:256]

        from_one = lambda q, off: 2 * q + off + 1
        fine_conv(2, joined_pieces, 320, 64, 2816, 2944, from_one, keep_hidden)
        rims = rim_copies(2, hid, (4, 0), (1, 5))
        start_all(rims)
        groups = fine_groups[0]
        sums = part_sums([hid[r].astype(F32) for r in range(1, 5)], groups, ROW_N)
        mean, rstd = columns(groups, exchanged(5, *sums, ROW_N))
        wait_all(rims)
        activate_rows(hid, 0, 6, 1, mean, rstd)
        for p in range(2):
            colj[p, 0:32, :] = jnp.zeros((32, 256), BF16)
            colj[p, 352:384, :] = jnp.zeros((32, 256), BF16)

        def keep_output(q, made):
            for p in range(2):
                for j in range(2):
                    px = slice(128 * j, 128 * j + 128)
                    colj[p, 32:192, px] = ud[2 * q + j + 2, 160 * p : 160 * p + 160, :]
                    colj[p, 192:352, px] = skb[2 * q + j + 2, 160 * p : 160 * p + 160, :]
            straight = weighted(7168, 384, colj)
            total = made * narrow_scale + straight * (1.0 / math.sqrt(640))
            rounded = total.astype(BF16)
            for j in range(2):
                flipped = lax.dot_general(
                    rounded[:, 128 * j : 128 * j + 128], exp_nat[...], (((0,), (0,)), ((), ())),
                    preferred_element_type=F32,
                )
                outs[2 * q + j] = flipped.astype(BF16)

        fine_conv(2, narrow_pieces, 160, 0, 5760, 1536, follow, keep_output)
        for copy in out_copies():
            copy.start()
        out_ref[...] = outs[:, 96:128, :]
        for copy in out_copies():
            copy.wait_send()

    @pl.when(sec < 3)
    def _():
        for copy in out_copies((0,)):
            copy.wait_recv()
        out_ref[...] = landed[...]

    gather_end()


def shards(features, section_packs):
    fields = jnp.swapaxes(features[0], 1, 2)
    packs = jnp.swapaxes(section_packs[0], 0, 1)
    tables = selections()
    dma = pltpu.SemaphoreType.DMA
    scratch = [
        pltpu.VMEM((4, 4, 48, LANES), BF16),
        pltpu.VMEM((4, 16, LANES), BF16),
        pltpu.VMEM((2, 2944, 256), BF16),
        pltpu.VMEM((5760, 128), BF16),
        pltpu.VMEM((2, 384, 256), BF16),
        pltpu.VMEM((3, 10, 640, 128), BF16),
        pltpu.VMEM((10, 320, 128), BF16),
        pltpu.VMEM((10, 320, 128), BF16),
        pltpu.VMEM((8, 320, 128), BF16),
        pltpu.VMEM((6, 320, 128), BF16),
        pltpu.VMEM((6, 320, 128), BF16),
        pltpu.VMEM((8, 320, 128), BF16),
        pltpu.VMEM((3, 640, 128), BF16),
        pltpu.VMEM((3, 640, 128), BF16),
        pltpu.VMEM((640, 128), BF16),
        pltpu.VMEM((640, 384), BF16),
        pltpu.VMEM((8, 320, 128), BF16),
        pltpu.VMEM((4, 128, 320), BF16),
        pltpu.VMEM((4, 32, 320), BF16),
        pltpu.VMEM((6, 8, 2, 128), F32),
        pltpu.VMEM((6, 8, 2, 128), F32),
        pltpu.VMEM((2, 128), F32),
        dma((15, 8)), dma((15, 8)),
        dma((6, 8)), dma((6, 8)), dma((6, 8)), dma((6, 8)),
        dma((2,)), dma((2,)), dma((4, 2)), dma((4, 2)), dma((3,)), dma((3,)), dma((3,)), dma((3,)), dma((3,)), dma((1,)),
    ]
    vmem = pl.BlockSpec(memory_space=pltpu.VMEM)
    out = pl.pallas_call(
        kernel,
        out_shape=jax.ShapeDtypeStruct((4, 32, 320), BF16),
        in_specs=[vmem] * (2 + len(tables)),
        out_specs=vmem,
        scratch_shapes=scratch,
        compiler_params=pltpu.CompilerParams(
            collective_id=0, has_side_effects=True, vmem_limit_bytes=62 * 1024 * 1024
        ),
        cost_estimate=pl.CostEstimate(
            flops=12_000_000_000, bytes_accessed=30_000_000, transcendentals=2_000_000
        ),
    )(fields, packs, *tables)
    return out[None]


def solution(mesh):
    return jax.shard_map(
        shards,
        mesh=mesh,
        in_specs=(P(None, "space", None, None), P("section", None, "space")),
        out_specs=P(None, "space", "section", None),
        check_vma=False,
    )
```

```python
import functools
import math

import jax
import jax.numpy as jnp
import numpy as np
from jax import lax
from jax.experimental import pallas as pl
from jax.experimental.pallas import tpu as pltpu
from jax.sharding import PartitionSpec as P

F32 = jnp.float32
BF16 = jnp.bfloat16
MESH = pl.DeviceIdType.MESH
EPSILON = 1e-05
CHUNK = 1536
HALF = CHUNK // 2
QUARTER = CHUNK // 4
ROW_N = 512 * 10
LANES = 8 * CHUNK


def selections():
    rows = np.arange(768)
    chan_wide = np.where(rows % 48 < 40, 40 * (rows // 48) + rows % 48, -1)
    chan_fine = chan_wide[:384]
    rows = np.arange(48)
    packed = np.where(rows < 40, 16 * (rows // 10) + rows % 10, -1)
    split = lambda n: np.concatenate([np.arange(0, n, 2), np.arange(1, n, 2)])
    di, di_wide = split(320), split(640)
    nat, nat_wide = np.arange(320), np.arange(640)
    eq = lambda a, b: (a[:, None] == b[None, :])
    b = np.arange(128)
    shifts = np.stack([eq(b, b + dx) for dx in (-1, 1)])
    strided = np.stack(
        [
            np.stack([eq(b, 2 * (b % 64) + dx) & (b // 64 == i)[None, :] for dx in (-1, 0, 1)])
            for i in (0, 1)
        ]
    )
    doubled = np.stack(
        [
            np.stack(
                [
                    eq(b, 64 * half + (b + dx) // 2) & ((b + dx >= 0) & (b + dx < 128))[None, :]
                    for dx in (-1, 0, 1)
                ]
            )
            for half in (0, 1)
        ]
    )

    def taps():
        a, c = np.arange(6 * 64), np.arange(2 * 64)
        out = []
        for dy in (0, 1, 2):
            for dx in (-1, 0, 1):
                col = c % 64 + dx
                out.append(
                    eq(a, (c // 64 + 1 + dy) * 64 + col) & ((col >= 0) & (col < 64))[None, :]
                )
        return np.stack(out)

    group = np.arange(128)
    fine_groups = np.stack(
        [eq(di // 10, group), eq(di // 20, group), eq(16 + di // 20, group)]
    )
    wide_groups = eq(nat_wide // 20, group)
    bf = lambda m: np.asarray(m, np.float32).astype(jnp.bfloat16)
    return (
        bf(eq(packed, np.arange(64))),
        bf(eq(di, chan_fine)),
        bf(eq(nat, chan_fine)),
        bf(eq(chan_fine, di)),
        bf(eq(chan_fine, nat)),
        bf(eq(nat_wide, chan_wide)),
        bf(eq(chan_wide, nat_wide)),
        bf(eq(di, nat)),
        bf(eq(di_wide, nat_wide)),
        bf(shifts),
        bf(strided),
        bf(doubled),
        bf(taps()),
        np.asarray(fine_groups, np.float32),
        np.asarray(wide_groups, np.float32),
    )


def dot(a, b):
    return jnp.dot(a, b, preferred_element_type=F32)


def activate(values, mean, rstd):
    z = (values - mean) * rstd
    return z / (1.0 + jnp.exp(-z))


def kernel(
    loads,     x_ref, w_ref, pack, sel_di, sel_nat, exp_di, exp_nat, sel_c, exp_c, perm_x, perm_c, shifts, strided,
    doubled, taps, fine_groups, wide_groups, out_ref,
    W, raw, col, colw, colj, sh, xr, xd, hid, skd, skn, skb, cb, ht, tile, a3, ud, outs, landed,
    SA, HS, HR, gather_send, gather_recv, a_send, a_recv, b_send, b_recv,
    x_send, x_recv, h_send, h_recv, c_send, c_recv, k_send, k_recv, o_send, o_recv,
):
    sec = lax.axis_index("section")
    d = lax.axis_index("space")
    c = lax.rem(d, 2)
    z = lax.rem(lax.div(d, 2), 2)
    x = lax.rem(lax.div(d, 4), 4)
    y = lax.div(d, 16)
    space = lambda y, x, z, c: ((y * 4 + x) * 2 + z) * 2 + c
    xp, xm = lax.rem(x + 1, 4), lax.rem(x + 3, 4)
    yp, ym = lax.rem(y + 1, 4), lax.rem(y + 3, 4)
    below, above = lax.rem(d + 1, 64), lax.rem(d + 63, 64)
    after, before = lax.rem(sec + 1, 4), lax.rem(sec + 3, 4)
    is_top = d == 0
    is_bottom = d == 63
    keep_top = jnp.where(is_top, 0.0, 1.0)
    keep_bottom = jnp.where(is_bottom, 0.0, 1.0)

    for load in loads:
        load.start()

    barrier = pltpu.get_barrier_semaphore()
    peers = [(lax.rem(sec + 2, 4), d)]
    for other in (after, before):
        peers += [(other, d), (other, below), (other, above)]
    for peer in peers:
        pl.semaphore_signal(barrier, inc=1, device_id=peer, device_id_type=MESH)

    def greet(k, carry):
        peer = (sec, lax.rem(d + k, 64))
        pl.semaphore_signal(barrier, inc=1, device_id=peer, device_id_type=MESH)
        return carry

    lax.fori_loop(1, 64, greet, 0)

    raw[2 * z + c] = jnp.zeros((16, LANES), BF16)
    raw[2 * z + c, 0:10, 0:11520] = w_ref[...]
    for load in loads:
        load.wait()
    pl.semaphore_wait(barrier, len(peers) + 63)

    def remote(src, dst, send, recv, peer):
        return pltpu.make_async_remote_copy(
            src_ref=src, dst_ref=dst, send_sem=send, recv_sem=recv, device_id=peer,
            device_id_type=MESH,
        )

    def combined(messages, count):
        means = messages[:, 0:1, :]
        mean = jnp.sum(means, axis=0) * (1.0 / 64)
        spread = jnp.sum(jnp.square(means - mean[None]), axis=0) * count
        squares = jnp.sum(messages[:, 1:2, :], axis=0) + spread
        return mean, lax.rsqrt(squares * (1.0 / (64 * count)) + EPSILON)

    def part_sums(blocks, groups, count, weight=None):
        total = blocks[0] if weight is None else blocks[0] * weight
        for block in blocks[1:]:
            total = total + block
        channel = jnp.sum(total, axis=1, keepdims=True)
        mean = jnp.sum(groups * channel, axis=0, keepdims=True) * (1.0 / count)
        own = jnp.sum(groups * mean, axis=1, keepdims=True)
        squares = None
        for block in blocks:
            off = jnp.square(block - own)
            off = off if weight is None else off * weight
            squares = off if squares is None else squares + off
        channel = jnp.sum(squares, axis=1, keepdims=True)
        return mean, jnp.sum(groups * channel, axis=0, keepdims=True)

    def start_exchange(e, mean, deviation):
        SA[e, 0] = jnp.concatenate([mean, deviation], axis=0)

        def one(k, carry):
            peer = (sec, lax.rem(d + k, 64))
            remote(SA.at[e, 0], SA.at[e, k], a_send.at[e], a_recv.at[e], peer).start()
            return carry

        lax.fori_loop(1, 64, one, 0)

    def finish_exchange(e, count):
        others = SA.at[e, pl.ds(1, 63)]
        remote(others, others, a_send.at[e], a_recv.at[e], (sec, below)).wait()
        return combined(SA[e], count)

    def exchanged(e, mean, deviation, count):
        start_exchange(e, mean, deviation)
        return finish_exchange(e, count)

    def columns(groups, rows):
        return [jnp.sum(groups * row, axis=1, keepdims=True) for row in rows]

    def across_copy():
        return remote(HS, HR, b_send.at[0], b_recv.at[0], (after, d))

    def rim_copies(kind, array, down, up):
        (down_from, down_to), (up_from, up_to) = down, up
        return [
            remote(array.at[pl.ds(down_from, size)], array.at[pl.ds(down_to, size)],
                   h_send.at[kind, 0], h_recv.at[kind, 0], (sec, below))
            for size in (2 if kind == 0 else 1,)
        ] + [
            remote(array.at[pl.ds(up_from, 1)], array.at[pl.ds(up_to, 1)],
                   h_send.at[kind, 1], h_recv.at[kind, 1], (sec, above))
        ]

    def start_all(copies):
        for copy in copies:
            copy.start()

    def wait_all(copies):
        for copy in copies:
            copy.wait()

    def tile_copies():
        return [
            remote(tile, cb.at[slot], c_send.at[slot], c_recv.at[slot], (after, peer))
            for slot, peer in ((1, d), (0, below), (2, above))
        ]

    def skip_copies():
        return [
            remote(skd.at[lax_rows(1, 4)], skb.at[lax_rows(2, 4)], k_send.at[0], k_recv.at[0], (before, d)),
            remote(skd.at[lax_rows(4, 1)], skb.at[lax_rows(1, 1)], k_send.at[1], k_recv.at[1], (before, below)),
            remote(skd.at[lax_rows(1, 1)], skb.at[lax_rows(6, 1)], k_send.at[2], k_recv.at[2], (before, above)),
        ]

    def lax_rows(start, size):
        return pl.ds(start, size)

    def hand_over(count):
        for copy in tile_copies():
            copy.start()

        @pl.when(sec < 2)
        def _():
            mean, deviation = part_sums([tile[...].astype(F32)], wide_groups[...], count)
            HS[...] = jnp.concatenate(exchanged(2, mean, deviation, count), axis=0)
            across_copy().start()
            across_copy().wait_send()

        for copy in tile_copies():
            copy.wait_send()

    def take_over():
        for copy in tile_copies():
            copy.wait_recv()

    chunks = jnp.where(sec == 0, 4, jnp.where(sec == 3, 5, 8))

    def gather_copies(core, stage, k):
        lanes = lambda off, size: pl.ds(pl.multiple_of(k * CHUNK + off, 128), size)
        mine, other = lanes(HALF * core, HALF), lanes(HALF * (1 - core), HALF)
        left, right = lanes(HALF * core, QUARTER), lanes(HALF * core + QUARTER, QUARTER)
        along_x = (space(y, xp, z, c), space(y, xm, z, c))
        along_y = (space(yp, x, z, c), space(ym, x, z, c))
        rows, every = pl.ds(0, 48), pl.ds(0, 4)
        array = W
        if stage == 0:
            array, whole = raw, pl.ds(0, 16)
            moves = [
                ((2 * z + c, whole, mine), space(y, x, 1 - z, c)),
                ((2 * z + c, whole, other), space(y, x, 1 - z, 1 - c)),
                ((2 * z + c, whole, other), space(y, x, z, 1 - c)),
            ]
        elif stage == 1:
            moves = [((y, x, rows, mine), peer) for peer in (along_y if core else along_x)]
        elif stage == 2 and core == 0:
            moves = [((y, xm, rows, left), along_x[0]), ((y, xp, rows, right), along_x[1])]
        elif stage == 2:
            moves = [((ym, x, rows, left), along_y[0]), ((yp, x, rows, right), along_y[1])]
        elif stage == 3 and core == 0:
            moves = [((y, every, rows, mine), peer) for peer in along_y]
        elif stage == 3:
            moves = [((every, x, rows, mine), peer) for peer in along_x]
        elif stage == 4 and core == 0:
            moves = [((ym, every, rows, left), along_y[0]), ((yp, every, rows, right), along_y[1])]
        elif stage == 4:
            moves = [((every, xm, rows, left), along_x[0]), ((every, xp, rows, right), along_x[1])]
        else:
            moves = [((every, every, rows, mine), space(y, x, z, 1 - c))]
        first_id = (0, 3, 5, 7, 9, 11)[stage]
        return [
            remote(
                array.at[where], array.at[where], gather_send.at[first_id + i, k],
                gather_recv.at[first_id + i, k], (sec, peer),
            )
            for i, (where, peer) in enumerate(moves)
        ]

    def gather_step(core, t):
        for stage in range(7):
            k = t - stage

            @pl.when((k >= 0) & (k < chunks))
            def _():
                if stage > 0:
                    for copy in gather_copies(core, stage - 1, k):
                        copy.wait_recv()
                if stage == 1:
                    lanes = pl.ds(pl.multiple_of(k * CHUNK + HALF * core, 128), HALF)
                    blocks = raw[:, :, lanes].reshape(64, HALF)
                    W[y, x, :, lanes] = dot(pack[...], blocks).astype(BF16)
                if stage < 6:
                    for copy in gather_copies(core, stage, k):
                        copy.start()

    def gather(first, last):
        def step(t, carry):
            for core in range(2):
                pl.when(c == core)(lambda core=core: gather_step(core, t))
            return carry

        lax.fori_loop(first, last, step, 0)

    def gather_end():
        def waits(core, k):
            for stage in range(6):
                for copy in gather_copies(core, stage, k):
                    copy.wait_send()

        def step(k, carry):
            for core in range(2):
                pl.when(c == core)(lambda core=core: waits(core, k))
            return carry

        lax.fori_loop(0, chunks, step, 0)

    def put_shifted(index, base, values):
        size = values.shape[0]
        sh[1, index, base : base + size, :] = values
        sh[0, index, base : base + size, :] = dot(values, shifts[0]).astype(BF16)
        sh[2, index, base : base + size, :] = dot(values, shifts[1]).astype(BF16)

    def fine_conv(pairs, pieces, per_tap, lead, lane_start, depth, source_row, use):
        taps = 9 * per_tap
        for p in range(2):
            if lead:
                col[p, 0:lead, :] = jnp.zeros((lead, 256), BF16)
            if lead + taps < depth:
                col[p, lead + taps : depth, :] = jnp.zeros((depth - lead - taps, 256), BF16)

        def pair(q, carry):
            for p in range(2):
                for dy in range(3):
                    for j in range(2):
                        row = source_row(q, j + dy)
                        for dx in range(3):
                            at = lead + (dy * 3 + dx) * per_tap
                            for to, start, size in pieces(p):
                                col[p, at + to : at + to + size, 128 * j : 128 * j + 128] = sh[
                                    dx, row, start : start + size, :
                                ]
            use(q, weighted(lane_start, depth, col))
            return carry

        lax.fori_loop(0, pairs, pair, 0)

    def weighted(lane_start, depth, source):
        total = None
        for p in range(2):
            kernels = W[2 * p : 2 * p + 2, :, :, lane_start : lane_start + depth]
            made = dot(kernels.reshape(384, depth), source[p, 0:depth, :])
            total = made if total is None else total + made
        return total

    narrow_pieces = lambda p: [(0, 160 * p, 160)]
    wide_pieces = lambda p: [(0, 320 * p, 320)]
    joined_pieces = lambda p: [(0, 160 * p, 160), (160, 320 + 160 * p, 160)]
    follow = lambda q, off: 2 * q + off
    narrow_scale = 1.0 / math.sqrt(9 * 320)
    wide_scale = 1.0 / math.sqrt(9 * 640)

    def row_kept(row):
        return jnp.where(row < 0, keep_top, jnp.where(row > 3, keep_bottom, 1.0))

    def activate_rows(source, start, stop, own_row, mean, rstd):
        def one(r, carry):
            values = activate(source[r].astype(F32), mean, rstd) * row_kept(r - own_row)
            put_shifted(r, 0, values.astype(BF16))
            return carry

        lax.fori_loop(start, stop, one, 0)

    @pl.when(sec == 0)
    def _():
        x_copies = [
            remote(x_ref.at[pl.ds(3, 1)], xr.at[pl.ds(2, 1)], x_send.at[0], x_recv.at[0], (0, below)),
            remote(x_ref.at[pl.ds(0, 1)], xr.at[pl.ds(7, 1)], x_send.at[1], x_recv.at[1], (0, above)),
        ]
        for copy in x_copies:
            copy.start()
        for r in range(4):
            xr[3 + r] = x_ref[r]
        hid[7] = jnp.zeros((320, 128), BF16)

        def permute(r, carry):
            xd[r] = dot(perm_x[...], xr[r]).astype(BF16)
            return carry

        lax.fori_loop(3, 7, permute, 0)
        groups = fine_groups[0]
        start_exchange(0, *part_sums([xd[r].astype(F32) for r in range(3, 7)], groups, ROW_N))
        gather(0, 7)
        for copy in x_copies:
            copy.wait()
        lax.fori_loop(2, 3, permute, 0)
        lax.fori_loop(7, 8, permute, 0)
        mean, rstd = columns(groups, finish_exchange(0, ROW_N))
        activate_rows(xd, 2, 8, 3, mean, rstd)

        def keep_hidden(q, made):
            rounded = (made * narrow_scale).astype(BF16)
            packed = dot(sel_di[...], rounded).astype(BF16)
            hid[2 * q + 2] = packed[:, 0:128]
            hid[2 * q + 3] = packed[:, 128:256]

        from_two = lambda q, off: 2 * q + off + 2
        fine_conv(2, narrow_pieces, 160, 0, 0, 1536, from_two, keep_hidden)
        rims = rim_copies(0, hid, (4, 0), (2, 6))
        start_all(rims)
        start_exchange(1, *part_sums([hid[r].astype(F32) for r in range(2, 6)], groups, ROW_N))
        gather(7, 8)
        mean, rstd = columns(groups, finish_exchange(1, ROW_N))
        wait_all(rims)
        activate_rows(hid, 0, 8, 2, mean, rstd)

        def keep_skip(q, made):
            for j in range(2):
                own = dot(exp_di[...], xd[2 * q + j + 2])
                rounded = (own + made[:, 128 * j : 128 * j + 128] * narrow_scale).astype(BF16)
                skd[2 * q + j] = dot(sel_di[...], rounded).astype(BF16)
                skn[2 * q + j] = dot(sel_nat[...], rounded).astype(BF16)

        fine_conv(3, narrow_pieces, 160, 32, 1408, 1536, follow, keep_skip)
        gather(8, 10)
        skn[0] = (skn[0].astype(F32) * keep_top).astype(BF16)
        col[0, 0:64, 0:128] = jnp.zeros((64, 128), BF16)
        for dy in range(3):
            for dx in range(3):
                at = 64 + (dy * 3 + dx) * 320
                made = dot(skn[dy], strided[0, dx]) + dot(skn[2 + dy], strided[1, dx])
                col[0, at : at + 320, 0:128] = made.astype(BF16)
        made = dot(W[:, :, :, 2816:5760].reshape(768, 2944), col[0, :, 0:128])
        rounded = (made * narrow_scale).astype(BF16)
        tile[...] = dot(sel_c[...], rounded).astype(BF16)
        hand_over(128 * 20)
        start_all(skip_copies())
        for copy in skip_copies():
            copy.wait_send()

    @pl.when((sec == 1) | (sec == 2))
    def _():
        gather(0, chunks + 6)
        take_over()
        count = 128 * 20
        groups = wide_groups[...]
        across_copy().wait_recv()
        mean, rstd = columns(groups, [HR[0:1, :], HR[1:2, :]])

        def activate_tiles(source):
            for i in range(3):
                values = activate(source[i].astype(F32), mean, rstd)
                values = values * (keep_top, 1.0, keep_bottom)[i]
                a3[:, 128 * i : 128 * i + 128] = values.astype(BF16)

        def coarse_conv(lane_start):
            for t in range(9):
                px = ((0, 256), (128, 256), (128, 384))[t // 3]
                moved = dot(a3[:, px[0] : px[1]], taps[t, px[0] : px[1], :])
                colw[640 * t : 640 * t + 640, :] = moved.astype(BF16)
            total = None
            for i in range(3):
                lanes = slice(lane_start + 1920 * i, lane_start + 1920 * i + 1920)
                source = colw[1920 * i : 1920 * i + 1920, :]
                made = dot(W[:, :, :, lanes].reshape(768, 1920), source)
                total = made if total is None else total + made
            return total * wide_scale

        activate_tiles(cb)
        rounded = coarse_conv(0).astype(BF16)
        hidden = dot(sel_c[...], rounded)
        ht[1] = hidden.astype(BF16)
        rims = rim_copies(3, ht, (1, 0), (1, 2))
        start_all(rims)
        sums = part_sums([hidden], groups, count)
        mean, rstd = columns(groups, exchanged(3, *sums, count))
        wait_all(rims)
        activate_tiles(ht)
        made = coarse_conv(5760)
        own = dot(exp_c[...], cb[1])
        rounded = (own + made).astype(BF16)
        tile[...] = dot(sel_c[...], rounded).astype(BF16)
        hand_over(count)

    def out_copies(sections=range(3)):
        return [
            remote(
                outs.at[pl.ds(0, 4), pl.ds(32 * t, 32)], landed, o_send.at[t], o_recv.at[0], (t, d)
            )
            for t in sections
        ]

    @pl.when(sec == 3)
    def _():
        gather(0, chunks + 6)
        for copy in skip_copies():
            copy.wait_recv()
        take_over()
        for i in range(3):
            moved = dot(perm_c[...], cb[i]) * (keep_top, 1.0, keep_bottom)[i]
            moved = moved.astype(BF16)
            for half in ((1,), (0, 1), (0,))[i]:
                for dx in range(3):
                    sh[dx, 2 * i + half] = dot(moved, doubled[half, dx]).astype(BF16)

        def keep_upper(q, made):
            rounded = (made * wide_scale).astype(BF16)
            packed = dot(sel_di[...], rounded).astype(BF16)
            ud[2 * q + 2] = packed[:, 0:128]
            ud[2 * q + 3] = packed[:, 128:256]

        half_row = lambda q, off: q + 1 + (off + 1) // 2
        fine_conv(2, wide_pieces, 320, 0, 0, 2944, half_row, keep_upper)
        rims = rim_copies(1, ud, (5, 1), (2, 6))
        start_all(rims)
        groups_u, groups_s = fine_groups[1], fine_groups[2]
        mean_u, dev_u = part_sums([ud[r].astype(F32) for r in range(2, 6)], groups_u, 2 * ROW_N)
        mean_s, dev_s = part_sums([skb[r].astype(F32) for r in range(2, 6)], groups_s, 2 * ROW_N)
        rows = exchanged(4, mean_u + mean_s, dev_u + dev_s, 2 * ROW_N)
        wait_all(rims)
        mean_u, rstd_u = columns(groups_u, rows)
        mean_s, rstd_s = columns(groups_s, rows)

        def joined_row(r, carry):
            kept = row_kept(r - 2)
            upper = activate(ud[r].astype(F32), mean_u, rstd_u) * kept
            put_shifted(r, 0, upper.astype(BF16))
            lower = activate(skb[r].astype(F32), mean_s, rstd_s) * kept
            put_shifted(r, 320, lower.astype(BF16))
            return carry

        lax.fori_loop(1, 7, joined_row, 0)

        def keep_hidden(q, made):
            rounded = (made * wide_scale).astype(BF16)
            packed = dot(sel_di[...], rounded).astype(BF16)
            hid[2 * q + 1] = packed[:, 0:128]
            hid[2 * q + 2] = packed[:, 128:256]

        from_one = lambda q, off: 2 * q + off + 1
        fine_conv(2, joined_pieces, 320, 64, 2816, 2944, from_one, keep_hidden)
        rims = rim_copies(2, hid, (4, 0), (1, 5))
        start_all(rims)
        groups = fine_groups[0]
        sums = part_sums([hid[r].astype(F32) for r in range(1, 5)], groups, ROW_N)
        mean, rstd = columns(groups, exchanged(5, *sums, ROW_N))
        wait_all(rims)
        activate_rows(hid, 0, 6, 1, mean, rstd)
        for p in range(2):
            colj[p, 0:32, :] = jnp.zeros((32, 256), BF16)
            colj[p, 352:384, :] = jnp.zeros((32, 256), BF16)

        def keep_output(q, made):
            for p in range(2):
                for j in range(2):
                    px = slice(128 * j, 128 * j + 128)
                    colj[p, 32:192, px] = ud[2 * q + j + 2, 160 * p : 160 * p + 160, :]
                    colj[p, 192:352, px] = skb[2 * q + j + 2, 160 * p : 160 * p + 160, :]
            straight = weighted(7168, 384, colj)
            total = made * narrow_scale + straight * (1.0 / math.sqrt(640))
            rounded = total.astype(BF16)
            for j in range(2):
                flipped = lax.dot_general(
                    rounded[:, 128 * j : 128 * j + 128], exp_nat[...], (((0,), (0,)), ((), ())),
                    preferred_element_type=F32,
                )
                outs[2 * q + j] = flipped.astype(BF16)

        fine_conv(2, narrow_pieces, 160, 0, 5760, 1536, follow, keep_output)
        for copy in out_copies():
            copy.start()
        out_ref[...] = outs[:, 96:128, :]
        for copy in out_copies():
            copy.wait_send()

    @pl.when(sec < 3)
    def _():
        for copy in out_copies((0,)):
            copy.wait_recv()
        out_ref[...] = landed[...]

    gather_end()


def entry(count, x_ref, w_ref, *refs):
    sources, out_ref, copies = refs[:count], refs[count], refs[count + 1 : 2 * count + 1]
    sems, others = refs[2 * count + 1], refs[2 * count + 2 :]
    loads = [
        pltpu.make_async_copy(source, copy, sems.at[i])
        for i, (source, copy) in enumerate(zip(sources, copies))
    ]
    kernel(loads, x_ref, w_ref, *copies, out_ref, *others)


def shards(features, section_packs):
    fields = jnp.swapaxes(features[0], 1, 2)
    packs = jnp.swapaxes(section_packs[0], 0, 1)
    tables = selections()
    dma = pltpu.SemaphoreType.DMA
    scratch = [pltpu.VMEM(table.shape, table.dtype) for table in tables]
    scratch += [
        dma((len(tables),)),
        pltpu.VMEM((4, 4, 48, LANES), BF16),
        pltpu.VMEM((4, 16, LANES), BF16),
        pltpu.VMEM((2, 2944, 256), BF16),
        pltpu.VMEM((5760, 128), BF16),
        pltpu.VMEM((2, 384, 256), BF16),
        pltpu.VMEM((3, 10, 640, 128), BF16),
        pltpu.VMEM((10, 320, 128), BF16),
        pltpu.VMEM((10, 320, 128), BF16),
        pltpu.VMEM((8, 320, 128), BF16),
        pltpu.VMEM((6, 320, 128), BF16),
        pltpu.VMEM((6, 320, 128), BF16),
        pltpu.VMEM((8, 320, 128), BF16),
        pltpu.VMEM((3, 640, 128), BF16),
        pltpu.VMEM((3, 640, 128), BF16),
        pltpu.VMEM((640, 128), BF16),
        pltpu.VMEM((640, 384), BF16),
        pltpu.VMEM((8, 320, 128), BF16),
        pltpu.VMEM((4, 128, 320), BF16),
        pltpu.VMEM((4, 32, 320), BF16),
        pltpu.VMEM((6, 64, 2, 128), F32),
        pltpu.VMEM((2, 128), F32),
        pltpu.VMEM((2, 128), F32),
        dma((12, 8)), dma((12, 8)),
        dma((6,)), dma((6,)), dma((1,)), dma((1,)),
        dma((2,)), dma((2,)), dma((4, 2)), dma((4, 2)), dma((3,)), dma((3,)), dma((3,)), dma((3,)), dma((3,)), dma((1,)),
    ]
    vmem = pl.BlockSpec(memory_space=pltpu.VMEM)
    out = pl.pallas_call(
        functools.partial(entry, len(tables)),
        out_shape=jax.ShapeDtypeStruct((4, 32, 320), BF16),
        in_specs=[vmem] * 2 + [pl.BlockSpec(memory_space=pl.ANY)] * len(tables),
        out_specs=vmem,
        scratch_shapes=scratch,
        compiler_params=pltpu.CompilerParams(
            collective_id=0, has_side_effects=True, vmem_limit_bytes=62 * 1024 * 1024
        ),
        cost_estimate=pl.CostEstimate(
            flops=12_000_000_000, bytes_accessed=30_000_000, transcendentals=2_000_000
        ),
    )(fields, packs, *tables)
    return out[None]


def solution(mesh):
    return jax.shard_map(
        shards,
        mesh=mesh,
        in_specs=(P(None, "space", None, None), P("section", None, "space")),
        out_specs=P(None, "space", "section", None),
        check_vma=False,
    )
```

```python
import functools
import math

import jax
import jax.numpy as jnp
import numpy as np
from jax import lax
from jax.experimental import pallas as pl
from jax.experimental.pallas import tpu as pltpu
from jax.sharding import PartitionSpec as P

F32 = jnp.float32
BF16 = jnp.bfloat16
MESH = pl.DeviceIdType.MESH
EPSILON = 1e-05
CHUNK = 1536
HALF = CHUNK // 2
QUARTER = CHUNK // 4
ROW_N = 512 * 10
LANES = 8 * CHUNK


def selections():
    rows = np.arange(768)
    chan_wide = np.where(rows % 48 < 40, 40 * (rows // 48) + rows % 48, -1)
    chan_fine = chan_wide[:384]
    rows = np.arange(48)
    packed = np.where(rows < 40, 16 * (rows // 10) + rows % 10, -1)
    split = lambda n: np.concatenate([np.arange(0, n, 2), np.arange(1, n, 2)])
    di, di_wide = split(320), split(640)
    nat, nat_wide = np.arange(320), np.arange(640)
    eq = lambda a, b: (a[:, None] == b[None, :])
    b = np.arange(128)
    shifts = np.stack([eq(b, b + dx) for dx in (-1, 1)])
    strided = np.stack(
        [
            np.stack([eq(b, 2 * (b % 64) + dx) & (b // 64 == i)[None, :] for dx in (-1, 0, 1)])
            for i in (0, 1)
        ]
    )
    doubled = np.stack(
        [
            np.stack(
                [
                    eq(b, 64 * half + (b + dx) // 2) & ((b + dx >= 0) & (b + dx < 128))[None, :]
                    for dx in (-1, 0, 1)
                ]
            )
            for half in (0, 1)
        ]
    )

    def taps():
        a, c = np.arange(6 * 64), np.arange(2 * 64)
        out = []
        for dy in (0, 1, 2):
            for dx in (-1, 0, 1):
                col = c % 64 + dx
                out.append(
                    eq(a, (c // 64 + 1 + dy) * 64 + col) & ((col >= 0) & (col < 64))[None, :]
                )
        return np.stack(out)

    group = np.arange(128)
    fine_groups = np.stack(
        [eq(di // 10, group), eq(di // 20, group), eq(16 + di // 20, group)]
    )
    wide_groups = eq(nat_wide // 20, group)
    bf = lambda m: np.asarray(m, np.float32).astype(jnp.bfloat16)
    return (
        bf(eq(packed, np.arange(64))),
        bf(eq(di, chan_fine)),
        bf(eq(nat, chan_fine)),
        bf(eq(chan_fine, di)),
        bf(eq(chan_fine, nat)),
        bf(eq(nat_wide, chan_wide)),
        bf(eq(chan_wide, nat_wide)),
        bf(eq(di, nat)),
        bf(eq(di_wide, nat_wide)),
        bf(shifts),
        bf(strided),
        bf(doubled),
        bf(taps()),
        np.asarray(fine_groups, np.float32),
        np.asarray(wide_groups, np.float32),
    )


def dot(a, b):
    return jnp.dot(a, b, preferred_element_type=F32)


def activate(values, mean, rstd):
    z = (values - mean) * rstd
    return z / (1.0 + jnp.exp(-z))


def kernel(
    loads,     x_ref, w_ref, pack, sel_di, sel_nat, exp_di, exp_nat, sel_c, exp_c, perm_x, perm_c, shifts, strided,
    doubled, taps, fine_groups, wide_groups, out_ref,
    W, raw, col, colw, colj, sh, xr, xd, hid, skd, skn, skb, cb, ht, tile, a3, ud, outs, landed,
    SA, HS, HR, gather_send, gather_recv, a_send, a_recv, b_send, b_recv,
    x_send, x_recv, h_send, h_recv, c_send, c_recv, k_send, k_recv, o_send, o_recv,
):
    sec = lax.axis_index("section")
    d = lax.axis_index("space")
    c = lax.rem(d, 2)
    z = lax.rem(lax.div(d, 2), 2)
    x = lax.rem(lax.div(d, 4), 4)
    y = lax.div(d, 16)
    space = lambda y, x, z, c: ((y * 4 + x) * 2 + z) * 2 + c
    xp, xm = lax.rem(x + 1, 4), lax.rem(x + 3, 4)
    yp, ym = lax.rem(y + 1, 4), lax.rem(y + 3, 4)
    below, above = lax.rem(d + 1, 64), lax.rem(d + 63, 64)
    after, before = lax.rem(sec + 1, 4), lax.rem(sec + 3, 4)
    is_top = d == 0
    is_bottom = d == 63
    keep_top = jnp.where(is_top, 0.0, 1.0)
    keep_bottom = jnp.where(is_bottom, 0.0, 1.0)

    for load in loads:
        load.start()

    barrier = pltpu.get_barrier_semaphore()
    peers = [(lax.rem(sec + 2, 4), d)]
    for other in (after, before):
        peers += [(other, d), (other, below), (other, above)]
    for peer in peers:
        pl.semaphore_signal(barrier, inc=1, device_id=peer, device_id_type=MESH)

    def greet(k, carry):
        peer = (sec, lax.rem(d + k, 64))
        pl.semaphore_signal(barrier, inc=1, device_id=peer, device_id_type=MESH)
        return carry

    lax.fori_loop(1, 64, greet, 0)

    raw[2 * z + c] = jnp.zeros((16, LANES), BF16)
    raw[2 * z + c, 0:10, 0:11520] = w_ref[...]
    for load in loads:
        load.wait()
    pl.semaphore_wait(barrier, len(peers) + 63)

    def remote(src, dst, send, recv, peer):
        return pltpu.make_async_remote_copy(
            src_ref=src, dst_ref=dst, send_sem=send, recv_sem=recv, device_id=peer,
            device_id_type=MESH,
        )

    def combined(messages, count):
        means = messages[:, 0:1, :]
        mean = jnp.sum(means, axis=0) * (1.0 / 64)
        spread = jnp.sum(jnp.square(means - mean[None]), axis=0) * count
        squares = jnp.sum(messages[:, 1:2, :], axis=0) + spread
        return mean, lax.rsqrt(squares * (1.0 / (64 * count)) + EPSILON)

    def part_sums(blocks, groups, count, weight=None):
        total = blocks[0] if weight is None else blocks[0] * weight
        for block in blocks[1:]:
            total = total + block
        channel = jnp.sum(total, axis=1, keepdims=True)
        mean = jnp.sum(groups * channel, axis=0, keepdims=True) * (1.0 / count)
        own = jnp.sum(groups * mean, axis=1, keepdims=True)
        squares = None
        for block in blocks:
            off = jnp.square(block - own)
            off = off if weight is None else off * weight
            squares = off if squares is None else squares + off
        channel = jnp.sum(squares, axis=1, keepdims=True)
        return mean, jnp.sum(groups * channel, axis=0, keepdims=True)

    def start_exchange(e, mean, deviation):
        SA[e, 0] = jnp.concatenate([mean, deviation], axis=0)

        def one(k, carry):
            peer = (sec, lax.rem(d + k, 64))
            remote(SA.at[e, 0], SA.at[e, k], a_send.at[e], a_recv.at[e], peer).start()
            return carry

        lax.fori_loop(1, 64, one, 0)

    def finish_exchange(e, count):
        others = SA.at[e, pl.ds(1, 63)]
        remote(others, others, a_send.at[e], a_recv.at[e], (sec, below)).wait()
        return combined(SA[e], count)

    def exchanged(e, mean, deviation, count):
        start_exchange(e, mean, deviation)
        return finish_exchange(e, count)

    def columns(groups, rows):
        return [jnp.sum(groups * row, axis=1, keepdims=True) for row in rows]

    def across_copy():
        return remote(HS, HR, b_send.at[0], b_recv.at[0], (after, d))

    def rim_copies(kind, array, down, up):
        (down_from, down_to), (up_from, up_to) = down, up
        return [
            remote(array.at[pl.ds(down_from, size)], array.at[pl.ds(down_to, size)],
                   h_send.at[kind, 0], h_recv.at[kind, 0], (sec, below))
            for size in (2 if kind == 0 else 1,)
        ] + [
            remote(array.at[pl.ds(up_from, 1)], array.at[pl.ds(up_to, 1)],
                   h_send.at[kind, 1], h_recv.at[kind, 1], (sec, above))
        ]

    def start_all(copies):
        for copy in copies:
            copy.start()

    def wait_all(copies):
        for copy in copies:
            copy.wait()

    def tile_copies():
        return [
            remote(tile, cb.at[slot], c_send.at[slot], c_recv.at[slot], (after, peer))
            for slot, peer in ((1, d), (0, below), (2, above))
        ]

    def skip_copies():
        return [
            remote(skd.at[lax_rows(1, 4)], skb.at[lax_rows(2, 4)], k_send.at[0], k_recv.at[0], (before, d)),
            remote(skd.at[lax_rows(4, 1)], skb.at[lax_rows(1, 1)], k_send.at[1], k_recv.at[1], (before, below)),
            remote(skd.at[lax_rows(1, 1)], skb.at[lax_rows(6, 1)], k_send.at[2], k_recv.at[2], (before, above)),
        ]

    def lax_rows(start, size):
        return pl.ds(start, size)

    def hand_over(count):
        for copy in tile_copies():
            copy.start()

        @pl.when(sec < 2)
        def _():
            mean, deviation = part_sums([tile[...].astype(F32)], wide_groups[...], count)
            HS[...] = jnp.concatenate(exchanged(2, mean, deviation, count), axis=0)
            across_copy().start()
            across_copy().wait_send()

        for copy in tile_copies():
            copy.wait_send()

    def take_over():
        for copy in tile_copies():
            copy.wait_recv()

    chunks = jnp.where(sec == 0, 4, jnp.where(sec == 3, 5, 8))

    def gather_copies(core, stage, k):
        lanes = lambda off, size: pl.ds(pl.multiple_of(k * CHUNK + off, 128), size)
        mine, other = lanes(HALF * core, HALF), lanes(HALF * (1 - core), HALF)
        left, right = lanes(HALF * core, QUARTER), lanes(HALF * core + QUARTER, QUARTER)
        along_x = (space(y, xp, z, c), space(y, xm, z, c))
        along_y = (space(yp, x, z, c), space(ym, x, z, c))
        rows, every = pl.ds(0, 48), pl.ds(0, 4)
        array = W
        if stage == 0:
            array, whole = raw, pl.ds(0, 16)
            moves = [
                ((2 * z + c, whole, mine), space(y, x, 1 - z, c)),
                ((2 * z + c, whole, other), space(y, x, 1 - z, 1 - c)),
                ((2 * z + c, whole, other), space(y, x, z, 1 - c)),
            ]
        elif stage == 1:
            moves = [((y, x, rows, mine), peer) for peer in (along_y if core else along_x)]
        elif stage == 2 and core == 0:
            moves = [((y, xm, rows, left), along_x[0]), ((y, xp, rows, right), along_x[1])]
        elif stage == 2:
            moves = [((ym, x, rows, left), along_y[0]), ((yp, x, rows, right), along_y[1])]
        elif stage == 3 and core == 0:
            moves = [((y, every, rows, mine), peer) for peer in along_y]
        elif stage == 3:
            moves = [((every, x, rows, mine), peer) for peer in along_x]
        elif stage == 4 and core == 0:
            moves = [((ym, every, rows, left), along_y[0]), ((yp, every, rows, right), along_y[1])]
        elif stage == 4:
            moves = [((every, xm, rows, left), along_x[0]), ((every, xp, rows, right), along_x[1])]
        else:
            moves = [((every, every, rows, mine), space(y, x, z, 1 - c))]
        first_id = (0, 3, 5, 7, 9, 11)[stage]
        return [
            remote(
                array.at[where], array.at[where], gather_send.at[first_id + i, k],
                gather_recv.at[first_id + i, k], (sec, peer),
            )
            for i, (where, peer) in enumerate(moves)
        ]

    def gather_step(core, t):
        for stage in range(7):
            k = t - stage

            @pl.when((k >= 0) & (k < chunks))
            def _():
                if stage > 0:
                    for copy in gather_copies(core, stage - 1, k):
                        copy.wait_recv()
                if stage == 1:
                    lanes = pl.ds(pl.multiple_of(k * CHUNK + HALF * core, 128), HALF)
                    blocks = raw[:, :, lanes].reshape(64, HALF)
                    W[y, x, :, lanes] = dot(pack[...], blocks).astype(BF16)
                if stage < 6:
                    for copy in gather_copies(core, stage, k):
                        copy.start()

    def gather(first, last):
        def step(t, carry):
            for core in range(2):
                pl.when(c == core)(lambda core=core: gather_step(core, t))
            return carry

        lax.fori_loop(first, last, step, 0)

    def gather_end():
        def waits(core, k):
            for stage in range(6):
                for copy in gather_copies(core, stage, k):
                    copy.wait_send()

        def step(k, carry):
            for core in range(2):
                pl.when(c == core)(lambda core=core: waits(core, k))
            return carry

        lax.fori_loop(0, chunks, step, 0)

    def put_shifted(index, base, values):
        size = values.shape[0]
        sh[1, index, base : base + size, :] = values
        sh[0, index, base : base + size, :] = dot(values, shifts[0]).astype(BF16)
        sh[2, index, base : base + size, :] = dot(values, shifts[1]).astype(BF16)

    def fine_conv(pairs, pieces, per_tap, lead, lane_start, depth, source_row, use):
        taps = 9 * per_tap
        for p in range(2):
            if lead:
                col[p, 0:lead, :] = jnp.zeros((lead, 256), BF16)
            if lead + taps < depth:
                col[p, lead + taps : depth, :] = jnp.zeros((depth - lead - taps, 256), BF16)

        def pair(q, carry):
            for p in range(2):
                for dy in range(3):
                    for j in range(2):
                        row = source_row(q, j + dy)
                        for dx in range(3):
                            at = lead + (dy * 3 + dx) * per_tap
                            for to, start, size in pieces(p):
                                col[p, at + to : at + to + size, 128 * j : 128 * j + 128] = sh[
                                    dx, row, start : start + size, :
                                ]
            use(q, weighted(lane_start, depth, col))
            return carry

        lax.fori_loop(0, pairs, pair, 0)

    def weighted(lane_start, depth, source):
        total = None
        for p in range(2):
            kernels = W[2 * p : 2 * p + 2, :, :, lane_start : lane_start + depth]
            made = dot(kernels.reshape(384, depth), source[p, 0:depth, :])
            total = made if total is None else total + made
        return total

    narrow_pieces = lambda p: [(0, 160 * p, 160)]
    wide_pieces = lambda p: [(0, 320 * p, 320)]
    joined_pieces = lambda p: [(0, 160 * p, 160), (160, 320 + 160 * p, 160)]
    follow = lambda q, off: 2 * q + off
    narrow_scale = 1.0 / math.sqrt(9 * 320)
    wide_scale = 1.0 / math.sqrt(9 * 640)

    def row_kept(row):
        return jnp.where(row < 0, keep_top, jnp.where(row > 3, keep_bottom, 1.0))

    def activate_rows(source, start, stop, own_row, mean, rstd):
        def one(r, carry):
            values = activate(source[r].astype(F32), mean, rstd) * row_kept(r - own_row)
            put_shifted(r, 0, values.astype(BF16))
            return carry

        lax.fori_loop(start, stop, one, 0)

    @pl.when(sec == 0)
    def _():
        x_copies = [
            remote(x_ref.at[pl.ds(3, 1)], xr.at[pl.ds(2, 1)], x_send.at[0], x_recv.at[0], (0, below)),
            remote(x_ref.at[pl.ds(0, 1)], xr.at[pl.ds(7, 1)], x_send.at[1], x_recv.at[1], (0, above)),
        ]
        for copy in x_copies:
            copy.start()
        gather(0, 1)
        for r in range(4):
            xr[3 + r] = x_ref[r]
        hid[7] = jnp.zeros((320, 128), BF16)

        def permute(r, carry):
            xd[r] = dot(perm_x[...], xr[r]).astype(BF16)
            return carry

        lax.fori_loop(3, 7, permute, 0)
        groups = fine_groups[0]
        sums = part_sums([xd[r].astype(F32) for r in range(3, 7)], groups, ROW_N)
        gather(1, 2)
        start_exchange(0, *sums)
        gather(2, 7)
        for copy in x_copies:
            copy.wait()
        lax.fori_loop(2, 3, permute, 0)
        lax.fori_loop(7, 8, permute, 0)
        mean, rstd = columns(groups, finish_exchange(0, ROW_N))
        activate_rows(xd, 2, 8, 3, mean, rstd)

        def keep_hidden(q, made):
            rounded = (made * narrow_scale).astype(BF16)
            packed = dot(sel_di[...], rounded).astype(BF16)
            hid[2 * q + 2] = packed[:, 0:128]
            hid[2 * q + 3] = packed[:, 128:256]

        from_two = lambda q, off: 2 * q + off + 2
        fine_conv(2, narrow_pieces, 160, 0, 0, 1536, from_two, keep_hidden)
        rims = rim_copies(0, hid, (4, 0), (2, 6))
        start_all(rims)
        start_exchange(1, *part_sums([hid[r].astype(F32) for r in range(2, 6)], groups, ROW_N))
        gather(7, 8)
        mean, rstd = columns(groups, finish_exchange(1, ROW_N))
        wait_all(rims)
        activate_rows(hid, 0, 8, 2, mean, rstd)

        def keep_skip(q, made):
            for j in range(2):
                own = dot(exp_di[...], xd[2 * q + j + 2])
                rounded = (own + made[:, 128 * j : 128 * j + 128] * narrow_scale).astype(BF16)
                skd[2 * q + j] = dot(sel_di[...], rounded).astype(BF16)
                skn[2 * q + j] = dot(sel_nat[...], rounded).astype(BF16)

        fine_conv(3, narrow_pieces, 160, 32, 1408, 1536, follow, keep_skip)
        gather(8, 10)
        skn[0] = (skn[0].astype(F32) * keep_top).astype(BF16)
        col[0, 0:64, 0:128] = jnp.zeros((64, 128), BF16)
        for dy in range(3):
            for dx in range(3):
                at = 64 + (dy * 3 + dx) * 320
                made = dot(skn[dy], strided[0, dx]) + dot(skn[2 + dy], strided[1, dx])
                col[0, at : at + 320, 0:128] = made.astype(BF16)
        made = dot(W[:, :, :, 2816:5760].reshape(768, 2944), col[0, :, 0:128])
        rounded = (made * narrow_scale).astype(BF16)
        tile[...] = dot(sel_c[...], rounded).astype(BF16)
        hand_over(128 * 20)
        start_all(skip_copies())
        for copy in skip_copies():
            copy.wait_send()

    @pl.when((sec == 1) | (sec == 2))
    def _():
        gather(0, chunks + 6)
        take_over()
        count = 128 * 20
        groups = wide_groups[...]
        across_copy().wait_recv()
        mean, rstd = columns(groups, [HR[0:1, :], HR[1:2, :]])

        def activate_tiles(source):
            for i in range(3):
                values = activate(source[i].astype(F32), mean, rstd)
                values = values * (keep_top, 1.0, keep_bottom)[i]
                a3[:, 128 * i : 128 * i + 128] = values.astype(BF16)

        def coarse_conv(lane_start):
            for t in range(9):
                px = ((0, 256), (128, 256), (128, 384))[t // 3]
                moved = dot(a3[:, px[0] : px[1]], taps[t, px[0] : px[1], :])
                colw[640 * t : 640 * t + 640, :] = moved.astype(BF16)
            total = None
            for i in range(3):
                lanes = slice(lane_start + 1920 * i, lane_start + 1920 * i + 1920)
                source = colw[1920 * i : 1920 * i + 1920, :]
                made = dot(W[:, :, :, lanes].reshape(768, 1920), source)
                total = made if total is None else total + made
            return total * wide_scale

        activate_tiles(cb)
        rounded = coarse_conv(0).astype(BF16)
        hidden = dot(sel_c[...], rounded)
        ht[1] = hidden.astype(BF16)
        rims = rim_copies(3, ht, (1, 0), (1, 2))
        start_all(rims)
        sums = part_sums([hidden], groups, count)
        mean, rstd = columns(groups, exchanged(3, *sums, count))
        wait_all(rims)
        activate_tiles(ht)
        made = coarse_conv(5760)
        own = dot(exp_c[...], cb[1])
        rounded = (own + made).astype(BF16)
        tile[...] = dot(sel_c[...], rounded).astype(BF16)
        hand_over(count)

    def out_copies(sections=range(3)):
        return [
            remote(
                outs.at[pl.ds(0, 4), pl.ds(32 * t, 32)], landed, o_send.at[t], o_recv.at[0], (t, d)
            )
            for t in sections
        ]

    @pl.when(sec == 3)
    def _():
        gather(0, chunks + 6)
        for copy in skip_copies():
            copy.wait_recv()
        take_over()
        for i in range(3):
            moved = dot(perm_c[...], cb[i]) * (keep_top, 1.0, keep_bottom)[i]
            moved = moved.astype(BF16)
            for half in ((1,), (0, 1), (0,))[i]:
                for dx in range(3):
                    sh[dx, 2 * i + half] = dot(moved, doubled[half, dx]).astype(BF16)

        def keep_upper(q, made):
            rounded = (made * wide_scale).astype(BF16)
            packed = dot(sel_di[...], rounded).astype(BF16)
            ud[2 * q + 2] = packed[:, 0:128]
            ud[2 * q + 3] = packed[:, 128:256]

        half_row = lambda q, off: q + 1 + (off + 1) // 2
        fine_conv(2, wide_pieces, 320, 0, 0, 2944, half_row, keep_upper)
        rims = rim_copies(1, ud, (5, 1), (2, 6))
        start_all(rims)
        groups_u, groups_s = fine_groups[1], fine_groups[2]
        mean_u, dev_u = part_sums([ud[r].astype(F32) for r in range(2, 6)], groups_u, 2 * ROW_N)
        mean_s, dev_s = part_sums([skb[r].astype(F32) for r in range(2, 6)], groups_s, 2 * ROW_N)
        rows = exchanged(4, mean_u + mean_s, dev_u + dev_s, 2 * ROW_N)
        wait_all(rims)
        mean_u, rstd_u = columns(groups_u, rows)
        mean_s, rstd_s = columns(groups_s, rows)

        def joined_row(r, carry):
            kept = row_kept(r - 2)
            upper = activate(ud[r].astype(F32), mean_u, rstd_u) * kept
            put_shifted(r, 0, upper.astype(BF16))
            lower = activate(skb[r].astype(F32), mean_s, rstd_s) * kept
            put_shifted(r, 320, lower.astype(BF16))
            return carry

        lax.fori_loop(1, 7, joined_row, 0)

        def keep_hidden(q, made):
            rounded = (made * wide_scale).astype(BF16)
            packed = dot(sel_di[...], rounded).astype(BF16)
            hid[2 * q + 1] = packed[:, 0:128]
            hid[2 * q + 2] = packed[:, 128:256]

        from_one = lambda q, off: 2 * q + off + 1
        fine_conv(2, joined_pieces, 320, 64, 2816, 2944, from_one, keep_hidden)
        rims = rim_copies(2, hid, (4, 0), (1, 5))
        start_all(rims)
        groups = fine_groups[0]
        sums = part_sums([hid[r].astype(F32) for r in range(1, 5)], groups, ROW_N)
        mean, rstd = columns(groups, exchanged(5, *sums, ROW_N))
        wait_all(rims)
        activate_rows(hid, 0, 6, 1, mean, rstd)
        for p in range(2):
            colj[p, 0:32, :] = jnp.zeros((32, 256), BF16)
            colj[p, 352:384, :] = jnp.zeros((32, 256), BF16)

        def keep_output(q, made):
            for p in range(2):
                for j in range(2):
                    px = slice(128 * j, 128 * j + 128)
                    colj[p, 32:192, px] = ud[2 * q + j + 2, 160 * p : 160 * p + 160, :]
                    colj[p, 192:352, px] = skb[2 * q + j + 2, 160 * p : 160 * p + 160, :]
            straight = weighted(7168, 384, colj)
            total = made * narrow_scale + straight * (1.0 / math.sqrt(640))
            rounded = total.astype(BF16)
            for j in range(2):
                flipped = lax.dot_general(
                    rounded[:, 128 * j : 128 * j + 128], exp_nat[...], (((0,), (0,)), ((), ())),
                    preferred_element_type=F32,
                )
                outs[2 * q + j] = flipped.astype(BF16)

        fine_conv(2, narrow_pieces, 160, 0, 5760, 1536, follow, keep_output)
        for copy in out_copies():
            copy.start()
        out_ref[...] = outs[:, 96:128, :]
        for copy in out_copies():
            copy.wait_send()

    @pl.when(sec < 3)
    def _():
        for copy in out_copies((0,)):
            copy.wait_recv()
        out_ref[...] = landed[...]

    gather_end()


def entry(count, x_ref, w_ref, *refs):
    sources, out_ref, copies = refs[:count], refs[count], refs[count + 1 : 2 * count + 1]
    sems, others = refs[2 * count + 1], refs[2 * count + 2 :]
    loads = [
        pltpu.make_async_copy(source, copy, sems.at[i])
        for i, (source, copy) in enumerate(zip(sources, copies))
    ]
    kernel(loads, x_ref, w_ref, *copies, out_ref, *others)


def shards(features, section_packs):
    fields = jnp.swapaxes(features[0], 1, 2)
    packs = jnp.swapaxes(section_packs[0], 0, 1)
    tables = selections()
    dma = pltpu.SemaphoreType.DMA
    scratch = [pltpu.VMEM(table.shape, table.dtype) for table in tables]
    scratch += [
        dma((len(tables),)),
        pltpu.VMEM((4, 4, 48, LANES), BF16),
        pltpu.VMEM((4, 16, LANES), BF16),
        pltpu.VMEM((2, 2944, 256), BF16),
        pltpu.VMEM((5760, 128), BF16),
        pltpu.VMEM((2, 384, 256), BF16),
        pltpu.VMEM((3, 10, 640, 128), BF16),
        pltpu.VMEM((10, 320, 128), BF16),
        pltpu.VMEM((10, 320, 128), BF16),
        pltpu.VMEM((8, 320, 128), BF16),
        pltpu.VMEM((6, 320, 128), BF16),
        pltpu.VMEM((6, 320, 128), BF16),
        pltpu.VMEM((8, 320, 128), BF16),
        pltpu.VMEM((3, 640, 128), BF16),
        pltpu.VMEM((3, 640, 128), BF16),
        pltpu.VMEM((640, 128), BF16),
        pltpu.VMEM((640, 384), BF16),
        pltpu.VMEM((8, 320, 128), BF16),
        pltpu.VMEM((4, 128, 320), BF16),
        pltpu.VMEM((4, 32, 320), BF16),
        pltpu.VMEM((6, 64, 2, 128), F32),
        pltpu.VMEM((2, 128), F32),
        pltpu.VMEM((2, 128), F32),
        dma((12, 8)), dma((12, 8)),
        dma((6,)), dma((6,)), dma((1,)), dma((1,)),
        dma((2,)), dma((2,)), dma((4, 2)), dma((4, 2)), dma((3,)), dma((3,)), dma((3,)), dma((3,)), dma((3,)), dma((1,)),
    ]
    vmem = pl.BlockSpec(memory_space=pltpu.VMEM)
    out = pl.pallas_call(
        functools.partial(entry, len(tables)),
        out_shape=jax.ShapeDtypeStruct((4, 32, 320), BF16),
        in_specs=[vmem] * 2 + [pl.BlockSpec(memory_space=pl.ANY)] * len(tables),
        out_specs=vmem,
        scratch_shapes=scratch,
        compiler_params=pltpu.CompilerParams(
            collective_id=0, has_side_effects=True, vmem_limit_bytes=62 * 1024 * 1024
        ),
        cost_estimate=pl.CostEstimate(
            flops=12_000_000_000, bytes_accessed=30_000_000, transcendentals=2_000_000
        ),
    )(fields, packs, *tables)
    return out[None]


def solution(mesh):
    return jax.shard_map(
        shards,
        mesh=mesh,
        in_specs=(P(None, "space", None, None), P("section", None, "space")),
        out_specs=P(None, "space", "section", None),
        check_vma=False,
    )
```

```python
import functools
import math

import jax
import jax.numpy as jnp
import numpy as np
from jax import lax
from jax.experimental import pallas as pl
from jax.experimental.pallas import tpu as pltpu
from jax.sharding import PartitionSpec as P

F32 = jnp.float32
BF16 = jnp.bfloat16
MESH = pl.DeviceIdType.MESH
EPSILON = 1e-05
CHUNK = 1536
HALF = CHUNK // 2
QUARTER = CHUNK // 4
ROW_N = 512 * 10
LANES = 8 * CHUNK


def selections():
    rows = np.arange(768)
    chan_wide = np.where(rows % 48 < 40, 40 * (rows // 48) + rows % 48, -1)
    chan_fine = chan_wide[:384]
    rows = np.arange(48)
    packed = np.where(rows < 40, 16 * (rows // 10) + rows % 10, -1)
    split = lambda n: np.concatenate([np.arange(0, n, 2), np.arange(1, n, 2)])
    di, di_wide = split(320), split(640)
    nat, nat_wide = np.arange(320), np.arange(640)
    eq = lambda a, b: (a[:, None] == b[None, :])
    b = np.arange(128)
    shifts = np.stack([eq(b, b + dx) for dx in (-1, 1)])
    strided = np.stack(
        [
            np.stack([eq(b, 2 * (b % 64) + dx) & (b // 64 == i)[None, :] for dx in (-1, 0, 1)])
            for i in (0, 1)
        ]
    )
    doubled = np.stack(
        [
            np.stack(
                [
                    eq(b, 64 * half + (b + dx) // 2) & ((b + dx >= 0) & (b + dx < 128))[None, :]
                    for dx in (-1, 0, 1)
                ]
            )
            for half in (0, 1)
        ]
    )

    def taps():
        a, c = np.arange(6 * 64), np.arange(2 * 64)
        out = []
        for dy in (0, 1, 2):
            for dx in (-1, 0, 1):
                col = c % 64 + dx
                out.append(
                    eq(a, (c // 64 + 1 + dy) * 64 + col) & ((col >= 0) & (col < 64))[None, :]
                )
        return np.stack(out)

    group = np.arange(128)
    fine_groups = np.stack(
        [eq(di // 10, group), eq(di // 20, group), eq(16 + di // 20, group)]
    )
    wide_groups = eq(nat_wide // 20, group)
    bf = lambda m: np.asarray(m, np.float32).astype(jnp.bfloat16)
    return (
        bf(eq(packed, np.arange(64))),
        bf(eq(di, chan_fine)),
        bf(eq(nat, chan_fine)),
        bf(eq(chan_fine, di)),
        bf(eq(chan_fine, nat)),
        bf(eq(nat_wide, chan_wide)),
        bf(eq(chan_wide, nat_wide)),
        bf(eq(di, nat)),
        bf(eq(di_wide, nat_wide)),
        bf(shifts),
        bf(strided),
        bf(doubled),
        bf(taps()),
        np.asarray(fine_groups, np.float32),
        np.asarray(wide_groups, np.float32),
    )


def dot(a, b):
    return jnp.dot(a, b, preferred_element_type=F32)


def activate(values, mean, rstd):
    z = (values - mean) * rstd
    return z / (1.0 + jnp.exp(-z))


def kernel(
    loads,     x_ref, w_ref, pack, sel_di, sel_nat, exp_di, exp_nat, sel_c, exp_c, perm_x, perm_c, shifts, strided,
    doubled, taps, fine_groups, wide_groups, out_ref,
    W, raw, col, colw, colj, sh, xr, xd, hid, skd, skn, skb, cb, ht, tile, a3, ud, outs, landed,
    SA, HS, HR, gather_send, gather_recv, a_send, a_recv, b_send, b_recv,
    x_send, x_recv, h_send, h_recv, c_send, c_recv, k_send, k_recv, o_send, o_recv,
):
    sec = lax.axis_index("section")
    d = lax.axis_index("space")
    c = lax.rem(d, 2)
    z = lax.rem(lax.div(d, 2), 2)
    x = lax.rem(lax.div(d, 4), 4)
    y = lax.div(d, 16)
    space = lambda y, x, z, c: ((y * 4 + x) * 2 + z) * 2 + c
    xp, xm = lax.rem(x + 1, 4), lax.rem(x + 3, 4)
    yp, ym = lax.rem(y + 1, 4), lax.rem(y + 3, 4)
    below, above = lax.rem(d + 1, 64), lax.rem(d + 63, 64)
    after, before = lax.rem(sec + 1, 4), lax.rem(sec + 3, 4)
    is_top = d == 0
    is_bottom = d == 63
    keep_top = jnp.where(is_top, 0.0, 1.0)
    keep_bottom = jnp.where(is_bottom, 0.0, 1.0)

    for load in loads:
        load.start()

    barrier = pltpu.get_barrier_semaphore()
    peers = [(lax.rem(sec + 2, 4), d)]
    for other in (after, before):
        peers += [(other, d), (other, below), (other, above)]
    for peer in peers:
        pl.semaphore_signal(barrier, inc=1, device_id=peer, device_id_type=MESH)

    def greet(k, carry):
        peer = (sec, lax.rem(d + k, 64))
        pl.semaphore_signal(barrier, inc=1, device_id=peer, device_id_type=MESH)
        return carry

    lax.fori_loop(1, 64, greet, 0)

    raw[2 * z + c] = jnp.zeros((16, LANES), BF16)
    raw[2 * z + c, 0:10, 0:11520] = w_ref[...]
    for load in loads:
        load.wait()
    pl.semaphore_wait(barrier, len(peers) + 63)

    def remote(src, dst, send, recv, peer):
        return pltpu.make_async_remote_copy(
            src_ref=src, dst_ref=dst, send_sem=send, recv_sem=recv, device_id=peer,
            device_id_type=MESH,
        )

    def combined(messages, count):
        means = messages[:, 0:1, :]
        mean = jnp.sum(means, axis=0) * (1.0 / 64)
        spread = jnp.sum(jnp.square(means - mean[None]), axis=0) * count
        squares = jnp.sum(messages[:, 1:2, :], axis=0) + spread
        return mean, lax.rsqrt(squares * (1.0 / (64 * count)) + EPSILON)

    def part_sums(blocks, groups, count, weight=None):
        total = blocks[0] if weight is None else blocks[0] * weight
        for block in blocks[1:]:
            total = total + block
        channel = jnp.sum(total, axis=1, keepdims=True)
        mean = jnp.sum(groups * channel, axis=0, keepdims=True) * (1.0 / count)
        own = jnp.sum(groups * mean, axis=1, keepdims=True)
        squares = None
        for block in blocks:
            off = jnp.square(block - own)
            off = off if weight is None else off * weight
            squares = off if squares is None else squares + off
        channel = jnp.sum(squares, axis=1, keepdims=True)
        return mean, jnp.sum(groups * channel, axis=0, keepdims=True)

    def start_exchange(e, mean, deviation):
        SA[e, 0] = jnp.concatenate([mean, deviation], axis=0)

        def one(k, carry):
            peer = (sec, lax.rem(d + k, 64))
            remote(SA.at[e, 0], SA.at[e, k], a_send.at[e], a_recv.at[e], peer).start()
            return carry

        lax.fori_loop(1, 64, one, 0)

    def finish_exchange(e, count):
        others = SA.at[e, pl.ds(1, 63)]
        remote(others, others, a_send.at[e], a_recv.at[e], (sec, below)).wait()
        return combined(SA[e], count)

    def exchanged(e, mean, deviation, count):
        start_exchange(e, mean, deviation)
        return finish_exchange(e, count)

    def columns(groups, rows):
        return [jnp.sum(groups * row, axis=1, keepdims=True) for row in rows]

    def across_copy():
        return remote(HS, HR, b_send.at[0], b_recv.at[0], (after, d))

    def rim_copies(kind, array, down, up):
        (down_from, down_to), (up_from, up_to) = down, up
        return [
            remote(array.at[pl.ds(down_from, size)], array.at[pl.ds(down_to, size)],
                   h_send.at[kind, 0], h_recv.at[kind, 0], (sec, below))
            for size in (2 if kind == 0 else 1,)
        ] + [
            remote(array.at[pl.ds(up_from, 1)], array.at[pl.ds(up_to, 1)],
                   h_send.at[kind, 1], h_recv.at[kind, 1], (sec, above))
        ]

    def start_all(copies):
        for copy in copies:
            copy.start()

    def wait_all(copies):
        for copy in copies:
            copy.wait()

    def tile_copies():
        return [
            remote(tile, cb.at[slot], c_send.at[slot], c_recv.at[slot], (after, peer))
            for slot, peer in ((1, d), (0, below), (2, above))
        ]

    def skip_copies():
        return [
            remote(skd.at[lax_rows(1, 4)], skb.at[lax_rows(2, 4)], k_send.at[0], k_recv.at[0], (before, d)),
            remote(skd.at[lax_rows(4, 1)], skb.at[lax_rows(1, 1)], k_send.at[1], k_recv.at[1], (before, below)),
            remote(skd.at[lax_rows(1, 1)], skb.at[lax_rows(6, 1)], k_send.at[2], k_recv.at[2], (before, above)),
        ]

    def lax_rows(start, size):
        return pl.ds(start, size)

    def hand_over(count):
        for copy in tile_copies():
            copy.start()

        @pl.when(sec < 2)
        def _():
            mean, deviation = part_sums([tile[...].astype(F32)], wide_groups[...], count)
            HS[...] = jnp.concatenate(exchanged(2, mean, deviation, count), axis=0)
            across_copy().start()
            across_copy().wait_send()

        for copy in tile_copies():
            copy.wait_send()

    def take_over():
        for copy in tile_copies():
            copy.wait_recv()

    chunks = jnp.where(sec == 0, 4, jnp.where(sec == 3, 5, 8))

    def gather_copies(core, stage, k):
        lanes = lambda off, size: pl.ds(pl.multiple_of(k * CHUNK + off, 128), size)
        mine, other = lanes(HALF * core, HALF), lanes(HALF * (1 - core), HALF)
        left, right = lanes(HALF * core, QUARTER), lanes(HALF * core + QUARTER, QUARTER)
        along_x = (space(y, xp, z, c), space(y, xm, z, c))
        along_y = (space(yp, x, z, c), space(ym, x, z, c))
        rows, every = pl.ds(0, 48), pl.ds(0, 4)
        array, sibling = W, space(y, x, z, 1 - c)

        def line(core, at, lanes=mine):
            return (every, at, rows, lanes) if core else (at, every, rows, lanes)

        if stage == 0:
            array, whole = raw, pl.ds(0, 16)
            moves = [
                ((2 * z + c, whole, mine), space(y, x, 1 - z, c)),
                ((2 * z + c, whole, other), space(y, x, 1 - z, 1 - c)),
                ((2 * z + c, whole, other), space(y, x, z, 1 - c)),
            ]
        elif stage == 1:
            moves = [((y, x, rows, mine), peer) for peer in (along_y if core else along_x)]
        elif stage == 2 and core == 0:
            moves = [((y, xm, rows, left), along_x[0]), ((y, xp, rows, right), along_x[1])]
        elif stage == 2:
            moves = [((ym, x, rows, left), along_y[0]), ((yp, x, rows, right), along_y[1])]
        elif stage == 3:
            own = line(core, x if core else y)
            moves = [(own, peer) for peer in (along_x if core else along_y)] + [(own, sibling)]
        elif stage == 4:
            up, down = (xm, xp) if core else (ym, yp)
            to_next, to_last = along_x if core else along_y
            moves = [(line(core, up, left), to_next), (line(core, down, right), to_last)]
            moves += [(line(core, up), sibling), (line(core, down), sibling)]
        else:
            moves = [(line(core, lax.rem((x if core else y) + 2, 4)), sibling)]
        first_id = (0, 3, 5, 7, 10, 14)[stage]
        return [
            remote(
                array.at[where], array.at[where], gather_send.at[first_id + i, k],
                gather_recv.at[first_id + i, k], (sec, peer),
            )
            for i, (where, peer) in enumerate(moves)
        ]

    def gather_step(core, t):
        for stage in range(7):
            k = t - stage

            @pl.when((k >= 0) & (k < chunks))
            def _():
                if stage > 0:
                    for copy in gather_copies(core, stage - 1, k):
                        copy.wait_recv()
                if stage == 1:
                    lanes = pl.ds(pl.multiple_of(k * CHUNK + HALF * core, 128), HALF)
                    blocks = raw[:, :, lanes].reshape(64, HALF)
                    W[y, x, :, lanes] = dot(pack[...], blocks).astype(BF16)
                if stage < 6:
                    for copy in gather_copies(core, stage, k):
                        copy.start()

    def gather(first, last):
        def step(t, carry):
            for core in range(2):
                pl.when(c == core)(lambda core=core: gather_step(core, t))
            return carry

        lax.fori_loop(first, last, step, 0)

    def gather_end():
        def waits(core, k):
            for stage in range(6):
                for copy in gather_copies(core, stage, k):
                    copy.wait_send()

        def step(k, carry):
            for core in range(2):
                pl.when(c == core)(lambda core=core: waits(core, k))
            return carry

        lax.fori_loop(0, chunks, step, 0)

    def put_shifted(index, base, values):
        size = values.shape[0]
        sh[1, index, base : base + size, :] = values
        sh[0, index, base : base + size, :] = dot(values, shifts[0]).astype(BF16)
        sh[2, index, base : base + size, :] = dot(values, shifts[1]).astype(BF16)

    def fine_conv(pairs, pieces, per_tap, lead, lane_start, depth, source_row, use):
        taps = 9 * per_tap
        for p in range(2):
            if lead:
                col[p, 0:lead, :] = jnp.zeros((lead, 256), BF16)
            if lead + taps < depth:
                col[p, lead + taps : depth, :] = jnp.zeros((depth - lead - taps, 256), BF16)

        def pair(q, carry):
            for p in range(2):
                for dy in range(3):
                    for j in range(2):
                        row = source_row(q, j + dy)
                        for dx in range(3):
                            at = lead + (dy * 3 + dx) * per_tap
                            for to, start, size in pieces(p):
                                col[p, at + to : at + to + size, 128 * j : 128 * j + 128] = sh[
                                    dx, row, start : start + size, :
                                ]
            use(q, weighted(lane_start, depth, col))
            return carry

        lax.fori_loop(0, pairs, pair, 0)

    def weighted(lane_start, depth, source):
        total = None
        for p in range(2):
            kernels = W[2 * p : 2 * p + 2, :, :, lane_start : lane_start + depth]
            made = dot(kernels.reshape(384, depth), source[p, 0:depth, :])
            total = made if total is None else total + made
        return total

    narrow_pieces = lambda p: [(0, 160 * p, 160)]
    wide_pieces = lambda p: [(0, 320 * p, 320)]
    joined_pieces = lambda p: [(0, 160 * p, 160), (160, 320 + 160 * p, 160)]
    follow = lambda q, off: 2 * q + off
    narrow_scale = 1.0 / math.sqrt(9 * 320)
    wide_scale = 1.0 / math.sqrt(9 * 640)

    def row_kept(row):
        return jnp.where(row < 0, keep_top, jnp.where(row > 3, keep_bottom, 1.0))

    def activate_rows(source, start, stop, own_row, mean, rstd):
        def one(r, carry):
            values = activate(source[r].astype(F32), mean, rstd) * row_kept(r - own_row)
            put_shifted(r, 0, values.astype(BF16))
            return carry

        lax.fori_loop(start, stop, one, 0)

    @pl.when(sec == 0)
    def _():
        x_copies = [
            remote(x_ref.at[pl.ds(3, 1)], xr.at[pl.ds(2, 1)], x_send.at[0], x_recv.at[0], (0, below)),
            remote(x_ref.at[pl.ds(0, 1)], xr.at[pl.ds(7, 1)], x_send.at[1], x_recv.at[1], (0, above)),
        ]
        for copy in x_copies:
            copy.start()
        gather(0, 1)
        for r in range(4):
            xr[3 + r] = x_ref[r]
        hid[7] = jnp.zeros((320, 128), BF16)

        def permute(r, carry):
            xd[r] = dot(perm_x[...], xr[r]).astype(BF16)
            return carry

        lax.fori_loop(3, 7, permute, 0)
        groups = fine_groups[0]
        sums = part_sums([xd[r].astype(F32) for r in range(3, 7)], groups, ROW_N)
        gather(1, 2)
        start_exchange(0, *sums)
        gather(2, 7)
        for copy in x_copies:
            copy.wait()
        lax.fori_loop(2, 3, permute, 0)
        lax.fori_loop(7, 8, permute, 0)
        mean, rstd = columns(groups, finish_exchange(0, ROW_N))
        activate_rows(xd, 2, 8, 3, mean, rstd)

        def keep_hidden(q, made):
            rounded = (made * narrow_scale).astype(BF16)
            packed = dot(sel_di[...], rounded).astype(BF16)
            hid[2 * q + 2] = packed[:, 0:128]
            hid[2 * q + 3] = packed[:, 128:256]

        from_two = lambda q, off: 2 * q + off + 2
        fine_conv(2, narrow_pieces, 160, 0, 0, 1536, from_two, keep_hidden)
        rims = rim_copies(0, hid, (4, 0), (2, 6))
        start_all(rims)
        start_exchange(1, *part_sums([hid[r].astype(F32) for r in range(2, 6)], groups, ROW_N))
        gather(7, 8)
        mean, rstd = columns(groups, finish_exchange(1, ROW_N))
        wait_all(rims)
        activate_rows(hid, 0, 8, 2, mean, rstd)

        def keep_skip(q, made):
            for j in range(2):
                own = dot(exp_di[...], xd[2 * q + j + 2])
                rounded = (own + made[:, 128 * j : 128 * j + 128] * narrow_scale).astype(BF16)
                skd[2 * q + j] = dot(sel_di[...], rounded).astype(BF16)
                skn[2 * q + j] = dot(sel_nat[...], rounded).astype(BF16)

        fine_conv(3, narrow_pieces, 160, 32, 1408, 1536, follow, keep_skip)
        gather(8, 10)
        skn[0] = (skn[0].astype(F32) * keep_top).astype(BF16)
        col[0, 0:64, 0:128] = jnp.zeros((64, 128), BF16)
        for dy in range(3):
            for dx in range(3):
                at = 64 + (dy * 3 + dx) * 320
                made = dot(skn[dy], strided[0, dx]) + dot(skn[2 + dy], strided[1, dx])
                col[0, at : at + 320, 0:128] = made.astype(BF16)
        made = dot(W[:, :, :, 2816:5760].reshape(768, 2944), col[0, :, 0:128])
        rounded = (made * narrow_scale).astype(BF16)
        tile[...] = dot(sel_c[...], rounded).astype(BF16)
        hand_over(128 * 20)
        start_all(skip_copies())
        for copy in skip_copies():
            copy.wait_send()

    @pl.when((sec == 1) | (sec == 2))
    def _():
        gather(0, chunks + 6)
        take_over()
        count = 128 * 20
        groups = wide_groups[...]
        across_copy().wait_recv()
        mean, rstd = columns(groups, [HR[0:1, :], HR[1:2, :]])

        def activate_tiles(source):
            for i in range(3):
                values = activate(source[i].astype(F32), mean, rstd)
                values = values * (keep_top, 1.0, keep_bottom)[i]
                a3[:, 128 * i : 128 * i + 128] = values.astype(BF16)

        def coarse_conv(lane_start):
            for t in range(9):
                px = ((0, 256), (128, 256), (128, 384))[t // 3]
                moved = dot(a3[:, px[0] : px[1]], taps[t, px[0] : px[1], :])
                colw[640 * t : 640 * t + 640, :] = moved.astype(BF16)
            total = None
            for i in range(3):
                lanes = slice(lane_start + 1920 * i, lane_start + 1920 * i + 1920)
                source = colw[1920 * i : 1920 * i + 1920, :]
                made = dot(W[:, :, :, lanes].reshape(768, 1920), source)
                total = made if total is None else total + made
            return total * wide_scale

        activate_tiles(cb)
        rounded = coarse_conv(0).astype(BF16)
        hidden = dot(sel_c[...], rounded)
        ht[1] = hidden.astype(BF16)
        rims = rim_copies(3, ht, (1, 0), (1, 2))
        start_all(rims)
        sums = part_sums([hidden], groups, count)
        mean, rstd = columns(groups, exchanged(3, *sums, count))
        wait_all(rims)
        activate_tiles(ht)
        made = coarse_conv(5760)
        own = dot(exp_c[...], cb[1])
        rounded = (own + made).astype(BF16)
        tile[...] = dot(sel_c[...], rounded).astype(BF16)
        hand_over(count)

    def out_copies(sections=range(3)):
        return [
            remote(
                outs.at[pl.ds(0, 4), pl.ds(32 * t, 32)], landed, o_send.at[t], o_recv.at[0], (t, d)
            )
            for t in sections
        ]

    @pl.when(sec == 3)
    def _():
        gather(0, chunks + 6)
        for copy in skip_copies():
            copy.wait_recv()
        take_over()
        for i in range(3):
            moved = dot(perm_c[...], cb[i]) * (keep_top, 1.0, keep_bottom)[i]
            moved = moved.astype(BF16)
            for half in ((1,), (0, 1), (0,))[i]:
                for dx in range(3):
                    sh[dx, 2 * i + half] = dot(moved, doubled[half, dx]).astype(BF16)

        def keep_upper(q, made):
            rounded = (made * wide_scale).astype(BF16)
            packed = dot(sel_di[...], rounded).astype(BF16)
            ud[2 * q + 2] = packed[:, 0:128]
            ud[2 * q + 3] = packed[:, 128:256]

        half_row = lambda q, off: q + 1 + (off + 1) // 2
        fine_conv(2, wide_pieces, 320, 0, 0, 2944, half_row, keep_upper)
        rims = rim_copies(1, ud, (5, 1), (2, 6))
        start_all(rims)
        groups_u, groups_s = fine_groups[1], fine_groups[2]
        mean_u, dev_u = part_sums([ud[r].astype(F32) for r in range(2, 6)], groups_u, 2 * ROW_N)
        mean_s, dev_s = part_sums([skb[r].astype(F32) for r in range(2, 6)], groups_s, 2 * ROW_N)
        rows = exchanged(4, mean_u + mean_s, dev_u + dev_s, 2 * ROW_N)
        wait_all(rims)
        mean_u, rstd_u = columns(groups_u, rows)
        mean_s, rstd_s = columns(groups_s, rows)

        def joined_row(r, carry):
            kept = row_kept(r - 2)
            upper = activate(ud[r].astype(F32), mean_u, rstd_u) * kept
            put_shifted(r, 0, upper.astype(BF16))
            lower = activate(skb[r].astype(F32), mean_s, rstd_s) * kept
            put_shifted(r, 320, lower.astype(BF16))
            return carry

        lax.fori_loop(1, 7, joined_row, 0)

        def keep_hidden(q, made):
            rounded = (made * wide_scale).astype(BF16)
            packed = dot(sel_di[...], rounded).astype(BF16)
            hid[2 * q + 1] = packed[:, 0:128]
            hid[2 * q + 2] = packed[:, 128:256]

        from_one = lambda q, off: 2 * q + off + 1
        fine_conv(2, joined_pieces, 320, 64, 2816, 2944, from_one, keep_hidden)
        rims = rim_copies(2, hid, (4, 0), (1, 5))
        start_all(rims)
        groups = fine_groups[0]
        sums = part_sums([hid[r].astype(F32) for r in range(1, 5)], groups, ROW_N)
        mean, rstd = columns(groups, exchanged(5, *sums, ROW_N))
        wait_all(rims)
        activate_rows(hid, 0, 6, 1, mean, rstd)
        for p in range(2):
            colj[p, 0:32, :] = jnp.zeros((32, 256), BF16)
            colj[p, 352:384, :] = jnp.zeros((32, 256), BF16)

        def keep_output(q, made):
            for p in range(2):
                for j in range(2):
                    px = slice(128 * j, 128 * j + 128)
                    colj[p, 32:192, px] = ud[2 * q + j + 2, 160 * p : 160 * p + 160, :]
                    colj[p, 192:352, px] = skb[2 * q + j + 2, 160 * p : 160 * p + 160, :]
            straight = weighted(7168, 384, colj)
            total = made * narrow_scale + straight * (1.0 / math.sqrt(640))
            rounded = total.astype(BF16)
            for j in range(2):
                flipped = lax.dot_general(
                    rounded[:, 128 * j : 128 * j + 128], exp_nat[...], (((0,), (0,)), ((), ())),
                    preferred_element_type=F32,
                )
                outs[2 * q + j] = flipped.astype(BF16)

        fine_conv(2, narrow_pieces, 160, 0, 5760, 1536, follow, keep_output)
        for copy in out_copies():
            copy.start()
        out_ref[...] = outs[:, 96:128, :]
        for copy in out_copies():
            copy.wait_send()

    @pl.when(sec < 3)
    def _():
        for copy in out_copies((0,)):
            copy.wait_recv()
        out_ref[...] = landed[...]

    gather_end()


def entry(count, x_ref, w_ref, *refs):
    sources, out_ref, copies = refs[:count], refs[count], refs[count + 1 : 2 * count + 1]
    sems, others = refs[2 * count + 1], refs[2 * count + 2 :]
    loads = [
        pltpu.make_async_copy(source, copy, sems.at[i])
        for i, (source, copy) in enumerate(zip(sources, copies))
    ]
    kernel(loads, x_ref, w_ref, *copies, out_ref, *others)


def shards(features, section_packs):
    fields = jnp.swapaxes(features[0], 1, 2)
    packs = jnp.swapaxes(section_packs[0], 0, 1)
    tables = selections()
    dma = pltpu.SemaphoreType.DMA
    scratch = [pltpu.VMEM(table.shape, table.dtype) for table in tables]
    scratch += [
        dma((len(tables),)),
        pltpu.VMEM((4, 4, 48, LANES), BF16),
        pltpu.VMEM((4, 16, LANES), BF16),
        pltpu.VMEM((2, 2944, 256), BF16),
        pltpu.VMEM((5760, 128), BF16),
        pltpu.VMEM((2, 384, 256), BF16),
        pltpu.VMEM((3, 10, 640, 128), BF16),
        pltpu.VMEM((10, 320, 128), BF16),
        pltpu.VMEM((10, 320, 128), BF16),
        pltpu.VMEM((8, 320, 128), BF16),
        pltpu.VMEM((6, 320, 128), BF16),
        pltpu.VMEM((6, 320, 128), BF16),
        pltpu.VMEM((8, 320, 128), BF16),
        pltpu.VMEM((3, 640, 128), BF16),
        pltpu.VMEM((3, 640, 128), BF16),
        pltpu.VMEM((640, 128), BF16),
        pltpu.VMEM((640, 384), BF16),
        pltpu.VMEM((8, 320, 128), BF16),
        pltpu.VMEM((4, 128, 320), BF16),
        pltpu.VMEM((4, 32, 320), BF16),
        pltpu.VMEM((6, 64, 2, 128), F32),
        pltpu.VMEM((2, 128), F32),
        pltpu.VMEM((2, 128), F32),
        dma((15, 8)), dma((15, 8)),
        dma((6,)), dma((6,)), dma((1,)), dma((1,)),
        dma((2,)), dma((2,)), dma((4, 2)), dma((4, 2)), dma((3,)), dma((3,)), dma((3,)), dma((3,)), dma((3,)), dma((1,)),
    ]
    vmem = pl.BlockSpec(memory_space=pltpu.VMEM)
    out = pl.pallas_call(
        functools.partial(entry, len(tables)),
        out_shape=jax.ShapeDtypeStruct((4, 32, 320), BF16),
        in_specs=[vmem] * 2 + [pl.BlockSpec(memory_space=pl.ANY)] * len(tables),
        out_specs=vmem,
        scratch_shapes=scratch,
        compiler_params=pltpu.CompilerParams(
            collective_id=0, has_side_effects=True, vmem_limit_bytes=62 * 1024 * 1024
        ),
        cost_estimate=pl.CostEstimate(
            flops=12_000_000_000, bytes_accessed=30_000_000, transcendentals=2_000_000
        ),
    )(fields, packs, *tables)
    return out[None]


def solution(mesh):
    return jax.shard_map(
        shards,
        mesh=mesh,
        in_specs=(P(None, "space", None, None), P("section", None, "space")),
        out_specs=P(None, "space", "section", None),
        check_vma=False,
    )
```

```python
import functools
import math

import jax
import jax.numpy as jnp
import numpy as np
from jax import lax
from jax.experimental import pallas as pl
from jax.experimental.pallas import tpu as pltpu
from jax.sharding import PartitionSpec as P

F32 = jnp.float32
BF16 = jnp.bfloat16
MESH = pl.DeviceIdType.MESH
EPSILON = 1e-05
CHUNK = 1536
HALF = CHUNK // 2
QUARTER = CHUNK // 4
ROW_N = 512 * 10
LANES = 8 * CHUNK


def selections():
    rows = np.arange(768)
    chan_wide = np.where(rows % 48 < 40, 40 * (rows // 48) + rows % 48, -1)
    chan_fine = chan_wide[:384]
    rows = np.arange(48)
    packed = np.where(rows < 40, 16 * (rows // 10) + rows % 10, -1)
    split = lambda n: np.concatenate([np.arange(0, n, 2), np.arange(1, n, 2)])
    di, di_wide = split(320), split(640)
    nat, nat_wide = np.arange(320), np.arange(640)
    eq = lambda a, b: (a[:, None] == b[None, :])
    b = np.arange(128)
    shifts = np.stack([eq(b, b + dx) for dx in (-1, 1)])
    strided = np.stack(
        [
            np.stack([eq(b, 2 * (b % 64) + dx) & (b // 64 == i)[None, :] for dx in (-1, 0, 1)])
            for i in (0, 1)
        ]
    )
    doubled = np.stack(
        [
            np.stack(
                [
                    eq(b, 64 * half + (b + dx) // 2) & ((b + dx >= 0) & (b + dx < 128))[None, :]
                    for dx in (-1, 0, 1)
                ]
            )
            for half in (0, 1)
        ]
    )

    def taps():
        a, c = np.arange(6 * 64), np.arange(2 * 64)
        out = []
        for dy in (0, 1, 2):
            for dx in (-1, 0, 1):
                col = c % 64 + dx
                out.append(
                    eq(a, (c // 64 + 1 + dy) * 64 + col) & ((col >= 0) & (col < 64))[None, :]
                )
        return np.stack(out)

    group = np.arange(128)
    fine_groups = np.stack(
        [eq(di // 10, group), eq(di // 20, group), eq(16 + di // 20, group)]
    )
    wide_groups = eq(nat_wide // 20, group)
    bf = lambda m: np.asarray(m, np.float32).astype(jnp.bfloat16)
    return (
        bf(eq(packed, np.arange(64))),
        bf(eq(di, chan_fine)),
        bf(eq(nat, chan_fine)),
        bf(eq(chan_fine, di)),
        bf(eq(chan_fine, nat)),
        bf(eq(nat_wide, chan_wide)),
        bf(eq(chan_wide, nat_wide)),
        bf(eq(di, nat)),
        bf(eq(di_wide, nat_wide)),
        bf(shifts),
        bf(strided),
        bf(doubled),
        bf(taps()),
        np.asarray(fine_groups, np.float32),
        np.asarray(wide_groups, np.float32),
    )


def dot(a, b):
    return jnp.dot(a, b, preferred_element_type=F32)


def activate(values, mean, rstd):
    z = (values - mean) * rstd
    return z / (1.0 + jnp.exp(-z))


def kernel(
    loads,     x_ref, w_ref, pack, sel_di, sel_nat, exp_di, exp_nat, sel_c, exp_c, perm_x, perm_c, shifts, strided,
    doubled, taps, fine_groups, wide_groups, out_ref,
    W, raw, col, colw, colj, sh, xr, xd, hid, skd, skn, skb, cb, ht, tile, a3, ud, outs, landed,
    SA, HS, HR, gather_send, gather_recv, a_send, a_recv, b_send, b_recv,
    x_send, x_recv, h_send, h_recv, c_send, c_recv, k_send, k_recv, o_send, o_recv,
):
    sec = lax.axis_index("section")
    d = lax.axis_index("space")
    c = lax.rem(d, 2)
    z = lax.rem(lax.div(d, 2), 2)
    x = lax.rem(lax.div(d, 4), 4)
    y = lax.div(d, 16)
    space = lambda y, x, z, c: ((y * 4 + x) * 2 + z) * 2 + c
    xp, xm = lax.rem(x + 1, 4), lax.rem(x + 3, 4)
    yp, ym = lax.rem(y + 1, 4), lax.rem(y + 3, 4)
    below, above = lax.rem(d + 1, 64), lax.rem(d + 63, 64)
    after, before = lax.rem(sec + 1, 4), lax.rem(sec + 3, 4)
    is_top = d == 0
    is_bottom = d == 63
    keep_top = jnp.where(is_top, 0.0, 1.0)
    keep_bottom = jnp.where(is_bottom, 0.0, 1.0)

    for load in loads:
        load.start()

    barrier = pltpu.get_barrier_semaphore()
    peers = [(lax.rem(sec + 2, 4), d)]
    for other in (after, before):
        peers += [(other, d), (other, below), (other, above)]
    for peer in peers:
        pl.semaphore_signal(barrier, inc=1, device_id=peer, device_id_type=MESH)

    def greet(k, carry):
        peer = (sec, lax.rem(d + k, 64))
        pl.semaphore_signal(barrier, inc=1, device_id=peer, device_id_type=MESH)
        return carry

    lax.fori_loop(1, 64, greet, 0)

    raw[2 * z + c] = jnp.zeros((16, LANES), BF16)
    raw[2 * z + c, 0:10, 0:11520] = w_ref[...]
    for load in loads:
        load.wait()
    pl.semaphore_wait(barrier, len(peers) + 63)

    def remote(src, dst, send, recv, peer):
        return pltpu.make_async_remote_copy(
            src_ref=src, dst_ref=dst, send_sem=send, recv_sem=recv, device_id=peer,
            device_id_type=MESH,
        )

    def combined(messages, count):
        means = messages[:, 0:1, :]
        mean = jnp.sum(means, axis=0) * (1.0 / 64)
        spread = jnp.sum(jnp.square(means - mean[None]), axis=0) * count
        squares = jnp.sum(messages[:, 1:2, :], axis=0) + spread
        return mean, lax.rsqrt(squares * (1.0 / (64 * count)) + EPSILON)

    def part_sums(blocks, groups, count, weight=None):
        total = blocks[0] if weight is None else blocks[0] * weight
        for block in blocks[1:]:
            total = total + block
        channel = jnp.sum(total, axis=1, keepdims=True)
        mean = jnp.sum(groups * channel, axis=0, keepdims=True) * (1.0 / count)
        own = jnp.sum(groups * mean, axis=1, keepdims=True)
        squares = None
        for block in blocks:
            off = jnp.square(block - own)
            off = off if weight is None else off * weight
            squares = off if squares is None else squares + off
        channel = jnp.sum(squares, axis=1, keepdims=True)
        return mean, jnp.sum(groups * channel, axis=0, keepdims=True)

    def start_exchange(e, mean, deviation):
        SA[e, 0] = jnp.concatenate([mean, deviation], axis=0)

        def one(k, carry):
            peer = (sec, lax.rem(d + k, 64))
            remote(SA.at[e, 0], SA.at[e, k], a_send.at[e], a_recv.at[e], peer).start()
            return carry

        lax.fori_loop(1, 64, one, 0)

    def finish_exchange(e, count):
        others = SA.at[e, pl.ds(1, 63)]
        remote(others, others, a_send.at[e], a_recv.at[e], (sec, below)).wait()
        return combined(SA[e], count)

    def exchanged(e, mean, deviation, count):
        start_exchange(e, mean, deviation)
        return finish_exchange(e, count)

    def columns(groups, rows):
        return [jnp.sum(groups * row, axis=1, keepdims=True) for row in rows]

    def across_copy():
        return remote(HS, HR, b_send.at[0], b_recv.at[0], (after, d))

    def rim_copies(kind, array, down, up):
        (down_from, down_to), (up_from, up_to) = down, up
        return [
            remote(array.at[pl.ds(down_from, size)], array.at[pl.ds(down_to, size)],
                   h_send.at[kind, 0], h_recv.at[kind, 0], (sec, below))
            for size in (2 if kind == 0 else 1,)
        ] + [
            remote(array.at[pl.ds(up_from, 1)], array.at[pl.ds(up_to, 1)],
                   h_send.at[kind, 1], h_recv.at[kind, 1], (sec, above))
        ]

    def start_all(copies):
        for copy in copies:
            copy.start()

    def wait_all(copies):
        for copy in copies:
            copy.wait()

    def tile_copies():
        return [
            remote(tile, cb.at[slot], c_send.at[slot], c_recv.at[slot], (after, peer))
            for slot, peer in ((1, d), (0, below), (2, above))
        ]

    def skip_copies():
        return [
            remote(skd.at[lax_rows(1, 4)], skb.at[lax_rows(2, 4)], k_send.at[0], k_recv.at[0], (before, d)),
            remote(skd.at[lax_rows(4, 1)], skb.at[lax_rows(1, 1)], k_send.at[1], k_recv.at[1], (before, below)),
            remote(skd.at[lax_rows(1, 1)], skb.at[lax_rows(6, 1)], k_send.at[2], k_recv.at[2], (before, above)),
        ]

    def lax_rows(start, size):
        return pl.ds(start, size)

    def hand_over(count):
        for copy in tile_copies():
            copy.start()

        @pl.when(sec < 2)
        def _():
            mean, deviation = part_sums([tile[...].astype(F32)], wide_groups[...], count)
            HS[...] = jnp.concatenate(exchanged(2, mean, deviation, count), axis=0)
            across_copy().start()
            across_copy().wait_send()

        for copy in tile_copies():
            copy.wait_send()

    def take_over():
        for copy in tile_copies():
            copy.wait_recv()

    chunks = jnp.where(sec == 0, 4, jnp.where(sec == 3, 5, 8))

    def gather_copies(core, stage, k):
        lanes = lambda off, size: pl.ds(pl.multiple_of(k * CHUNK + off, 128), size)
        mine, other = lanes(HALF * core, HALF), lanes(HALF * (1 - core), HALF)
        left, right = lanes(HALF * core, QUARTER), lanes(HALF * core + QUARTER, QUARTER)
        along_x = (space(y, xp, z, c), space(y, xm, z, c))
        along_y = (space(yp, x, z, c), space(ym, x, z, c))
        rows, every = pl.ds(0, 48), pl.ds(0, 4)
        array, sibling = W, space(y, x, z, 1 - c)

        def line(core, at, lanes=mine):
            return (every, at, rows, lanes) if core else (at, every, rows, lanes)

        if stage == 0:
            array, whole = raw, pl.ds(0, 16)
            moves = [
                ((2 * z + c, whole, mine), space(y, x, 1 - z, c)),
                ((2 * z + c, whole, other), space(y, x, 1 - z, 1 - c)),
                ((2 * z + c, whole, other), space(y, x, z, 1 - c)),
            ]
        elif stage == 1:
            moves = [((y, x, rows, mine), peer) for peer in (along_y if core else along_x)]
        elif stage == 2 and core == 0:
            moves = [((y, xm, rows, left), along_x[0]), ((y, xp, rows, right), along_x[1])]
        elif stage == 2:
            moves = [((ym, x, rows, left), along_y[0]), ((yp, x, rows, right), along_y[1])]
        elif stage == 3:
            own = line(core, x if core else y)
            moves = [(own, peer) for peer in (along_x if core else along_y)] + [(own, sibling)]
        elif stage == 4:
            up, down = (xm, xp) if core else (ym, yp)
            to_next, to_last = along_x if core else along_y
            moves = [(line(core, up, left), to_next), (line(core, down, right), to_last)]
            moves += [(line(core, up), sibling), (line(core, down), sibling)]
        else:
            moves = [(line(core, lax.rem((x if core else y) + 2, 4)), sibling)]
        first_id = (0, 3, 5, 7, 10, 14)[stage]
        return [
            remote(
                array.at[where], array.at[where], gather_send.at[first_id + i, k],
                gather_recv.at[first_id + i, k], (sec, peer),
            )
            for i, (where, peer) in enumerate(moves)
        ]

    def gather_step(core, t):
        for stage in range(7):
            k = t - stage

            @pl.when((k >= 0) & (k < chunks))
            def _():
                if stage > 0:
                    for copy in gather_copies(core, stage - 1, k):
                        copy.wait_recv()
                if stage == 1:
                    lanes = pl.ds(pl.multiple_of(k * CHUNK + HALF * core, 128), HALF)
                    blocks = raw[:, :, lanes].reshape(64, HALF)
                    W[y, x, :, lanes] = dot(pack[...], blocks).astype(BF16)
                if stage < 6:
                    for copy in gather_copies(core, stage, k):
                        copy.start()

    def gather(first, last):
        def step(t, carry):
            for core in range(2):
                pl.when(c == core)(lambda core=core: gather_step(core, t))
            return carry

        lax.fori_loop(first, last, step, 0)

    def gather_end():
        def waits(core, k):
            for stage in range(6):
                for copy in gather_copies(core, stage, k):
                    copy.wait_send()

        def step(k, carry):
            for core in range(2):
                pl.when(c == core)(lambda core=core: waits(core, k))
            return carry

        lax.fori_loop(0, chunks, step, 0)

    def put_shifted(index, base, values):
        size = values.shape[0]
        sh[1, index, base : base + size, :] = values
        sh[0, index, base : base + size, :] = dot(values, shifts[0]).astype(BF16)
        sh[2, index, base : base + size, :] = dot(values, shifts[1]).astype(BF16)

    def fine_conv(pairs, pieces, per_tap, lead, lane_start, depth, source_row, use):
        taps = 9 * per_tap
        for p in range(2):
            if lead:
                col[p, 0:lead, :] = jnp.zeros((lead, 256), BF16)
            if lead + taps < depth:
                col[p, lead + taps : depth, :] = jnp.zeros((depth - lead - taps, 256), BF16)

        def pair(q, carry):
            for p in range(2):
                for dy in range(3):
                    for j in range(2):
                        row = source_row(q, j + dy)
                        for dx in range(3):
                            at = lead + (dy * 3 + dx) * per_tap
                            for to, start, size in pieces(p):
                                col[p, at + to : at + to + size, 128 * j : 128 * j + 128] = sh[
                                    dx, row, start : start + size, :
                                ]
            use(q, weighted(lane_start, depth, col))
            return carry

        lax.fori_loop(0, pairs, pair, 0)

    def weighted(lane_start, depth, source):
        total = None
        for p in range(2):
            kernels = W[2 * p : 2 * p + 2, :, :, lane_start : lane_start + depth]
            made = dot(kernels.reshape(384, depth), source[p, 0:depth, :])
            total = made if total is None else total + made
        return total

    narrow_pieces = lambda p: [(0, 160 * p, 160)]
    wide_pieces = lambda p: [(0, 320 * p, 320)]
    joined_pieces = lambda p: [(0, 160 * p, 160), (160, 320 + 160 * p, 160)]
    follow = lambda q, off: 2 * q + off
    narrow_scale = 1.0 / math.sqrt(9 * 320)
    wide_scale = 1.0 / math.sqrt(9 * 640)

    def row_kept(row):
        return jnp.where(row < 0, keep_top, jnp.where(row > 3, keep_bottom, 1.0))

    def activate_rows(source, start, stop, own_row, mean, rstd):
        def one(r, carry):
            values = activate(source[r].astype(F32), mean, rstd) * row_kept(r - own_row)
            put_shifted(r, 0, values.astype(BF16))
            return carry

        lax.fori_loop(start, stop, one, 0)

    @pl.when(sec == 0)
    def _():
        x_copies = [
            remote(x_ref.at[pl.ds(3, 1)], xr.at[pl.ds(2, 1)], x_send.at[0], x_recv.at[0], (0, below)),
            remote(x_ref.at[pl.ds(0, 1)], xr.at[pl.ds(7, 1)], x_send.at[1], x_recv.at[1], (0, above)),
        ]
        for copy in x_copies:
            copy.start()
        gather(0, 1)
        for r in range(4):
            xr[3 + r] = x_ref[r]
        hid[7] = jnp.zeros((320, 128), BF16)

        def permute(r, carry):
            xd[r] = dot(perm_x[...], xr[r]).astype(BF16)
            return carry

        lax.fori_loop(3, 7, permute, 0)
        groups = fine_groups[0]
        sums = part_sums([xd[r].astype(F32) for r in range(3, 7)], groups, ROW_N)
        gather(1, 2)
        start_exchange(0, *sums)
        gather(2, 7)
        for copy in x_copies:
            copy.wait()
        lax.fori_loop(2, 3, permute, 0)
        lax.fori_loop(7, 8, permute, 0)
        mean, rstd = columns(groups, finish_exchange(0, ROW_N))
        activate_rows(xd, 2, 8, 3, mean, rstd)

        def keep_hidden(q, made):
            rounded = (made * narrow_scale).astype(BF16)
            packed = dot(sel_di[...], rounded).astype(BF16)
            hid[2 * q + 2] = packed[:, 0:128]
            hid[2 * q + 3] = packed[:, 128:256]

        from_two = lambda q, off: 2 * q + off + 2
        fine_conv(2, narrow_pieces, 160, 0, 0, 1536, from_two, keep_hidden)
        rims = rim_copies(0, hid, (4, 0), (2, 6))
        start_all(rims)
        start_exchange(1, *part_sums([hid[r].astype(F32) for r in range(2, 6)], groups, ROW_N))
        gather(7, 8)
        mean, rstd = columns(groups, finish_exchange(1, ROW_N))
        wait_all(rims)
        activate_rows(hid, 0, 8, 2, mean, rstd)

        def keep_skip(q, made):
            for j in range(2):
                own = dot(exp_di[...], xd[2 * q + j + 2])
                rounded = (own + made[:, 128 * j : 128 * j + 128] * narrow_scale).astype(BF16)
                skd[2 * q + j] = dot(sel_di[...], rounded).astype(BF16)
                skn[2 * q + j] = dot(sel_nat[...], rounded).astype(BF16)

        fine_conv(3, narrow_pieces, 160, 32, 1408, 1536, follow, keep_skip)
        gather(8, 10)
        skn[0] = (skn[0].astype(F32) * keep_top).astype(BF16)
        col[0, 0:64, 0:128] = jnp.zeros((64, 128), BF16)
        for dy in range(3):
            for dx in range(3):
                at = 64 + (dy * 3 + dx) * 320
                made = dot(skn[dy], strided[0, dx]) + dot(skn[2 + dy], strided[1, dx])
                col[0, at : at + 320, 0:128] = made.astype(BF16)
        made = dot(W[:, :, :, 2816:5760].reshape(768, 2944), col[0, :, 0:128])
        rounded = (made * narrow_scale).astype(BF16)
        tile[...] = dot(sel_c[...], rounded).astype(BF16)
        hand_over(128 * 20)
        start_all(skip_copies())
        for copy in skip_copies():
            copy.wait_send()

    @pl.when((sec == 1) | (sec == 2))
    def _():
        gather(0, chunks + 6)
        take_over()
        count = 128 * 20
        groups = wide_groups[...]
        across_copy().wait_recv()
        mean, rstd = columns(groups, [HR[0:1, :], HR[1:2, :]])

        def activate_tiles(source):
            for i in range(3):
                values = activate(source[i].astype(F32), mean, rstd)
                values = values * (keep_top, 1.0, keep_bottom)[i]
                a3[:, 128 * i : 128 * i + 128] = values.astype(BF16)

        def coarse_conv(lane_start):
            for t in range(9):
                px = ((0, 256), (128, 256), (128, 384))[t // 3]
                moved = dot(a3[:, px[0] : px[1]], taps[t, px[0] : px[1], :])
                colw[640 * t : 640 * t + 640, :] = moved.astype(BF16)
            total = None
            for i in range(3):
                lanes = slice(lane_start + 1920 * i, lane_start + 1920 * i + 1920)
                source = colw[1920 * i : 1920 * i + 1920, :]
                made = dot(W[:, :, :, lanes].reshape(768, 1920), source)
                total = made if total is None else total + made
            return total * wide_scale

        activate_tiles(cb)
        rounded = coarse_conv(0).astype(BF16)
        hidden = dot(sel_c[...], rounded)
        ht[1] = hidden.astype(BF16)
        rims = rim_copies(3, ht, (1, 0), (1, 2))
        start_all(rims)
        sums = part_sums([hidden], groups, count)
        start_exchange(3, *sums)
        own = dot(exp_c[...], cb[1])
        mean, rstd = columns(groups, finish_exchange(3, count))
        wait_all(rims)
        activate_tiles(ht)
        made = coarse_conv(5760)
        rounded = (own + made).astype(BF16)
        tile[...] = dot(sel_c[...], rounded).astype(BF16)
        hand_over(count)

    def out_copies(sections=range(3)):
        return [
            remote(
                outs.at[pl.ds(0, 4), pl.ds(32 * t, 32)], landed, o_send.at[t], o_recv.at[0], (t, d)
            )
            for t in sections
        ]

    @pl.when(sec == 3)
    def _():
        gather(0, chunks + 6)
        for copy in skip_copies():
            copy.wait_recv()
        groups_u, groups_s = fine_groups[1], fine_groups[2]
        mean_s, dev_s = part_sums([skb[r].astype(F32) for r in range(2, 6)], groups_s, 2 * ROW_N)
        take_over()
        for i in range(3):
            moved = dot(perm_c[...], cb[i]) * (keep_top, 1.0, keep_bottom)[i]
            moved = moved.astype(BF16)
            for half in ((1,), (0, 1), (0,))[i]:
                for dx in range(3):
                    sh[dx, 2 * i + half] = dot(moved, doubled[half, dx]).astype(BF16)

        def keep_upper(q, made):
            rounded = (made * wide_scale).astype(BF16)
            packed = dot(sel_di[...], rounded).astype(BF16)
            ud[2 * q + 2] = packed[:, 0:128]
            ud[2 * q + 3] = packed[:, 128:256]

        half_row = lambda q, off: q + 1 + (off + 1) // 2
        fine_conv(2, wide_pieces, 320, 0, 0, 2944, half_row, keep_upper)
        rims = rim_copies(1, ud, (5, 1), (2, 6))
        start_all(rims)
        mean_u, dev_u = part_sums([ud[r].astype(F32) for r in range(2, 6)], groups_u, 2 * ROW_N)
        rows = exchanged(4, mean_u + mean_s, dev_u + dev_s, 2 * ROW_N)
        wait_all(rims)
        mean_u, rstd_u = columns(groups_u, rows)
        mean_s, rstd_s = columns(groups_s, rows)

        def joined_row(r, carry):
            kept = row_kept(r - 2)
            upper = activate(ud[r].astype(F32), mean_u, rstd_u) * kept
            put_shifted(r, 0, upper.astype(BF16))
            lower = activate(skb[r].astype(F32), mean_s, rstd_s) * kept
            put_shifted(r, 320, lower.astype(BF16))
            return carry

        lax.fori_loop(1, 7, joined_row, 0)

        def keep_hidden(q, made):
            rounded = (made * wide_scale).astype(BF16)
            packed = dot(sel_di[...], rounded).astype(BF16)
            hid[2 * q + 1] = packed[:, 0:128]
            hid[2 * q + 2] = packed[:, 128:256]

        from_one = lambda q, off: 2 * q + off + 1
        fine_conv(2, joined_pieces, 320, 64, 2816, 2944, from_one, keep_hidden)
        rims = rim_copies(2, hid, (4, 0), (1, 5))
        start_all(rims)
        groups = fine_groups[0]
        sums = part_sums([hid[r].astype(F32) for r in range(1, 5)], groups, ROW_N)
        mean, rstd = columns(groups, exchanged(5, *sums, ROW_N))
        wait_all(rims)
        activate_rows(hid, 0, 6, 1, mean, rstd)
        for p in range(2):
            colj[p, 0:32, :] = jnp.zeros((32, 256), BF16)
            colj[p, 352:384, :] = jnp.zeros((32, 256), BF16)

        def keep_output(q, made):
            for p in range(2):
                for j in range(2):
                    px = slice(128 * j, 128 * j + 128)
                    colj[p, 32:192, px] = ud[2 * q + j + 2, 160 * p : 160 * p + 160, :]
                    colj[p, 192:352, px] = skb[2 * q + j + 2, 160 * p : 160 * p + 160, :]
            straight = weighted(7168, 384, colj)
            total = made * narrow_scale + straight * (1.0 / math.sqrt(640))
            rounded = total.astype(BF16)
            for j in range(2):
                flipped = lax.dot_general(
                    rounded[:, 128 * j : 128 * j + 128], exp_nat[...], (((0,), (0,)), ((), ())),
                    preferred_element_type=F32,
                )
                outs[2 * q + j] = flipped.astype(BF16)

        fine_conv(2, narrow_pieces, 160, 0, 5760, 1536, follow, keep_output)
        for copy in out_copies():
            copy.start()
        out_ref[...] = outs[:, 96:128, :]
        for copy in out_copies():
            copy.wait_send()

    @pl.when(sec < 3)
    def _():
        for copy in out_copies((0,)):
            copy.wait_recv()
        out_ref[...] = landed[...]

    gather_end()


def entry(count, x_ref, w_ref, *refs):
    sources, out_ref, copies = refs[:count], refs[count], refs[count + 1 : 2 * count + 1]
    sems, others = refs[2 * count + 1], refs[2 * count + 2 :]
    loads = [
        pltpu.make_async_copy(source, copy, sems.at[i])
        for i, (source, copy) in enumerate(zip(sources, copies))
    ]
    kernel(loads, x_ref, w_ref, *copies, out_ref, *others)


def shards(features, section_packs):
    fields = jnp.swapaxes(features[0], 1, 2)
    packs = jnp.swapaxes(section_packs[0], 0, 1)
    tables = selections()
    dma = pltpu.SemaphoreType.DMA
    scratch = [pltpu.VMEM(table.shape, table.dtype) for table in tables]
    scratch += [
        dma((len(tables),)),
        pltpu.VMEM((4, 4, 48, LANES), BF16),
        pltpu.VMEM((4, 16, LANES), BF16),
        pltpu.VMEM((2, 2944, 256), BF16),
        pltpu.VMEM((5760, 128), BF16),
        pltpu.VMEM((2, 384, 256), BF16),
        pltpu.VMEM((3, 10, 640, 128), BF16),
        pltpu.VMEM((10, 320, 128), BF16),
        pltpu.VMEM((10, 320, 128), BF16),
        pltpu.VMEM((8, 320, 128), BF16),
        pltpu.VMEM((6, 320, 128), BF16),
        pltpu.VMEM((6, 320, 128), BF16),
        pltpu.VMEM((8, 320, 128), BF16),
        pltpu.VMEM((3, 640, 128), BF16),
        pltpu.VMEM((3, 640, 128), BF16),
        pltpu.VMEM((640, 128), BF16),
        pltpu.VMEM((640, 384), BF16),
        pltpu.VMEM((8, 320, 128), BF16),
        pltpu.VMEM((4, 128, 320), BF16),
        pltpu.VMEM((4, 32, 320), BF16),
        pltpu.VMEM((6, 64, 2, 128), F32),
        pltpu.VMEM((2, 128), F32),
        pltpu.VMEM((2, 128), F32),
        dma((15, 8)), dma((15, 8)),
        dma((6,)), dma((6,)), dma((1,)), dma((1,)),
        dma((2,)), dma((2,)), dma((4, 2)), dma((4, 2)), dma((3,)), dma((3,)), dma((3,)), dma((3,)), dma((3,)), dma((1,)),
    ]
    vmem = pl.BlockSpec(memory_space=pltpu.VMEM)
    out = pl.pallas_call(
        functools.partial(entry, len(tables)),
        out_shape=jax.ShapeDtypeStruct((4, 32, 320), BF16),
        in_specs=[vmem] * 2 + [pl.BlockSpec(memory_space=pl.ANY)] * len(tables),
        out_specs=vmem,
        scratch_shapes=scratch,
        compiler_params=pltpu.CompilerParams(
            collective_id=0, has_side_effects=True, vmem_limit_bytes=62 * 1024 * 1024
        ),
        cost_estimate=pl.CostEstimate(
            flops=12_000_000_000, bytes_accessed=30_000_000, transcendentals=2_000_000
        ),
    )(fields, packs, *tables)
    return out[None]


def solution(mesh):
    return jax.shard_map(
        shards,
        mesh=mesh,
        in_specs=(P(None, "space", None, None), P("section", None, "space")),
        out_specs=P(None, "space", "section", None),
        check_vma=False,
    )
```
